128 devices in a mesh: seq: 16 (over z, y), expert: 8 (over x, core).
Axes of the slice: x: 4, y: 4, z: 4, core: 2. Of those that a mesh axis runs over, the one named last changes fastest.
Arguments:
- tokens: bfloat16 [2048, 4096], P(('seq', 'expert')), may hold values from -6 to 6
- gain_mamba: float32 [4096], replicated, may hold values from 0.1 to 1.9
- in_weight: bfloat16 [2, 4096, 8192], P(None, 'seq', 'expert'), may hold values from -0.09375 to 0.09375
- conv_weight: float32 [4, 8192], P(None, 'expert'), may hold values from -3 to 3
- conv_bias: float32 [8192], P('expert'), may hold values from -3 to 3
- xproj_weight: bfloat16 [8192, 288], P('expert'), may hold values from -0.0625 to 0.0625
- dt_weight: bfloat16 [256, 8192], P(None, 'expert'), may hold values from -0.375 to 0.375
- dt_bias: float32 [8192], P('expert'), may hold values from -7 to -2
- a_rate: float32 [16, 8192], P(None, 'expert'), may hold values from 0.01 to 8
- skip_d: float32 [8192], P('expert'), may hold values from 0.5 to 1.5
- out_weight: bfloat16 [8192, 4096], P('expert', 'seq'), may hold values from -0.0625 to 0.0625
- gain_moe: float32 [4096], replicated, may hold values from 0.1 to 1.9
- expert_ids: int32 [2048, 2], P(('seq', 'expert')), may hold values from 0 to 15, all different within a row; in each aligned block of 16 rows (0 to 15, 16 to 31, ...) at most 4 rows name the same one
- gate_weights: float32 [2048, 2], P(('seq', 'expert')), may hold values from 0.2 to 1
- w_gate: bfloat16 [16, 4096, 7168], P('seq', None, 'expert'), may hold values from -0.09375 to 0.09375
- w_up: bfloat16 [16, 4096, 7168], P('seq', None, 'expert'), may hold values from -0.09375 to 0.09375
- w_down: bfloat16 [16, 7168, 4096], P('seq', 'expert'), may hold values from -0.0625 to 0.0625
Outputs:
- mixed: bfloat16 [2048, 4096], P(('seq', 'expert'))
The draws below stay inside these ranges and needn't reach their ends.
Inputs may be any that keep to these rules, and one draw needn't show every extreme that they name: `expert_ids`: each row names 2 different experts. In each aligned block of 16 rows (the rows of one device) no expert is named by more than 4 rows, a bound that some block reaches.
All inputs are finite; a program needn't handle non-finite values.
Results may differ from the reference program's by a relative error of at most 0.03.
Values may be sent and summed in bfloat16 or wider, within the bound.
A program may use at most 192 MiB of HBM per device.

```python
import math
import jax
import jax.numpy as jnp
import numpy as np
from jax import lax

D = 4096
INNER = 8192
STATE = 16
CONV = 4
RANK = 256
FFE = 7168
TOP = 2
ROWS = 16
EXPERTS = 16
CAP = 4
TOKENS = 2048
N_EXPERT = 8


def level_of(key, dims, pieces, least, top_value):
    level = 1.0
    for dim, parts in pieces:
        heights = jax.random.uniform(jax.random.fold_in(jax.random.fold_in(key, 6), dim), (parts,), jnp.float32, least / len(pieces), top_value / len(pieces))
        level = level * jnp.repeat(jnp.exp(heights), dims[dim] // parts).reshape((-1,) + (1,) * (len(dims) - 1 - dim))
    return level


def deal_out(key, own, number, rows, number_of, top, bound, slope):
    sequence = jax.random.permutation(key, number_of)
    packed, usual = portions_of(number_of, rows * top, bound, slope, True), portions_of(number_of, rows * top, bound, slope, False)
    places = jnp.arange(number_of)

    def named(sizes, offset_by):
        used = int((sizes > 0).sum())
        fixed = max(1, used // 4)
        passed = fixed + (places - fixed + offset_by * (used - fixed)) % max(1, number_of - fixed)
        return jnp.zeros((number_of,), jnp.int32).at[sequence[jnp.where(places < fixed, places, passed)]].set(jnp.asarray(sizes, jnp.int32))

    sizes = jnp.where(number % 4 == 0, named(packed, number // 4), named(usual, number - number // 4 - 1))
    mixed = jax.random.permutation(jax.random.fold_in(own, 3), number_of)
    donor, sink = mixed[0:number_of // 2 * 2:2], mixed[1:number_of // 2 * 2:2]
    room = jnp.minimum(sizes[donor] - 1, bound - sizes[sink]) // 2
    room = jnp.where((donor == sequence[0]) | (sink == sequence[0]) | (sizes[sink] == 0), 0, jnp.maximum(room, 0))
    passed = jax.random.randint(jax.random.fold_in(own, 4), (number_of // 2,), 0, 1 << 20) % (room + 1)
    sizes = sizes.at[donor].add(-passed).at[sink].add(passed)
    members = jnp.searchsorted(jnp.cumsum(sizes), jnp.arange(rows * top), side="right").astype(jnp.int32)
    listing = members.reshape(top, rows).T
    listing = listing[jax.random.permutation(jax.random.fold_in(own, 1), rows)]
    offset_by = jax.random.randint(jax.random.fold_in(own, 2), (rows, 1), 0, top)
    return jnp.take_along_axis(listing, (jnp.arange(top)[None, :] + offset_by) % top, axis=1)


def portions_of(amount, total, most, skew, full):
    loads = [(1 << 20) // math.isqrt(rank ** skew) + 1 for rank in range(1, amount + 1)]
    largest = most if full else min(most, max(-(-total // amount), total * loads[0] // sum(loads)))
    least = 1 if total - largest >= amount - 1 else 0
    counts, rest = [largest] + [least] * (amount - 1), total - largest - least * (amount - 1)
    while rest > 0:
        candidates = [i for i in range(1, amount) if counts[i] < largest] or [i for i in range(1, amount) if counts[i] < most]
        whole, budget = sum([loads[i] for i in candidates]), rest
        for i in candidates:
            more = min(most - counts[i], max(1, budget * loads[i] // whole), rest)
            counts[i] = counts[i] + more
            rest = rest - more
    return np.array(counts)


def scatter_about(own_key, extent, deviation, reach, shards=(), kind=jnp.bfloat16):
    level = level_of(own_key, extent, shards, -0.22, 0.18) if shards else 1.0
    drawn = jax.random.normal(own_key, extent, jnp.float32) * deviation * level
    return jnp.minimum(jnp.maximum(drawn, -reach), reach).astype(kind)


def setup_inputs(seed: int = 0) -> dict:
    splits = jax.random.split(jax.random.key(seed), 18)
    tokens = scatter_about(splits[0], (TOKENS, D), 1.0, 6.0, ((0, 128),))
    gain_mamba = jnp.clip(1.0 + 0.18 * jax.random.normal(splits[1], (D,), jnp.float32), 0.1, 1.9)
    in_weight = scatter_about(splits[2], (2, D, INNER), D ** -0.5, 0.09375, ((1, 16), (2, 8)))
    conv_weight = scatter_about(splits[3], (CONV, INNER), CONV ** -0.5, 3.0, ((1, 8),), jnp.float32)
    conv_bias = scatter_about(splits[4], (INNER,), 0.5, 3.0, ((0, 8),), jnp.float32)
    xproj_weight = scatter_about(splits[5], (INNER, RANK + 2 * STATE), INNER ** -0.5, 0.0625, ((0, 8),))
    dt_weight = scatter_about(splits[6], (RANK, INNER), RANK ** -0.5, 0.375, ((1, 8),))
    dt_bias = jnp.clip(-7.0 + 5.0 * jax.random.uniform(splits[7], (INNER,), jnp.float32) ** level_of(splits[7], (INNER,), ((0, 8),), -0.2, 0.2), -7.0, -2.0)
    a_rate = jnp.clip(jnp.exp(math.log(8.0) - 6.684612 * jax.random.uniform(splits[8], (STATE, INNER), jnp.float32) ** level_of(splits[8], (STATE, INNER), ((1, 8),), -0.2, 0.2)), 0.01, 8.0)
    skip_d = jnp.clip(0.5 + 1.0 * jax.random.uniform(splits[9], (INNER,), jnp.float32) ** level_of(splits[9], (INNER,), ((0, 8),), -0.2, 0.2), 0.5, 1.5)
    out_weight = scatter_about(splits[10], (INNER, D), INNER ** -0.5, 0.0625, ((0, 8), (1, 16)))
    gain_moe = jnp.clip(1.0 + 0.18 * jax.random.normal(splits[11], (D,), jnp.float32), 0.1, 1.9)
    expert_ids_keys = jax.random.split(jax.random.fold_in(splits[12], 1), TOKENS // ROWS)
    expert_ids_turns = jax.random.permutation(jax.random.fold_in(splits[12], 3), TOKENS // ROWS)
    expert_ids = jax.vmap(lambda own, number: deal_out(jax.random.fold_in(splits[12], 2), own, number, ROWS, EXPERTS, TOP, CAP, 2))(expert_ids_keys, expert_ids_turns).reshape((TOKENS, TOP))
    gate_weights = jnp.clip(0.2 + 0.8 * jax.random.uniform(splits[13], (TOKENS, TOP), jnp.float32) ** level_of(splits[13], (TOKENS, TOP), ((0, 128),), -0.2, 0.2), 0.2, 1.0)
    w_gate = scatter_about(splits[14], (EXPERTS, D, FFE), D ** -0.5, 0.09375, ((0, 16), (2, 8)))
    w_up = scatter_about(splits[15], (EXPERTS, D, FFE), D ** -0.5, 0.09375, ((0, 16), (2, 8)))
    w_down = scatter_about(splits[16], (EXPERTS, FFE, D), FFE ** -0.5, 0.0625, ((0, 16), (1, 8)))
    return dict(tokens=tokens, gain_mamba=gain_mamba, in_weight=in_weight, conv_weight=conv_weight, conv_bias=conv_bias, xproj_weight=xproj_weight, dt_weight=dt_weight, dt_bias=dt_bias, a_rate=a_rate, skip_d=skip_d, out_weight=out_weight, gain_moe=gain_moe, expert_ids=expert_ids, gate_weights=gate_weights, w_gate=w_gate, w_up=w_up, w_down=w_down)


def rms_norm(values, gain):
    wide = values.astype(jnp.float32)
    return wide * lax.rsqrt(lax.optimization_barrier(jnp.mean(wide * wide, axis=-1, keepdims=True)) + 1e-05) * gain

def grouped_product(left, right, groups):
    width = left.shape[1] // groups
    total = jnp.zeros((left.shape[0], right.shape[1]), jnp.float32)
    for group_index in range(groups):
        part = jnp.dot(left[:, group_index * width:(group_index + 1) * width], right[group_index * width:(group_index + 1) * width], preferred_element_type=jnp.float32)
        rounded = lax.optimization_barrier(part.astype(jnp.bfloat16))
        total = total + rounded.astype(jnp.float32)
    return total

def reference(tokens, gain_mamba, in_weight, conv_weight, conv_bias, xproj_weight, dt_weight, dt_bias, a_rate, skip_d, out_weight, gain_moe, expert_ids, gate_weights, w_gate, w_up, w_down):
    normed = rms_norm(tokens, gain_mamba).astype(jnp.bfloat16)
    xpart = jnp.dot(normed, in_weight[0], preferred_element_type=jnp.float32)
    zpart = jnp.dot(normed, in_weight[1], preferred_element_type=jnp.float32)
    padded = jnp.concatenate([jnp.zeros((CONV - 1, INNER), jnp.float32), xpart], axis=0)
    conv = conv_bias
    for tap in range(CONV):
        conv = conv + conv_weight[tap] * padded[tap:tap + TOKENS]
    inner = jax.nn.silu(conv).astype(jnp.bfloat16)
    proj = jnp.dot(inner, xproj_weight, preferred_element_type=jnp.float32)
    dt_low = proj[:, :RANK].astype(jnp.bfloat16)
    bmat = proj[:, RANK:RANK + STATE]
    cmat = proj[:, RANK + STATE:]
    step = jax.nn.softplus(jnp.dot(dt_low, dt_weight, preferred_element_type=jnp.float32) + dt_bias)
    inner_f = inner.astype(jnp.float32)

    def advance(state, items):
        step_t, inner_t, b_t, c_t = items
        state = jnp.exp(-step_t[None, :] * a_rate) * state + b_t[:, None] * (step_t * inner_t)[None, :]
        return (state, lax.optimization_barrier(jnp.sum(c_t[:, None] * state, axis=0)))
    start = jnp.zeros((STATE, INNER), jnp.float32)
    _, readout = lax.scan(advance, start, (step, inner_f, bmat, cmat))
    gated = ((readout + skip_d * inner_f) * jax.nn.silu(zpart)).astype(jnp.bfloat16)
    mamba_out = grouped_product(gated, out_weight, N_EXPERT)
    resid = (tokens.astype(jnp.float32) + mamba_out).astype(jnp.bfloat16)
    normed2 = rms_norm(resid, gain_moe).astype(jnp.bfloat16)
    blocks = TOKENS // ROWS
    ids = expert_ids.reshape(blocks, ROWS * TOP)
    onehot = (ids[:, :, None] == jnp.arange(EXPERTS, dtype=jnp.int32)[None, None, :]).astype(jnp.int32)
    before = jnp.cumsum(onehot, axis=1) - onehot
    slot = lax.optimization_barrier(jnp.sum(before * onehot, axis=2))
    block_index = jnp.arange(blocks, dtype=jnp.int32)[:, None]
    position = ((ids * blocks + block_index) * CAP + slot).reshape(-1).astype(jnp.int32)
    source_rows = jnp.repeat(normed2, TOP, axis=0)
    buffer = jnp.zeros((EXPERTS * blocks * CAP, D), jnp.bfloat16).at[position].set(source_rows)
    buffer = buffer.reshape(EXPERTS, blocks * CAP, D)

    def one_expert(items):
        rows_in, gate_w, up_w, down_w = items
        gate = jnp.dot(rows_in, gate_w, preferred_element_type=jnp.float32)
        upper = jnp.dot(rows_in, up_w, preferred_element_type=jnp.float32)
        act = (jax.nn.silu(gate) * upper).astype(jnp.bfloat16)
        return grouped_product(act, down_w, N_EXPERT).astype(jnp.bfloat16)
    outputs = lax.map(one_expert, (buffer, w_gate, w_up, w_down))
    picked = outputs.reshape(EXPERTS * blocks * CAP, D)[position].reshape(TOKENS, TOP, D)
    moe = lax.optimization_barrier(jnp.sum(gate_weights[:, :, None] * picked.astype(jnp.float32), axis=1))
    return (resid.astype(jnp.float32) + moe).astype(jnp.bfloat16)
```

```python
import jax
import jax.numpy as jnp
from jax import lax
from jax.sharding import PartitionSpec as P

STATE = 16
CONV = 4
RANK = 256
TOP = 2


def from_behind(block, axis, distance):
    devices = range(lax.axis_size(axis))
    route = [(i - distance, i) for i in devices if i - distance in devices]
    return lax.ppermute(block, axis, route)


def rms_norm(values, gain):
    wide = values.astype(jnp.float32)
    return wide * lax.rsqrt(jnp.mean(wide * wide, axis=-1, keepdims=True) + 1e-05) * gain


def combine_states(earlier, later):
    return (earlier[0] * later[0], later[0] * earlier[1] + later[1])


def per_device(
    tokens,
    gain_mamba,
    in_weight,
    conv_weight,
    conv_bias,
    xproj_weight,
    dt_weight,
    dt_bias,
    a_rate,
    skip_d,
    out_weight,
    gain_moe,
    expert_ids,
    gate_weights,
    w_gate,
    w_up,
    w_down,
):
    rows, dim = tokens.shape
    n_seq = lax.axis_size("seq")
    n_exp = lax.axis_size("expert")
    group = lax.all_gather(tokens, "expert", axis=0, tiled=True)
    local_tok = group.shape[0]
    normed = rms_norm(group, gain_mamba).astype(jnp.bfloat16)
    both = jnp.einsum(
        "td,kdc->tkc",
        normed,
        lax.all_gather(in_weight, "seq", axis=1, tiled=True),
        preferred_element_type=jnp.float32,
    )
    xpart = both[:, 0]
    zpart = both[:, 1]
    edge = from_behind(xpart[local_tok - (CONV - 1) :], "seq", 1)
    padded = jnp.concatenate([edge, xpart], axis=0)
    conv = conv_bias
    for tap in range(CONV):
        conv = conv + conv_weight[tap] * padded[tap : tap + local_tok]
    inner = jax.nn.silu(conv).astype(jnp.bfloat16)
    partial_value = jnp.dot(inner, xproj_weight, preferred_element_type=jnp.float32)
    low_part, edge_part = (
        lax.psum(partial_value[:, :RANK].astype(jnp.bfloat16), "expert").astype(jnp.float32),
        lax.psum(partial_value[:, RANK:].astype(jnp.bfloat16), "expert").astype(jnp.float32),
    )
    dt_low = low_part.astype(jnp.bfloat16)
    bmat = edge_part[:, :STATE]
    cmat = edge_part[:, STATE:]
    step = jax.nn.softplus(jnp.dot(dt_low, dt_weight, preferred_element_type=jnp.float32) + dt_bias)
    inner_f = inner.astype(jnp.float32)
    decay = jnp.exp(-step[:, None, :] * a_rate[None, :, :])
    source = bmat[:, :, None] * (step * inner_f)[:, None, :]
    cumulative, states = lax.associative_scan(combine_states, (decay, source), axis=0)
    total = cumulative[-1]
    final = states[-1]

    def relay(turn, incoming):
        return from_behind((total * incoming + final).astype(jnp.bfloat16), "seq", 1).astype(
            jnp.float32
        )

    arriving = lax.fori_loop(0, n_seq - 1, relay, jnp.zeros_like(final))
    states = states + cumulative * arriving[None, :, :]
    readout = jnp.sum(cmat[:, :, None] * states, axis=1)
    gated = ((readout + skip_d * inner_f) * jax.nn.silu(zpart)).astype(jnp.bfloat16)
    terms = jnp.dot(
        gated,
        lax.all_gather(out_weight, "seq", axis=1, tiled=True),
        preferred_element_type=jnp.float32,
    )
    mixer = lax.psum_scatter(
        terms.astype(jnp.bfloat16), "expert", scatter_dimension=0, tiled=True
    ).astype(jnp.float32)
    resid = (tokens.astype(jnp.float32) + mixer).astype(jnp.bfloat16)
    normed2 = rms_norm(resid, gain_moe).astype(jnp.bfloat16)
    capacity = max(2, 4 * rows // n_seq)
    slots_all = n_seq * capacity
    flat_ids = expert_ids.reshape(-1)
    order = jnp.arange(flat_ids.shape[0], dtype=jnp.int32)
    same = (flat_ids[:, None] == flat_ids[None, :]) & (order[None, :] < order[:, None])
    slot = jnp.sum(same.astype(jnp.int32), axis=1)
    target = flat_ids * capacity + slot
    places = target[:, None] == jnp.arange(slots_all, dtype=jnp.int32)[None, :]
    dispatch_mat = jnp.any(places.reshape(rows, TOP, slots_all), axis=1).astype(jnp.bfloat16)
    send = jnp.einsum(
        "rp,rd->pd", dispatch_mat, normed2, preferred_element_type=jnp.float32
    ).astype(jnp.bfloat16)
    received = lax.all_to_all(
        send.reshape(n_seq, capacity, dim), "seq", split_axis=0, concat_axis=0, tiled=True
    )
    pooled = lax.all_gather(
        received.reshape(1, slots_all, dim), "expert", axis=0, tiled=True
    ).reshape(n_exp * slots_all, dim)
    gate = jnp.dot(pooled, w_gate[0], preferred_element_type=jnp.float32)
    upper = jnp.dot(pooled, w_up[0], preferred_element_type=jnp.float32)
    act = (jax.nn.silu(gate) * upper).astype(jnp.bfloat16)
    outputs = lax.psum_scatter(
        jnp.dot(act, w_down[0], preferred_element_type=jnp.float32).astype(jnp.bfloat16),
        "expert",
        scatter_dimension=0,
        tiled=True,
    )
    returned = lax.all_to_all(
        outputs.reshape(n_seq, capacity, dim), "seq", split_axis=0, concat_axis=0, tiled=True
    ).reshape(slots_all, dim)
    weighting = jnp.where(places, gate_weights.reshape(-1)[:, None], 0.0)
    weighting = jnp.sum(weighting.reshape(rows, TOP, slots_all), axis=1)
    moe = jnp.dot(weighting, returned.astype(jnp.float32), precision=lax.Precision.HIGHEST)
    return (resid.astype(jnp.float32) + moe).astype(jnp.bfloat16)


def solution(mesh):
    placed = (
        P(("seq", "expert"), None),
        P(),
        P(None, "seq", "expert"),
        P(None, "expert"),
        P("expert"),
        P("expert", None),
        P(None, "expert"),
        P("expert"),
        P(None, "expert"),
        P("expert"),
        P("expert", "seq"),
        P(),
        P(("seq", "expert"), None),
        P(("seq", "expert"), None),
        P("seq", None, "expert"),
        P("seq", None, "expert"),
        P("seq", "expert", None),
    )
    return jax.shard_map(
        per_device,
        mesh=mesh,
        in_specs=placed,
        out_specs=P(("seq", "expert"), None),
        check_vma=False,
    )
```

```python
import functools

import jax
import jax.numpy as jnp
from jax import lax
from jax.experimental import pallas as pl
from jax.experimental.pallas import tpu as pltpu
from jax.sharding import PartitionSpec as P

MESH = pl.DeviceIdType.MESH
VMEM_LIMIT = 56 * 2**20

STATE = 16
CONV = 4
RANK = 256
TOP = 2


def from_behind(block, axis, distance):
    devices = range(lax.axis_size(axis))
    route = [(i - distance, i) for i in devices if i - distance in devices]
    return lax.ppermute(block, axis, route)


def rms_norm(values, gain):
    wide = values.astype(jnp.float32)
    return wide * lax.rsqrt(jnp.mean(wide * wide, axis=-1, keepdims=True) + 1e-05) * gain


def gather_kernel(axis, n, x_ref, o_ref, send_sems, recv_sems, local_sem):
    me = lax.axis_index(axis)
    barrier = pltpu.get_barrier_semaphore()
    for d in range(1, n):
        pl.semaphore_signal(
            barrier, inc=1, device_id={axis: lax.rem(me + d, n)}, device_id_type=MESH
        )
    pl.semaphore_wait(barrier, n - 1)
    own = pltpu.make_async_copy(x_ref, o_ref.at[me], local_sem)
    own.start()
    sent = []
    for d in range(1, n):
        copy = pltpu.make_async_remote_copy(
            src_ref=x_ref,
            dst_ref=o_ref.at[me],
            send_sem=send_sems.at[d],
            recv_sem=recv_sems.at[d],
            device_id={axis: lax.rem(me + d, n)},
            device_id_type=MESH,
        )
        copy.start()
        sent.append(copy)
    own.wait()
    for d in range(1, n):
        pltpu.make_async_remote_copy(
            src_ref=x_ref,
            dst_ref=o_ref.at[lax.rem(me + n - d, n)],
            send_sem=send_sems.at[d],
            recv_sem=recv_sems.at[d],
            device_id={axis: lax.rem(me + d, n)},
            device_id_type=MESH,
        ).wait_recv()
    for copy in sent:
        copy.wait_send()


def direct_gather(x, axis, collective_id):
    n = lax.axis_size(axis)
    return pl.pallas_call(
        functools.partial(gather_kernel, axis, n),
        out_shape=jax.ShapeDtypeStruct((n, *x.shape), x.dtype),
        in_specs=[pl.BlockSpec(memory_space=pltpu.VMEM)],
        out_specs=pl.BlockSpec(memory_space=pltpu.VMEM),
        scratch_shapes=[
            pltpu.SemaphoreType.DMA((n,)),
            pltpu.SemaphoreType.DMA((n,)),
            pltpu.SemaphoreType.DMA,
        ],
        compiler_params=pltpu.CompilerParams(
            collective_id=collective_id, has_side_effects=True, vmem_limit_bytes=VMEM_LIMIT
        ),
    )(x)


def lanes_of(value, width):
    return jnp.concatenate([value] * (width // 128), axis=1)


def first_pass(low_ref, weight_ref, bias_ref, inner_ref, a_ref, b_ref, step_ref, out_ref, u_ref):
    tokens, width = inner_ref.shape
    for at in range(0, width, 256):
        cols = pl.ds(at, 256)
        raw = jnp.dot(low_ref[...], weight_ref[:, cols], preferred_element_type=jnp.float32)
        raw = raw + bias_ref[:, cols]
        step = jnp.maximum(raw, 0.0) + jnp.log1p(jnp.exp(-jnp.abs(raw)))
        step_ref[:, cols] = step
        u_ref[:, cols] = step * inner_ref[:, cols].astype(jnp.float32)
    rate = a_ref[...]

    def group(g, state):
        base = pl.multiple_of(g * 8, 8)
        step8 = step_ref[pl.ds(base, 8), :]
        u8 = u_ref[pl.ds(base, 8), :]
        for r in range(8):
            decay = jnp.exp(-(step8[r : r + 1, :] * rate))
            state = decay * state + lanes_of(b_ref[base + r], width) * u8[r : r + 1, :]
        return state

    final = lax.fori_loop(0, tokens // 8, group, jnp.zeros_like(rate))
    out_ref[:STATE, :] = final
    out_ref[STATE : STATE + 8, :] = jnp.broadcast_to(
        jnp.sum(step_ref[...], axis=0, keepdims=True), (8, width)
    )


def second_pass(step_ref, inner_ref, a_ref, b_ref, c_ref, start_ref, skip_ref, z_ref, out_ref, u_ref):
    tokens, width = inner_ref.shape
    u_ref[...] = step_ref[...] * inner_ref[...].astype(jnp.float32)
    rate = a_ref[...]

    def group(g, state):
        base = pl.multiple_of(g * 8, 8)
        step8 = step_ref[pl.ds(base, 8), :]
        u8 = u_ref[pl.ds(base, 8), :]
        rows = []
        for r in range(8):
            decay = jnp.exp(-(step8[r : r + 1, :] * rate))
            state = decay * state + lanes_of(b_ref[base + r], width) * u8[r : r + 1, :]
            rows.append(jnp.sum(lanes_of(c_ref[base + r], width) * state, axis=0, keepdims=True))
        u_ref[pl.ds(base, 8), :] = jnp.concatenate(rows, axis=0)
        return state

    lax.fori_loop(0, tokens // 8, group, start_ref[...])
    z = z_ref[...]
    out_ref[...] = (
        (u_ref[...] + skip_ref[...] * inner_ref[...].astype(jnp.float32)) * (z / (1.0 + jnp.exp(-z)))
    ).astype(out_ref.dtype)


def per_device(
    tokens,
    gain_mamba,
    in_weight,
    conv_weight,
    conv_bias,
    xproj_weight,
    dt_weight,
    dt_bias,
    a_rate,
    skip_d,
    out_weight,
    gain_moe,
    expert_ids,
    gate_weights,
    w_gate,
    w_up,
    w_down,
):
    rows, dim = tokens.shape
    n_seq = lax.axis_size("seq")
    n_exp = lax.axis_size("expert")
    group = lax.all_gather(tokens, "expert", axis=0, tiled=True)
    local_tok = group.shape[0]
    normed = rms_norm(group, gain_mamba).astype(jnp.bfloat16)
    both = jnp.einsum(
        "td,kdc->tkc",
        normed,
        lax.all_gather(in_weight, "seq", axis=1, tiled=True),
        preferred_element_type=jnp.float32,
    )
    xpart = both[:, 0]
    zpart = both[:, 1]
    edge = from_behind(xpart[local_tok - (CONV - 1) :], "seq", 1)
    padded = jnp.concatenate([edge, xpart], axis=0)
    conv = conv_bias
    for tap in range(CONV):
        conv = conv + conv_weight[tap] * padded[tap : tap + local_tok]
    inner = jax.nn.silu(conv).astype(jnp.bfloat16)
    partial_value = jnp.dot(inner, xproj_weight, preferred_element_type=jnp.float32)
    proj = jnp.sum(
        direct_gather(partial_value.astype(jnp.bfloat16), "expert", 1).astype(jnp.float32), axis=0
    )
    dt_low = proj[:, :RANK].astype(jnp.bfloat16)
    width = inner.shape[1]
    bmat = jnp.broadcast_to(proj[:, RANK : RANK + STATE, None], (local_tok, STATE, 128))
    cmat = jnp.broadcast_to(proj[:, RANK + STATE :, None], (local_tok, STATE, 128))
    step, local_end = pl.pallas_call(
        first_pass,
        out_shape=(
            jax.ShapeDtypeStruct((local_tok, width), jnp.float32),
            jax.ShapeDtypeStruct((STATE + 8, width), jnp.float32),
        ),
        scratch_shapes=[pltpu.VMEM((local_tok, width), jnp.float32)],
        compiler_params=pltpu.CompilerParams(vmem_limit_bytes=VMEM_LIMIT),
    )(dt_low, dt_weight, dt_bias[None, :], inner, a_rate, bmat)
    ends = direct_gather(local_end, "seq", 2)
    me = lax.axis_index("seq")
    start = jnp.zeros_like(a_rate)
    for block in range(n_seq - 1):
        after = jnp.exp(-a_rate * ends[block, STATE : STATE + 1]) * start + ends[block, :STATE]
        start = jnp.where(block < me, after, start)
    gated = pl.pallas_call(
        second_pass,
        out_shape=jax.ShapeDtypeStruct((local_tok, width), jnp.bfloat16),
        scratch_shapes=[pltpu.VMEM((local_tok, width), jnp.float32)],
        compiler_params=pltpu.CompilerParams(vmem_limit_bytes=VMEM_LIMIT),
    )(step, inner, a_rate, bmat, cmat, start, skip_d[None, :], zpart)
    terms = jnp.dot(
        gated,
        lax.all_gather(out_weight, "seq", axis=1, tiled=True),
        preferred_element_type=jnp.float32,
    )
    mixer = lax.psum_scatter(
        terms.astype(jnp.bfloat16), "expert", scatter_dimension=0, tiled=True
    ).astype(jnp.float32)
    resid = (tokens.astype(jnp.float32) + mixer).astype(jnp.bfloat16)
    normed2 = rms_norm(resid, gain_moe).astype(jnp.bfloat16)
    capacity = max(2, 4 * rows // n_seq)
    slots_all = n_seq * capacity
    flat_ids = expert_ids.reshape(-1)
    order = jnp.arange(flat_ids.shape[0], dtype=jnp.int32)
    same = (flat_ids[:, None] == flat_ids[None, :]) & (order[None, :] < order[:, None])
    slot = jnp.sum(same.astype(jnp.int32), axis=1)
    target = flat_ids * capacity + slot
    places = target[:, None] == jnp.arange(slots_all, dtype=jnp.int32)[None, :]
    dispatch_mat = jnp.any(places.reshape(rows, TOP, slots_all), axis=1).astype(jnp.bfloat16)
    send = jnp.einsum(
        "rp,rd->pd", dispatch_mat, normed2, preferred_element_type=jnp.float32
    ).astype(jnp.bfloat16)
    received = lax.all_to_all(
        send.reshape(n_seq, capacity, dim), "seq", split_axis=0, concat_axis=0, tiled=True
    )
    pooled = lax.all_gather(
        received.reshape(1, slots_all, dim), "expert", axis=0, tiled=True
    ).reshape(n_exp * slots_all, dim)
    gate = jnp.dot(pooled, w_gate[0], preferred_element_type=jnp.float32)
    upper = jnp.dot(pooled, w_up[0], preferred_element_type=jnp.float32)
    act = (jax.nn.silu(gate) * upper).astype(jnp.bfloat16)
    outputs = lax.psum_scatter(
        jnp.dot(act, w_down[0], preferred_element_type=jnp.float32).astype(jnp.bfloat16),
        "expert",
        scatter_dimension=0,
        tiled=True,
    )
    returned = lax.all_to_all(
        outputs.reshape(n_seq, capacity, dim), "seq", split_axis=0, concat_axis=0, tiled=True
    ).reshape(slots_all, dim)
    weighting = jnp.where(places, gate_weights.reshape(-1)[:, None], 0.0)
    weighting = jnp.sum(weighting.reshape(rows, TOP, slots_all), axis=1)
    moe = jnp.dot(weighting, returned.astype(jnp.float32), precision=lax.Precision.HIGHEST)
    return (resid.astype(jnp.float32) + moe).astype(jnp.bfloat16)


def solution(mesh):
    placed = (
        P(("seq", "expert"), None),
        P(),
        P(None, "seq", "expert"),
        P(None, "expert"),
        P("expert"),
        P("expert", None),
        P(None, "expert"),
        P("expert"),
        P(None, "expert"),
        P("expert"),
        P("expert", "seq"),
        P(),
        P(("seq", "expert"), None),
        P(("seq", "expert"), None),
        P("seq", None, "expert"),
        P("seq", None, "expert"),
        P("seq", "expert", None),
    )
    return jax.shard_map(
        per_device,
        mesh=mesh,
        in_specs=placed,
        out_specs=P(("seq", "expert"), None),
        check_vma=False,
    )
```

```python
import functools

import jax
import jax.numpy as jnp
from jax import lax
from jax.experimental import pallas as pl
from jax.experimental.pallas import tpu as pltpu
from jax.sharding import PartitionSpec as P

MESH = pl.DeviceIdType.MESH
VMEM_LIMIT = 56 * 2**20

STATE = 16
CONV = 4
RANK = 256
TOP = 2


def from_behind(block, axis, distance):
    devices = range(lax.axis_size(axis))
    route = [(i - distance, i) for i in devices if i - distance in devices]
    return lax.ppermute(block, axis, route)


def rms_norm(values, gain):
    wide = values.astype(jnp.float32)
    return wide * lax.rsqrt(jnp.mean(wide * wide, axis=-1, keepdims=True) + 1e-05) * gain


def gather_kernel(axis, n, x_ref, o_ref, send_sems, recv_sems, local_sem):
    me = lax.axis_index(axis)
    barrier = pltpu.get_barrier_semaphore()
    for d in range(1, n):
        pl.semaphore_signal(
            barrier, inc=1, device_id={axis: lax.rem(me + d, n)}, device_id_type=MESH
        )
    pl.semaphore_wait(barrier, n - 1)
    own = pltpu.make_async_copy(x_ref, o_ref.at[me], local_sem)
    own.start()
    sent = []
    for d in range(1, n):
        copy = pltpu.make_async_remote_copy(
            src_ref=x_ref,
            dst_ref=o_ref.at[me],
            send_sem=send_sems.at[d],
            recv_sem=recv_sems.at[d],
            device_id={axis: lax.rem(me + d, n)},
            device_id_type=MESH,
        )
        copy.start()
        sent.append(copy)
    own.wait()
    for d in range(1, n):
        pltpu.make_async_remote_copy(
            src_ref=x_ref,
            dst_ref=o_ref.at[lax.rem(me + n - d, n)],
            send_sem=send_sems.at[d],
            recv_sem=recv_sems.at[d],
            device_id={axis: lax.rem(me + d, n)},
            device_id_type=MESH,
        ).wait_recv()
    for copy in sent:
        copy.wait_send()


def direct_gather(x, axis, collective_id):
    n = lax.axis_size(axis)
    return pl.pallas_call(
        functools.partial(gather_kernel, axis, n),
        out_shape=jax.ShapeDtypeStruct((n, *x.shape), x.dtype),
        in_specs=[pl.BlockSpec(memory_space=pltpu.VMEM)],
        out_specs=pl.BlockSpec(memory_space=pltpu.VMEM),
        scratch_shapes=[
            pltpu.SemaphoreType.DMA((n,)),
            pltpu.SemaphoreType.DMA((n,)),
            pltpu.SemaphoreType.DMA,
        ],
        compiler_params=pltpu.CompilerParams(
            collective_id=collective_id, has_side_effects=True, vmem_limit_bytes=VMEM_LIMIT
        ),
    )(x)


def ring_of(axis_seq, kind):
    z, y = axis_seq // 4, axis_seq % 4
    if kind == 0:
        return y, lambda d: z * 4 + (y + d) % 4
    return z, lambda d: ((z + d) % 4) * 4 + y


def remote(src, dst, sems, index, target):
    return pltpu.make_async_remote_copy(
        src_ref=src,
        dst_ref=dst,
        send_sem=sems[0].at[index],
        recv_sem=sems[1].at[index],
        device_id=target,
        device_id_type=MESH,
    )


def greet(targets):
    barrier = pltpu.get_barrier_semaphore()
    for target in targets:
        pl.semaphore_signal(barrier, inc=1, device_id=target, device_id_type=MESH)
    pl.semaphore_wait(barrier, len(targets))


def expert_ring(e):
    return (e ^ 1, (e + 2) % 8, (e + 6) % 8)


def project_kernel(
    tok_ref, gain_ref, w_ref, x_ref, z_ref,
    n_ref, t_ref, g_ref, p_ref, relay_ref, in_ref,
    ws, wr, ts, tr, xs, xr, rs, rr, local_sems,
):
    s = lax.axis_index("seq")
    e = lax.axis_index("expert")
    at_y, along_y = ring_of(s, 0)
    at_z, along_z = ring_of(s, 1)
    sib, nxt, prv = expert_ring(e)
    gather = ((at_y, along_y), (at_z, along_z))
    reduce = ((at_z, along_z), (at_y, along_y))
    seq = lambda index: {"seq": index}
    exp = lambda index: {"expert": index}
    greet(
        [seq(along_y(d)) for d in (1, 2, 3)]
        + [seq(along_z(d)) for d in (1, 2, 3)]
        + [exp(sib), exp(nxt), exp(prv)]
    )
    half = w_ref.shape[1] // 2
    halves = (pl.ds(0, half), pl.ds(half, half))
    sent, own = [], []
    for k, (at, along) in enumerate(gather):
        for m, (h, d) in enumerate(((0, 1), (1, 3), (1, 1), (0, 3))):
            copy = remote(
                w_ref.at[k, halves[h]], g_ref.at[k, at, halves[h]], (ws, wr), k * 6 + m, seq(along(d))
            )
            copy.start()
            sent.append(copy)
        copy = pltpu.make_async_copy(w_ref.at[k], g_ref.at[k, at], local_sems.at[k])
        copy.start()
        own.append(copy)
    wide = tok_ref[...].astype(jnp.float32)
    scale = lax.rsqrt(jnp.mean(wide * wide, axis=-1, keepdims=True) + 1e-05)
    normed = (wide * scale * gain_ref[...]).astype(jnp.bfloat16)
    for q in range(4):
        n_ref[0, q] = normed[:, q * 1024 : (q + 1) * 1024]
        for r in range(4):
            n_ref[1, q, :, r * 256 : (r + 1) * 256] = normed[:, (r * 4 + q) * 256 : (r * 4 + q + 1) * 256]
    mine = pl.ds(pl.multiple_of(e * 16, 16), 16)
    for k, (at, along) in enumerate(reduce):
        for d in (2, 1, 3):
            copy = remote(
                n_ref.at[k, (at + d) % 4], t_ref.at[k, at, mine], (ts, tr), k * 4 + d, seq(along(d))
            )
            copy.start()
            sent.append(copy)
        copy = pltpu.make_async_copy(n_ref.at[k, at], t_ref.at[k, at, mine], local_sems.at[2 + k])
        copy.start()
        own.append(copy)
    for copy in own:
        copy.wait()
    rows_of = lambda index: pl.ds(pl.multiple_of(index * 16, 16), 16)

    def pass_on(k, m, index, part, target):
        span = (slice(None), slice(0, 2), slice(2, 4))[part]
        block = t_ref.at[k, span, rows_of(index)]
        copy = remote(block, block, (xs, xr), k * 9 + m, exp(target))
        copy.start()
        sent.append(copy)

    def arrive(k, m, index, part):
        span = (slice(None), slice(0, 2), slice(2, 4))[part]
        block = t_ref.at[k, span, rows_of(index)]
        remote(block, block, (xs, xr), k * 9 + m, exp(sib)).wait_recv()

    for k, (at, along) in enumerate(reduce):
        for d in (1, 3, 2):
            remote(
                n_ref.at[k, at], t_ref.at[k, (at + 4 - d) % 4, mine], (ts, tr), k * 4 + d, seq(along(d))
            ).wait_recv()
        pass_on(k, 0, e, 0, nxt)
        pass_on(k, 1, e, 0, prv)
        pass_on(k, 2, e, 0, sib)
    for k, (at, along) in enumerate(gather):
        remote(
            w_ref.at[k, halves[0]], g_ref.at[k, (at + 3) % 4, halves[0]], (ws, wr), k * 6, seq(along(1))
        ).wait_recv()
        block = g_ref.at[k, (at + 3) % 4, halves[0]]
        copy = remote(block, block, (ws, wr), k * 6 + 4, seq(along(1)))
        copy.start()
        sent.append(copy)
        remote(
            w_ref.at[k, halves[1]], g_ref.at[k, (at + 1) % 4, halves[1]], (ws, wr), k * 6 + 1, seq(along(3))
        ).wait_recv()
        block = g_ref.at[k, (at + 1) % 4, halves[1]]
        copy = remote(block, block, (ws, wr), k * 6 + 5, seq(along(3)))
        copy.start()
        sent.append(copy)
    far = (e + 4) % 8
    for k in range(2):
        arrive(k, 0, prv, 0)
        pass_on(k, 3, prv, 1, nxt)
        pass_on(k, 4, prv, 0, sib)
        arrive(k, 1, nxt, 0)
        pass_on(k, 5, nxt, 2, prv)
        pass_on(k, 6, nxt, 0, sib)
    for k in range(2):
        arrive(k, 3, far, 1)
        pass_on(k, 7, far, 1, sib)
        arrive(k, 5, far, 2)
        pass_on(k, 8, far, 2, sib)
    for k in range(2):
        arrive(k, 2, e ^ 1, 0)
        arrive(k, 4, prv ^ 1, 0)
        arrive(k, 6, nxt ^ 1, 0)
        arrive(k, 7, far ^ 1, 1)
        arrive(k, 8, far ^ 1, 2)
    top, low = pl.ds(0, 64), pl.ds(64, 64)
    outs = (x_ref, z_ref)

    def product(k, block, put):
        def tile(c, carry):
            cols = pl.ds(pl.multiple_of(c * 256, 256), 256)
            rows = t_ref[k, block]
            total = jnp.zeros((rows.shape[0], 256), jnp.float32)
            for q in range(4):
                total = total + jnp.dot(
                    rows[:, q * 256 : (q + 1) * 256],
                    g_ref[k, q, :, cols],
                    preferred_element_type=jnp.float32,
                )
            put(cols, total)
            return carry

        lax.fori_loop(0, 4, tile, 0)

    def push(k, m, src, dst, target):
        copy = remote(src, dst, (rs, rr), k * 6 + m, seq(target))
        copy.start()
        sent.append(copy)

    def landed(k, m, dst, target):
        remote(dst, dst, (rs, rr), k * 6 + m, seq(target)).wait_recv()

    for k, (at, along) in enumerate(gather):
        later = (at + 3) % 4
        for m, (h, o) in enumerate(((0, 3), (1, 1), (1, 3), (0, 1))):
            if m >= 2:
                remote(
                    w_ref.at[k, halves[h]], g_ref.at[k, (at + o) % 4, halves[h]], (ws, wr), k * 6 + m, seq(along(1))
                ).wait_recv()
        for m, h in ((4, 0), (5, 1)):
            remote(
                w_ref.at[k, halves[h]], g_ref.at[k, (at + 2) % 4, halves[h]], (ws, wr), k * 6 + m, seq(along(1))
            ).wait_recv()
        del later
        at, along = reduce[k]
        for d in (2, 1, 3):

            def put(cols, total, k=k, d=d):
                p_ref[k, d - 1, :, cols] = total.astype(jnp.bfloat16)

            product(k, (at + d) % 4, put)
            if d == 2:
                push(k, 0, p_ref.at[k, 1, top], relay_ref.at[k, 0], along(1))
                push(k, 1, p_ref.at[k, 1, low], relay_ref.at[k, 1], along(3))
            if d == 1:
                push(k, 2, p_ref.at[k, 0, low], in_ref.at[k, 0, low], along(1))
            if d == 3:
                push(k, 3, p_ref.at[k, 2, top], in_ref.at[k, 1, top], along(3))

        def keep(cols, total, k=k):
            outs[k][:, cols] = total

        product(k, at, keep)
    for k, (at, along) in enumerate(reduce):
        landed(k, 0, relay_ref.at[k, 0], along(1))
        p_ref[k, 0, top] = (
            p_ref[k, 0, top].astype(jnp.float32) + relay_ref[k, 0].astype(jnp.float32)
        ).astype(jnp.bfloat16)
        push(k, 4, p_ref.at[k, 0, top], in_ref.at[k, 0, top], along(1))
        landed(k, 1, relay_ref.at[k, 1], along(3))
        p_ref[k, 2, low] = (
            p_ref[k, 2, low].astype(jnp.float32) + relay_ref[k, 1].astype(jnp.float32)
        ).astype(jnp.bfloat16)
        push(k, 5, p_ref.at[k, 2, low], in_ref.at[k, 1, low], along(3))
    for k, (at, along) in enumerate(reduce):
        landed(k, 2, in_ref.at[k, 0, low], along(1))
        landed(k, 3, in_ref.at[k, 1, top], along(3))
        landed(k, 4, in_ref.at[k, 0, top], along(1))
        landed(k, 5, in_ref.at[k, 1, low], along(3))
        outs[k][...] = outs[k][...] + (in_ref[k, 0].astype(jnp.float32) + in_ref[k, 1].astype(jnp.float32))
    for copy in sent:
        copy.wait_send()


def project(tokens, gain, weight, collective_id):
    width = weight.shape[2]
    out = jax.ShapeDtypeStruct((128, width), jnp.float32)
    dma = pltpu.SemaphoreType.DMA
    return pl.pallas_call(
        project_kernel,
        out_shape=(out, out),
        in_specs=[
            pl.BlockSpec(memory_space=pltpu.VMEM),
            pl.BlockSpec(memory_space=pltpu.VMEM),
            pl.BlockSpec(memory_space=pltpu.VMEM),
        ],
        out_specs=[pl.BlockSpec(memory_space=pltpu.VMEM)] * 2,
        scratch_shapes=[
            pltpu.VMEM((2, 4, 16, 1024), jnp.bfloat16),
            pltpu.VMEM((2, 4, 128, 1024), jnp.bfloat16),
            pltpu.VMEM((2, 4, 256, width), jnp.bfloat16),
            pltpu.VMEM((2, 3, 128, width), jnp.bfloat16),
            pltpu.VMEM((2, 2, 64, width), jnp.bfloat16),
            pltpu.VMEM((2, 2, 128, width), jnp.bfloat16),
            dma((12,)), dma((12,)), dma((8,)), dma((8,)), dma((18,)), dma((18,)), dma((12,)), dma((12,)),
            dma((4,)),
        ],
        compiler_params=pltpu.CompilerParams(
            collective_id=collective_id, has_side_effects=True, vmem_limit_bytes=VMEM_LIMIT
        ),
    )(tokens, gain[None, :], weight)


def lanes_of(value, width):
    return jnp.concatenate([value] * (width // 128), axis=1)


def first_pass(low_ref, weight_ref, bias_ref, inner_ref, a_ref, b_ref, step_ref, out_ref, u_ref):
    tokens, width = inner_ref.shape
    for at in range(0, width, 256):
        cols = pl.ds(at, 256)
        raw = jnp.dot(low_ref[...], weight_ref[:, cols], preferred_element_type=jnp.float32)
        raw = raw + bias_ref[:, cols]
        step = jnp.maximum(raw, 0.0) + jnp.log1p(jnp.exp(-jnp.abs(raw)))
        step_ref[:, cols] = step
        u_ref[:, cols] = step * inner_ref[:, cols].astype(jnp.float32)
    rate = a_ref[...]

    def group(g, state):
        base = pl.multiple_of(g * 8, 8)
        step8 = step_ref[pl.ds(base, 8), :]
        u8 = u_ref[pl.ds(base, 8), :]
        for r in range(8):
            decay = jnp.exp(-(step8[r : r + 1, :] * rate))
            state = decay * state + lanes_of(b_ref[base + r], width) * u8[r : r + 1, :]
        return state

    final = lax.fori_loop(0, tokens // 8, group, jnp.zeros_like(rate))
    out_ref[:STATE, :] = final
    out_ref[STATE : STATE + 8, :] = jnp.broadcast_to(
        jnp.sum(step_ref[...], axis=0, keepdims=True), (8, width)
    )


def second_pass(step_ref, inner_ref, a_ref, b_ref, c_ref, start_ref, skip_ref, z_ref, out_ref, u_ref):
    tokens, width = inner_ref.shape
    u_ref[...] = step_ref[...] * inner_ref[...].astype(jnp.float32)
    rate = a_ref[...]

    def group(g, state):
        base = pl.multiple_of(g * 8, 8)
        step8 = step_ref[pl.ds(base, 8), :]
        u8 = u_ref[pl.ds(base, 8), :]
        rows = []
        for r in range(8):
            decay = jnp.exp(-(step8[r : r + 1, :] * rate))
            state = decay * state + lanes_of(b_ref[base + r], width) * u8[r : r + 1, :]
            rows.append(jnp.sum(lanes_of(c_ref[base + r], width) * state, axis=0, keepdims=True))
        u_ref[pl.ds(base, 8), :] = jnp.concatenate(rows, axis=0)
        return state

    lax.fori_loop(0, tokens // 8, group, start_ref[...])
    z = z_ref[...]
    out_ref[...] = (
        (u_ref[...] + skip_ref[...] * inner_ref[...].astype(jnp.float32)) * (z / (1.0 + jnp.exp(-z)))
    ).astype(out_ref.dtype)


def per_device(
    tokens,
    gain_mamba,
    in_weight,
    conv_weight,
    conv_bias,
    xproj_weight,
    dt_weight,
    dt_bias,
    a_rate,
    skip_d,
    out_weight,
    gain_moe,
    expert_ids,
    gate_weights,
    w_gate,
    w_up,
    w_down,
):
    rows, dim = tokens.shape
    n_seq = lax.axis_size("seq")
    n_exp = lax.axis_size("expert")
    xpart, zpart = project(tokens, gain_mamba, in_weight, 3)
    local_tok = xpart.shape[0]
    edge = from_behind(xpart[local_tok - (CONV - 1) :], "seq", 1)
    padded = jnp.concatenate([edge, xpart], axis=0)
    conv = conv_bias
    for tap in range(CONV):
        conv = conv + conv_weight[tap] * padded[tap : tap + local_tok]
    inner = jax.nn.silu(conv).astype(jnp.bfloat16)
    partial_value = jnp.dot(inner, xproj_weight, preferred_element_type=jnp.float32)
    proj = jnp.sum(
        direct_gather(partial_value.astype(jnp.bfloat16), "expert", 1).astype(jnp.float32), axis=0
    )
    dt_low = proj[:, :RANK].astype(jnp.bfloat16)
    width = inner.shape[1]
    bmat = jnp.broadcast_to(proj[:, RANK : RANK + STATE, None], (local_tok, STATE, 128))
    cmat = jnp.broadcast_to(proj[:, RANK + STATE :, None], (local_tok, STATE, 128))
    step, local_end = pl.pallas_call(
        first_pass,
        out_shape=(
            jax.ShapeDtypeStruct((local_tok, width), jnp.float32),
            jax.ShapeDtypeStruct((STATE + 8, width), jnp.float32),
        ),
        scratch_shapes=[pltpu.VMEM((local_tok, width), jnp.float32)],
        compiler_params=pltpu.CompilerParams(vmem_limit_bytes=VMEM_LIMIT),
    )(dt_low, dt_weight, dt_bias[None, :], inner, a_rate, bmat)
    ends = direct_gather(local_end, "seq", 2)
    me = lax.axis_index("seq")
    start = jnp.zeros_like(a_rate)
    for block in range(n_seq - 1):
        after = jnp.exp(-a_rate * ends[block, STATE : STATE + 1]) * start + ends[block, :STATE]
        start = jnp.where(block < me, after, start)
    gated = pl.pallas_call(
        second_pass,
        out_shape=jax.ShapeDtypeStruct((local_tok, width), jnp.bfloat16),
        scratch_shapes=[pltpu.VMEM((local_tok, width), jnp.float32)],
        compiler_params=pltpu.CompilerParams(vmem_limit_bytes=VMEM_LIMIT),
    )(step, inner, a_rate, bmat, cmat, start, skip_d[None, :], zpart)
    terms = jnp.dot(
        gated,
        lax.all_gather(out_weight, "seq", axis=1, tiled=True),
        preferred_element_type=jnp.float32,
    )
    mixer = lax.psum_scatter(
        terms.astype(jnp.bfloat16), "expert", scatter_dimension=0, tiled=True
    ).astype(jnp.float32)
    resid = (tokens.astype(jnp.float32) + mixer).astype(jnp.bfloat16)
    normed2 = rms_norm(resid, gain_moe).astype(jnp.bfloat16)
    capacity = max(2, 4 * rows // n_seq)
    slots_all = n_seq * capacity
    flat_ids = expert_ids.reshape(-1)
    order = jnp.arange(flat_ids.shape[0], dtype=jnp.int32)
    same = (flat_ids[:, None] == flat_ids[None, :]) & (order[None, :] < order[:, None])
    slot = jnp.sum(same.astype(jnp.int32), axis=1)
    target = flat_ids * capacity + slot
    places = target[:, None] == jnp.arange(slots_all, dtype=jnp.int32)[None, :]
    dispatch_mat = jnp.any(places.reshape(rows, TOP, slots_all), axis=1).astype(jnp.bfloat16)
    send = jnp.einsum(
        "rp,rd->pd", dispatch_mat, normed2, preferred_element_type=jnp.float32
    ).astype(jnp.bfloat16)
    received = lax.all_to_all(
        send.reshape(n_seq, capacity, dim), "seq", split_axis=0, concat_axis=0, tiled=True
    )
    pooled = lax.all_gather(
        received.reshape(1, slots_all, dim), "expert", axis=0, tiled=True
    ).reshape(n_exp * slots_all, dim)
    gate = jnp.dot(pooled, w_gate[0], preferred_element_type=jnp.float32)
    upper = jnp.dot(pooled, w_up[0], preferred_element_type=jnp.float32)
    act = (jax.nn.silu(gate) * upper).astype(jnp.bfloat16)
    outputs = lax.psum_scatter(
        jnp.dot(act, w_down[0], preferred_element_type=jnp.float32).astype(jnp.bfloat16),
        "expert",
        scatter_dimension=0,
        tiled=True,
    )
    returned = lax.all_to_all(
        outputs.reshape(n_seq, capacity, dim), "seq", split_axis=0, concat_axis=0, tiled=True
    ).reshape(slots_all, dim)
    weighting = jnp.where(places, gate_weights.reshape(-1)[:, None], 0.0)
    weighting = jnp.sum(weighting.reshape(rows, TOP, slots_all), axis=1)
    moe = jnp.dot(weighting, returned.astype(jnp.float32), precision=lax.Precision.HIGHEST)
    return (resid.astype(jnp.float32) + moe).astype(jnp.bfloat16)


def solution(mesh):
    placed = (
        P(("seq", "expert"), None),
        P(),
        P(None, "seq", "expert"),
        P(None, "expert"),
        P("expert"),
        P("expert", None),
        P(None, "expert"),
        P("expert"),
        P(None, "expert"),
        P("expert"),
        P("expert", "seq"),
        P(),
        P(("seq", "expert"), None),
        P(("seq", "expert"), None),
        P("seq", None, "expert"),
        P("seq", None, "expert"),
        P("seq", "expert", None),
    )
    return jax.shard_map(
        per_device,
        mesh=mesh,
        in_specs=placed,
        out_specs=P(("seq", "expert"), None),
        check_vma=False,
    )
```

```python
import functools

import jax
import jax.numpy as jnp
from jax import lax
from jax.experimental import pallas as pl
from jax.experimental.pallas import tpu as pltpu
from jax.sharding import PartitionSpec as P

MESH = pl.DeviceIdType.MESH
VMEM_LIMIT = 56 * 2**20

STATE = 16
CONV = 4
RANK = 256
TOP = 2


def ring_of(axis_seq, kind):
    z, y = axis_seq // 4, axis_seq % 4
    if kind == 0:
        return y, lambda d: z * 4 + (y + d) % 4
    return z, lambda d: ((z + d) % 4) * 4 + y


def remote(src, dst, sems, index, target):
    return pltpu.make_async_remote_copy(
        src_ref=src,
        dst_ref=dst,
        send_sem=sems[0].at[index],
        recv_sem=sems[1].at[index],
        device_id=target,
        device_id_type=MESH,
    )


def greet(targets):
    barrier = pltpu.get_barrier_semaphore()
    for target in targets:
        pl.semaphore_signal(barrier, inc=1, device_id=target, device_id_type=MESH)
    pl.semaphore_wait(barrier, len(targets))


def expert_ring(e):
    return (e ^ 1, (e + 2) % 8, (e + 6) % 8)


def project_kernel(
    tok_ref, gain_ref, w_ref, x_ref, z_ref,
    n_ref, t_ref, g_ref, p_ref, relay_ref, in_ref,
    ws, wr, ts, tr, xs, xr, rs, rr, local_sems,
):
    s = lax.axis_index("seq")
    e = lax.axis_index("expert")
    at_y, along_y = ring_of(s, 0)
    at_z, along_z = ring_of(s, 1)
    sib, nxt, prv = expert_ring(e)
    gather = ((at_y, along_y), (at_z, along_z))
    reduce = ((at_z, along_z), (at_y, along_y))
    seq = lambda index: {"seq": index}
    exp = lambda index: {"expert": index}
    greet(
        [seq(along_y(d)) for d in (1, 2, 3)]
        + [seq(along_z(d)) for d in (1, 2, 3)]
        + [exp(sib), exp(nxt), exp(prv)]
    )
    half = w_ref.shape[1] // 2
    halves = (pl.ds(0, half), pl.ds(half, half))
    sent, own = [], []
    for k, (at, along) in enumerate(gather):
        for m, (h, d) in enumerate(((0, 1), (1, 3), (1, 1), (0, 3))):
            copy = remote(
                w_ref.at[k, halves[h]], g_ref.at[k, at, halves[h]], (ws, wr), k * 6 + m, seq(along(d))
            )
            copy.start()
            sent.append(copy)
        copy = pltpu.make_async_copy(w_ref.at[k], g_ref.at[k, at], local_sems.at[k])
        copy.start()
        own.append(copy)
    wide = tok_ref[...].astype(jnp.float32)
    scale = lax.rsqrt(jnp.mean(wide * wide, axis=-1, keepdims=True) + 1e-05)
    normed = (wide * scale * gain_ref[...]).astype(jnp.bfloat16)
    for q in range(4):
        n_ref[0, q] = normed[:, q * 1024 : (q + 1) * 1024]
        for r in range(4):
            n_ref[1, q, :, r * 256 : (r + 1) * 256] = normed[:, (r * 4 + q) * 256 : (r * 4 + q + 1) * 256]
    mine = pl.ds(pl.multiple_of(e * 16, 16), 16)
    for k, (at, along) in enumerate(reduce):
        for d in (2, 1, 3):
            copy = remote(
                n_ref.at[k, (at + d) % 4], t_ref.at[k, at, mine], (ts, tr), k * 4 + d, seq(along(d))
            )
            copy.start()
            sent.append(copy)
        copy = pltpu.make_async_copy(n_ref.at[k, at], t_ref.at[k, at, mine], local_sems.at[2 + k])
        copy.start()
        own.append(copy)
    for copy in own:
        copy.wait()
    rows_of = lambda index: pl.ds(pl.multiple_of(index * 16, 16), 16)

    def pass_on(k, m, index, part, target):
        span = (slice(None), slice(0, 2), slice(2, 4))[part]
        block = t_ref.at[k, span, rows_of(index)]
        copy = remote(block, block, (xs, xr), k * 9 + m, exp(target))
        copy.start()
        sent.append(copy)

    def arrive(k, m, index, part):
        span = (slice(None), slice(0, 2), slice(2, 4))[part]
        block = t_ref.at[k, span, rows_of(index)]
        remote(block, block, (xs, xr), k * 9 + m, exp(sib)).wait_recv()

    for k, (at, along) in enumerate(reduce):
        for d in (1, 3, 2):
            remote(
                n_ref.at[k, at], t_ref.at[k, (at + 4 - d) % 4, mine], (ts, tr), k * 4 + d, seq(along(d))
            ).wait_recv()
        pass_on(k, 0, e, 0, nxt)
        pass_on(k, 1, e, 0, prv)
        pass_on(k, 2, e, 0, sib)
    for k, (at, along) in enumerate(gather):
        remote(
            w_ref.at[k, halves[0]], g_ref.at[k, (at + 3) % 4, halves[0]], (ws, wr), k * 6, seq(along(1))
        ).wait_recv()
        block = g_ref.at[k, (at + 3) % 4, halves[0]]
        copy = remote(block, block, (ws, wr), k * 6 + 4, seq(along(1)))
        copy.start()
        sent.append(copy)
        remote(
            w_ref.at[k, halves[1]], g_ref.at[k, (at + 1) % 4, halves[1]], (ws, wr), k * 6 + 1, seq(along(3))
        ).wait_recv()
        block = g_ref.at[k, (at + 1) % 4, halves[1]]
        copy = remote(block, block, (ws, wr), k * 6 + 5, seq(along(3)))
        copy.start()
        sent.append(copy)
    far = (e + 4) % 8
    for k in range(2):
        arrive(k, 0, prv, 0)
        pass_on(k, 3, prv, 1, nxt)
        pass_on(k, 4, prv, 0, sib)
        arrive(k, 1, nxt, 0)
        pass_on(k, 5, nxt, 2, prv)
        pass_on(k, 6, nxt, 0, sib)
    for k in range(2):
        arrive(k, 3, far, 1)
        pass_on(k, 7, far, 1, sib)
        arrive(k, 5, far, 2)
        pass_on(k, 8, far, 2, sib)
    for k in range(2):
        arrive(k, 2, e ^ 1, 0)
        arrive(k, 4, prv ^ 1, 0)
        arrive(k, 6, nxt ^ 1, 0)
        arrive(k, 7, far ^ 1, 1)
        arrive(k, 8, far ^ 1, 2)
    top, low = pl.ds(0, 64), pl.ds(64, 64)
    outs = (x_ref, z_ref)

    def product(k, block, put):
        def tile(c, carry):
            cols = pl.ds(pl.multiple_of(c * 256, 256), 256)
            rows = t_ref[k, block]
            total = jnp.zeros((rows.shape[0], 256), jnp.float32)
            for q in range(4):
                total = total + jnp.dot(
                    rows[:, q * 256 : (q + 1) * 256],
                    g_ref[k, q, :, cols],
                    preferred_element_type=jnp.float32,
                )
            put(cols, total)
            return carry

        lax.fori_loop(0, 4, tile, 0)

    def push(k, m, src, dst, target):
        copy = remote(src, dst, (rs, rr), k * 6 + m, seq(target))
        copy.start()
        sent.append(copy)

    def landed(k, m, dst, target):
        remote(dst, dst, (rs, rr), k * 6 + m, seq(target)).wait_recv()

    for k, (at, along) in enumerate(gather):
        later = (at + 3) % 4
        for m, (h, o) in enumerate(((0, 3), (1, 1), (1, 3), (0, 1))):
            if m >= 2:
                remote(
                    w_ref.at[k, halves[h]], g_ref.at[k, (at + o) % 4, halves[h]], (ws, wr), k * 6 + m, seq(along(1))
                ).wait_recv()
        for m, h in ((4, 0), (5, 1)):
            remote(
                w_ref.at[k, halves[h]], g_ref.at[k, (at + 2) % 4, halves[h]], (ws, wr), k * 6 + m, seq(along(1))
            ).wait_recv()
        del later
        at, along = reduce[k]
        for d in (2, 1, 3):

            def put(cols, total, k=k, d=d):
                p_ref[k, d - 1, :, cols] = total.astype(jnp.bfloat16)

            product(k, (at + d) % 4, put)
            if d == 2:
                push(k, 0, p_ref.at[k, 1, top], relay_ref.at[k, 0], along(1))
                push(k, 1, p_ref.at[k, 1, low], relay_ref.at[k, 1], along(3))
            if d == 1:
                push(k, 2, p_ref.at[k, 0, low], in_ref.at[k, 0, low], along(1))
            if d == 3:
                push(k, 3, p_ref.at[k, 2, top], in_ref.at[k, 1, top], along(3))

        def keep(cols, total, k=k):
            outs[k][:, cols] = total

        product(k, at, keep)
    for k, (at, along) in enumerate(reduce):
        landed(k, 0, relay_ref.at[k, 0], along(1))
        p_ref[k, 0, top] = (
            p_ref[k, 0, top].astype(jnp.float32) + relay_ref[k, 0].astype(jnp.float32)
        ).astype(jnp.bfloat16)
        push(k, 4, p_ref.at[k, 0, top], in_ref.at[k, 0, top], along(1))
        landed(k, 1, relay_ref.at[k, 1], along(3))
        p_ref[k, 2, low] = (
            p_ref[k, 2, low].astype(jnp.float32) + relay_ref[k, 1].astype(jnp.float32)
        ).astype(jnp.bfloat16)
        push(k, 5, p_ref.at[k, 2, low], in_ref.at[k, 1, low], along(3))
    for k, (at, along) in enumerate(reduce):
        landed(k, 2, in_ref.at[k, 0, low], along(1))
        landed(k, 3, in_ref.at[k, 1, top], along(3))
        landed(k, 4, in_ref.at[k, 0, top], along(1))
        landed(k, 5, in_ref.at[k, 1, low], along(3))
        outs[k][...] = outs[k][...] + (in_ref[k, 0].astype(jnp.float32) + in_ref[k, 1].astype(jnp.float32))
    for copy in sent:
        copy.wait_send()


def project(tokens, gain, weight, collective_id):
    width = weight.shape[2]
    out = jax.ShapeDtypeStruct((128, width), jnp.float32)
    dma = pltpu.SemaphoreType.DMA
    return pl.pallas_call(
        project_kernel,
        out_shape=(out, out),
        in_specs=[
            pl.BlockSpec(memory_space=pltpu.VMEM),
            pl.BlockSpec(memory_space=pltpu.VMEM),
            pl.BlockSpec(memory_space=pltpu.VMEM),
        ],
        out_specs=[pl.BlockSpec(memory_space=pltpu.VMEM)] * 2,
        scratch_shapes=[
            pltpu.VMEM((2, 4, 16, 1024), jnp.bfloat16),
            pltpu.VMEM((2, 4, 128, 1024), jnp.bfloat16),
            pltpu.VMEM((2, 4, 256, width), jnp.bfloat16),
            pltpu.VMEM((2, 3, 128, width), jnp.bfloat16),
            pltpu.VMEM((2, 2, 64, width), jnp.bfloat16),
            pltpu.VMEM((2, 2, 128, width), jnp.bfloat16),
            dma((12,)), dma((12,)), dma((8,)), dma((8,)), dma((18,)), dma((18,)), dma((12,)), dma((12,)),
            dma((4,)),
        ],
        compiler_params=pltpu.CompilerParams(
            collective_id=collective_id, has_side_effects=True, vmem_limit_bytes=VMEM_LIMIT
        ),
    )(tokens, gain[None, :], weight)


def mailbox(sems, sent):
    def send(i, src, dst, target):
        copy = remote(src, dst, sems, i, target)
        copy.start()
        sent.append(copy)

    def land(i, dst):
        remote(dst, dst, sems, i, {"expert": lax.axis_index("expert") ^ 1}).wait_recv()

    return send, land


def ring_gather_open(send, base, block, at, to):
    for m, (h, d) in enumerate(((0, 1), (1, 3), (1, 1), (0, 3))):
        send(base + m, block(at, h), block(at, h), to(d))


def ring_gather_pass(send, land, base, block, at, to):
    for m, h, o, d in ((0, 0, 3, 1), (1, 1, 1, 3)):
        ref = block((at + o) % 4, h)
        land(base + m, ref)
        send(base + 4 + m, ref, ref, to(d))


def expert_gather(send, land, base, block, e):
    sib, nxt, prv = expert_ring(e)
    far = (e + 4) % 8
    to = lambda index: {"expert": index}

    def pass_on(m, index, h, target):
        ref = block(index, h)
        send(base + m, ref, ref, to(target))

    pass_on(0, e, None, nxt)
    pass_on(1, e, None, prv)
    pass_on(2, e, None, sib)
    land(base + 0, block(prv, None))
    pass_on(3, prv, 0, nxt)
    pass_on(4, prv, None, sib)
    land(base + 1, block(nxt, None))
    pass_on(5, nxt, 1, prv)
    pass_on(6, nxt, None, sib)
    land(base + 3, block(far, 0))
    pass_on(7, far, 0, sib)
    land(base + 5, block(far, 1))
    pass_on(8, far, 1, sib)
    land(base + 2, block(sib, None))
    land(base + 4, block(prv ^ 1, None))
    land(base + 6, block(nxt ^ 1, None))
    land(base + 7, block(far ^ 1, 0))
    land(base + 8, block(far ^ 1, 1))


def expert_reduce(send, land, base, src, e, sib_ref, p_ref, relay_ref, in_ref):
    sib, nxt, prv = expert_ring(e)
    to = lambda index: {"expert": index}
    wide = lambda value: value.astype(jnp.float32)
    half = (pl.ds(0, 32), pl.ds(32, 32))
    for d in (2, 1, 3, 0):
        send(base + d, src(((e + 2 * d) % 8) ^ 1), sib_ref.at[d], to(sib))
    for d in (2, 1, 3):
        land(base + d, sib_ref.at[d])
        p_ref[d - 1] = (wide(src((e + 2 * d) % 8)[...]) + wide(sib_ref[d])).astype(jnp.bfloat16)
        if d == 2:
            send(base + 4, p_ref.at[1, half[0]], relay_ref.at[0], to(nxt))
            send(base + 5, p_ref.at[1, half[1]], relay_ref.at[1], to(prv))
        if d == 1:
            send(base + 6, p_ref.at[0, half[1]], in_ref.at[0, half[1]], to(nxt))
        if d == 3:
            send(base + 7, p_ref.at[2, half[0]], in_ref.at[1, half[0]], to(prv))
    land(base + 4, relay_ref.at[0])
    p_ref[0, half[0]] = (wide(p_ref[0, half[0]]) + wide(relay_ref[0])).astype(jnp.bfloat16)
    send(base + 8, p_ref.at[0, half[0]], in_ref.at[0, half[0]], to(nxt))
    land(base + 5, relay_ref.at[1])
    p_ref[2, half[1]] = (wide(p_ref[2, half[1]]) + wide(relay_ref[1])).astype(jnp.bfloat16)
    send(base + 9, p_ref.at[2, half[1]], in_ref.at[1, half[1]], to(prv))
    land(base + 0, sib_ref.at[0])
    total = wide(src(e)[...]) + wide(sib_ref[0])
    land(base + 6, in_ref.at[0, half[1]])
    land(base + 7, in_ref.at[1, half[0]])
    land(base + 8, in_ref.at[0, half[0]])
    land(base + 9, in_ref.at[1, half[1]])
    return total + (wide(in_ref[0]) + wide(in_ref[1]))


def swap_blocks(send, land, base, out_ref, got_ref, s):
    for d in (10, 5, 6, 7, 9, 11, 13, 14, 15, 8, 2, 1, 3, 4, 12):
        to = (s + d) % 16
        send(base + d, out_ref.at[to], got_ref.at[s], {"seq": to})
    got_ref[s] = out_ref[s]
    for d in range(1, 16):
        land(base + d, got_ref.at[(s + 16 - d) % 16])


def all_partners(s, e):
    return [{"seq": (s + d) % 16} for d in range(1, 16)] + [{"expert": i} for i in expert_ring(e)]


def mix_kernel(
    gated_ref, w_ref, tok_ref, gain_ref, place_ref, order_ref, resid_ref, pool_ref,
    gg_ref, t_ref, sib_ref, p_ref, relay_ref, in_ref, u_ref, v_ref, n_ref, out_ref, got_ref,
    gs, gr, es, er, ys, yr, ds, dr, xs, xr,
):
    s = lax.axis_index("seq")
    e = lax.axis_index("expert")
    at, along = ring_of(s, 0)
    to = lambda d: {"seq": along(d)}
    greet(all_partners(s, e))
    sent = []
    gsend, gland = mailbox((gs, gr), sent)
    esend, eland = mailbox((es, er), sent)
    ysend, yland = mailbox((ys, yr), sent)
    dsend, dland = mailbox((ds, dr), sent)
    xsend, xland = mailbox((xs, xr), sent)
    gg_ref[at] = gated_ref[...]
    span = (pl.ds(0, 64), pl.ds(64, 64))
    block = lambda i, h: gg_ref.at[i, span[h]]
    ring_gather_open(gsend, 0, block, at, to)

    def product(y):
        def tile(q, carry):
            total = jnp.dot(gg_ref[y], w_ref[q], preferred_element_type=jnp.float32)
            rows = pl.ds(pl.multiple_of(y * 16, 16), 16)
            cols = pl.ds(pl.multiple_of(q * 256, 256), 256)
            t_ref[:, rows, cols] = total.astype(jnp.bfloat16).reshape(8, 16, 256)
            return carry

        lax.fori_loop(0, 4, tile, 0)

    product(at)
    ring_gather_pass(gsend, gland, 0, block, at, to)
    gland(2, block((at + 3) % 4, 1))
    product((at + 3) % 4)
    gland(3, block((at + 1) % 4, 0))
    product((at + 1) % 4)
    gland(4, block((at + 2) % 4, 0))
    gland(5, block((at + 2) % 4, 1))
    product((at + 2) % 4)
    total = expert_reduce(
        esend, eland, 0, lambda i: t_ref.at[i], e, sib_ref, p_ref, relay_ref, in_ref
    )
    for y in range(4):
        u_ref[y] = total[y * 16 : (y + 1) * 16].astype(jnp.bfloat16)
    for d in (2, 1, 3):
        ysend(d, u_ref.at[(at + d) % 4], v_ref.at[at], to(d))
    v_ref[at] = u_ref[at]
    for d in (1, 3, 2):
        yland(d, v_ref.at[(at + 4 - d) % 4])
    mixer = jnp.concatenate(
        [v_ref[y][:, z * 256 : (z + 1) * 256] for z in range(4) for y in range(4)], axis=1
    )
    resid = (tok_ref[...].astype(jnp.float32) + mixer.astype(jnp.float32)).astype(jnp.bfloat16)
    resid_ref[...] = resid
    wide = resid.astype(jnp.float32)
    scale = lax.rsqrt(jnp.mean(wide * wide, axis=-1, keepdims=True) + 1e-05)
    normed = (wide * scale * gain_ref[...]).astype(jnp.bfloat16)
    for q in range(4):
        n_ref[q * 16 : (q + 1) * 16] = normed[:, q * 1024 : (q + 1) * 1024]
    out_ref[...] = (
        jnp.dot(place_ref[...], n_ref[...], preferred_element_type=jnp.float32)
        .astype(jnp.bfloat16)
        .reshape(16, 16, 1024)
    )
    swap_blocks(dsend, dland, 0, out_ref, got_ref, s)
    rows = jnp.dot(
        order_ref[...], got_ref[...].reshape(256, 1024), preferred_element_type=jnp.float32
    ).astype(jnp.bfloat16)
    for q in range(4):
        pool_ref[e, :, q * 1024 : (q + 1) * 1024] = rows[q * 64 : (q + 1) * 64]
    whole = (pl.ds(0, 32), pl.ds(32, 32))
    expert_gather(
        xsend, xland, 0, lambda i, h: pool_ref.at[i] if h is None else pool_ref.at[i, whole[h]], e
    )
    for copy in sent:
        copy.wait_send()


def mix(gated, weight, tokens, gain, place, order, collective_id):
    dma = pltpu.SemaphoreType.DMA
    bf16 = jnp.bfloat16
    return pl.pallas_call(
        mix_kernel,
        out_shape=(
            jax.ShapeDtypeStruct((16, 4096), bf16),
            jax.ShapeDtypeStruct((8, 64, 4096), bf16),
        ),
        in_specs=[pl.BlockSpec(memory_space=pltpu.VMEM)] * 6,
        out_specs=[pl.BlockSpec(memory_space=pltpu.VMEM)] * 2,
        scratch_shapes=[
            pltpu.VMEM((4, 128, 1024), bf16),
            pltpu.VMEM((8, 64, 1024), bf16),
            pltpu.VMEM((4, 64, 1024), bf16),
            pltpu.VMEM((3, 64, 1024), bf16),
            pltpu.VMEM((2, 32, 1024), bf16),
            pltpu.VMEM((2, 64, 1024), bf16),
            pltpu.VMEM((4, 16, 1024), bf16),
            pltpu.VMEM((4, 16, 1024), bf16),
            pltpu.VMEM((64, 1024), bf16),
            pltpu.VMEM((16, 16, 1024), bf16),
            pltpu.VMEM((16, 16, 1024), bf16),
            dma((6,)), dma((6,)), dma((10,)), dma((10,)), dma((4,)), dma((4,)),
            dma((16,)), dma((16,)), dma((9,)), dma((9,)),
        ],
        compiler_params=pltpu.CompilerParams(
            collective_id=collective_id, has_side_effects=True, vmem_limit_bytes=VMEM_LIMIT
        ),
    )(gated, weight, tokens, gain[None, :], place, order)


def finish_kernel(
    terms_ref, resid_ref, back_ref, weigh_ref, o_ref,
    sib_ref, p_ref, relay_ref, in_ref, stack_ref, out_ref, got_ref,
    es, er, ds, dr,
):
    s = lax.axis_index("seq")
    e = lax.axis_index("expert")
    greet(all_partners(s, e))
    sent = []
    esend, eland = mailbox((es, er), sent)
    dsend, dland = mailbox((ds, dr), sent)
    total = expert_reduce(
        esend, eland, 0, lambda i: terms_ref.at[i], e, sib_ref, p_ref, relay_ref, in_ref
    ).astype(jnp.bfloat16)
    for q in range(4):
        stack_ref[q * 64 : (q + 1) * 64] = total[:, q * 1024 : (q + 1) * 1024]
    out_ref[...] = (
        jnp.dot(back_ref[...], stack_ref[...], preferred_element_type=jnp.float32)
        .astype(jnp.bfloat16)
        .reshape(16, 16, 1024)
    )
    swap_blocks(dsend, dland, 0, out_ref, got_ref, s)
    values = got_ref[...].reshape(256, 1024)
    moe = jnp.dot(weigh_ref[0], values, preferred_element_type=jnp.float32) + jnp.dot(
        weigh_ref[1], values, preferred_element_type=jnp.float32
    )
    for q in range(4):
        cols = slice(q * 1024, (q + 1) * 1024)
        o_ref[:, cols] = (
            resid_ref[:, cols].astype(jnp.float32) + moe[q * 16 : (q + 1) * 16]
        ).astype(jnp.bfloat16)
    for copy in sent:
        copy.wait_send()


def finish(terms, resid, back, weigh, collective_id):
    dma = pltpu.SemaphoreType.DMA
    bf16 = jnp.bfloat16
    return pl.pallas_call(
        finish_kernel,
        out_shape=jax.ShapeDtypeStruct((16, 4096), bf16),
        in_specs=[pl.BlockSpec(memory_space=pltpu.VMEM)] * 4,
        out_specs=pl.BlockSpec(memory_space=pltpu.VMEM),
        scratch_shapes=[
            pltpu.VMEM((4, 64, 4096), bf16),
            pltpu.VMEM((3, 64, 4096), bf16),
            pltpu.VMEM((2, 32, 4096), bf16),
            pltpu.VMEM((2, 64, 4096), bf16),
            pltpu.VMEM((256, 1024), bf16),
            pltpu.VMEM((16, 16, 1024), bf16),
            pltpu.VMEM((16, 16, 1024), bf16),
            dma((10,)), dma((10,)), dma((16,)), dma((16,)),
        ],
        compiler_params=pltpu.CompilerParams(
            collective_id=collective_id, has_side_effects=True, vmem_limit_bytes=VMEM_LIMIT
        ),
    )(terms, resid, back, weigh)


def lanes_of(value, width):
    return jnp.concatenate([value] * (width // 128), axis=1)


def split_sum(value):
    top = value.astype(jnp.bfloat16)
    low = (value - top.astype(jnp.float32)).astype(jnp.bfloat16)
    width = value.shape[1]
    return jnp.concatenate(
        [jnp.broadcast_to(top.astype(jnp.float32), (8, width)), jnp.broadcast_to(low.astype(jnp.float32), (8, width))],
        axis=0,
    ).astype(jnp.bfloat16)


def read_end(ref, index):
    final = ref[index, :STATE].astype(jnp.float32)
    rows = ref[index, STATE:].astype(jnp.float32)
    return final, rows[0:1] + rows[8:9]


def scan_kernel(
    x_ref, z_ref, taps_ref, cbias_ref, xproj_ref, dtw_ref, dtb_ref, a_ref, skip_ref, w_ref,
    out_ref, g_ref,
    pad_ref, inner_ref, part_ref, rbox_ref, proj_ref, b_ref, c_ref, step_ref, u_ref, ybox_ref, zbox_ref, zmsg_ref,
    ws, wr, as_, ar, bs, br, ys, yr, zs, zr, edge_s, edge_r, local_sem,
):
    s = lax.axis_index("seq")
    e = lax.axis_index("expert")
    at_y, along_y = ring_of(s, 0)
    at_z, along_z = ring_of(s, 1)
    tokens, width = x_ref.shape
    greet(
        [{"expert": (e + d) % 8} for d in range(1, 8)]
        + [{"seq": (s + 1) % 16}, {"seq": (s + 15) % 16}]
        + [{"seq": along_y(d)} for d in (1, 2, 3)]
        + [{"seq": along_z(d)} for d in (1, 2, 3)]
    )
    sent = []
    wsend, wland = mailbox((ws, wr), sent)
    asend, aland = mailbox((as_, ar), sent)
    bsend, bland = mailbox((bs, br), sent)
    ysend, yland = mailbox((ys, yr), sent)
    zsend, zland = mailbox((zs, zr), sent)
    esend, eland = mailbox((edge_s, edge_r), sent)
    esend(0, x_ref.at[pl.ds(tokens - 8, 8)], pad_ref.at[pl.ds(0, 8)], {"seq": (s + 1) % 16})
    own = pltpu.make_async_copy(w_ref, g_ref.at[at_z], local_sem)
    own.start()
    half = w_ref.shape[0] // 2
    span = (pl.ds(0, half), pl.ds(half, half))
    block = lambda i, h: g_ref.at[i, span[h]]
    to_z = lambda d: {"seq": along_z(d)}
    own.wait()
    ring_gather_open(wsend, 0, block, at_z, to_z)
    pad_ref[8:] = x_ref[...]
    eland(0, pad_ref.at[pl.ds(0, 8)])
    pad_ref[:8] = jnp.where(s > 0, pad_ref[:8], 0.0)
    part = jnp.zeros((tokens, xproj_ref.shape[1]), jnp.float32)
    for at in range(0, width, 256):
        cols = slice(at, at + 256)
        conv = jnp.broadcast_to(cbias_ref[:, cols], (tokens, 256))
        for tap in range(CONV):
            conv = conv + taps_ref[tap : tap + 1, cols] * pad_ref[5 + tap : 5 + tap + tokens, cols]
        inner = (conv / (1.0 + jnp.exp(-conv))).astype(jnp.bfloat16)
        inner_ref[:, cols] = inner
        part = part + jnp.dot(inner, xproj_ref[cols, :], preferred_element_type=jnp.float32)
    part_ref[...] = part.astype(jnp.bfloat16).reshape(8, tokens // 8, part.shape[1])
    for d in (4, 5, 3, 2, 6, 1, 7):
        to = (e + d) % 8
        asend(d, part_ref.at[to], rbox_ref.at[e], {"expert": to})
    rbox_ref[e] = part_ref[e]
    for d in range(1, 8):
        aland(d, rbox_ref.at[(e + 8 - d) % 8])
    proj_ref[e] = jnp.sum(rbox_ref[...].astype(jnp.float32), axis=0)
    for d in (4, 5, 3, 2, 6, 1, 7):
        bsend(d, proj_ref.at[e], proj_ref.at[e], {"expert": (e + d) % 8})
    ring_gather_pass(wsend, wland, 0, block, at_z, to_z)
    for d in range(1, 8):
        bland(d, proj_ref.at[(e + 8 - d) % 8])
    low = proj_ref[:, :, :RANK].reshape(tokens, RANK).astype(jnp.bfloat16)
    for at in range(0, width, 256):
        cols = slice(at, at + 256)
        raw = jnp.dot(low, dtw_ref[:, cols], preferred_element_type=jnp.float32) + dtb_ref[:, cols]
        step = jnp.maximum(raw, 0.0) + jnp.log1p(jnp.exp(-jnp.abs(raw)))
        step_ref[:, cols] = step
        u_ref[:, cols] = step * inner_ref[:, cols].astype(jnp.float32)
    same = lax.broadcasted_iota(jnp.int32, (1, STATE, STATE), 1) == lax.broadcasted_iota(
        jnp.int32, (1, STATE, STATE), 2
    )

    def spread(i, carry):
        rows = pl.ds(pl.multiple_of(i * 16, 16), 16)
        for ref, at in ((b_ref, RANK), (c_ref, RANK + STATE)):
            values = proj_ref[i][:, at : at + STATE]
            column = jnp.sum(jnp.where(same, values[:, None, :], 0.0), axis=-1, keepdims=True)
            ref[rows] = jnp.broadcast_to(column, (16, STATE, 128))
        return carry

    lax.fori_loop(0, 8, spread, 0)
    rate = a_ref[...]

    def advance(state, step8, u8, r, t):
        decay = jnp.exp(-(step8[r : r + 1, :] * rate))
        return decay * state + lanes_of(b_ref[t], width) * u8[r : r + 1, :]

    def first(g, state):
        base = pl.multiple_of(g * 8, 8)
        step8 = step_ref[pl.ds(base, 8), :]
        u8 = u_ref[pl.ds(base, 8), :]
        for r in range(8):
            state = advance(state, step8, u8, r, base + r)
        return state

    final = lax.fori_loop(0, tokens // 8, first, jnp.zeros_like(rate))
    ybox_ref[at_y, :STATE] = final.astype(jnp.bfloat16)
    ybox_ref[at_y, STATE:] = split_sum(jnp.sum(step_ref[...], axis=0, keepdims=True))
    for d in (2, 1, 3):
        ysend(d, ybox_ref.at[at_y], ybox_ref.at[at_y], {"seq": along_y(d)})
    for d in (1, 3, 2):
        yland(d, ybox_ref.at[(at_y + 4 - d) % 4])
    plane = jnp.zeros_like(rate)
    total = jnp.zeros((1, width), jnp.float32)
    for y in range(4):
        end, summed = read_end(ybox_ref, y)
        plane = jnp.exp(-(summed * rate)) * plane + end
        total = total + summed
    zmsg_ref[:STATE] = plane.astype(jnp.bfloat16)
    zmsg_ref[STATE:] = split_sum(total)
    for d in (2, 1, 3):
        zsend(d, zmsg_ref, zbox_ref.at[at_z], to_z(d))
    zbox_ref[at_z] = zmsg_ref[...]
    for d in (1, 3, 2):
        zland(d, zbox_ref.at[(at_z + 4 - d) % 4])
    start = jnp.zeros_like(rate)
    for ref, at in ((zbox_ref, at_z), (ybox_ref, at_y)):
        for i in range(3):
            end, summed = read_end(ref, i)
            start = jnp.where(i < at, jnp.exp(-(summed * rate)) * start + end, start)

    def second(g, state):
        base = pl.multiple_of(g * 8, 8)
        step8 = step_ref[pl.ds(base, 8), :]
        u8 = u_ref[pl.ds(base, 8), :]
        rows = []
        for r in range(8):
            state = advance(state, step8, u8, r, base + r)
            rows.append(jnp.sum(lanes_of(c_ref[base + r], width) * state, axis=0, keepdims=True))
        u_ref[pl.ds(base, 8), :] = jnp.concatenate(rows, axis=0)
        return state

    lax.fori_loop(0, tokens // 8, second, start)
    for at in range(0, width, 256):
        cols = slice(at, at + 256)
        z = z_ref[:, cols]
        out_ref[:, cols] = (
            (u_ref[:, cols] + skip_ref[:, cols] * inner_ref[:, cols].astype(jnp.float32))
            * (z / (1.0 + jnp.exp(-z)))
        ).astype(jnp.bfloat16)
    for m, h, o in ((2, 1, 3), (3, 0, 1), (4, 0, 2), (5, 1, 2)):
        wland(m, block((at_z + o) % 4, h))
    for copy in sent:
        copy.wait_send()


def scan(x, z, taps, conv_bias, xproj, dt_weight, dt_bias, rate, skip, weight, collective_id):
    dma = pltpu.SemaphoreType.DMA
    tokens, width = x.shape
    bf16, f32 = jnp.bfloat16, jnp.float32
    return pl.pallas_call(
        scan_kernel,
        out_shape=(
            jax.ShapeDtypeStruct((tokens, width), bf16),
            jax.ShapeDtypeStruct((4, *weight.shape), bf16),
        ),
        in_specs=[pl.BlockSpec(memory_space=pltpu.VMEM)] * 10,
        out_specs=[pl.BlockSpec(memory_space=pltpu.VMEM)] * 2,
        scratch_shapes=[
            pltpu.VMEM((tokens + 8, width), f32),
            pltpu.VMEM((tokens, width), bf16),
            pltpu.VMEM((8, 16, xproj.shape[1]), bf16),
            pltpu.VMEM((8, 16, xproj.shape[1]), bf16),
            pltpu.VMEM((8, 16, xproj.shape[1]), f32),
            pltpu.VMEM((tokens, STATE, 128), f32),
            pltpu.VMEM((tokens, STATE, 128), f32),
            pltpu.VMEM((tokens, width), f32),
            pltpu.VMEM((tokens, width), f32),
            pltpu.VMEM((4, 2 * STATE, width), bf16),
            pltpu.VMEM((4, 2 * STATE, width), bf16),
            pltpu.VMEM((2 * STATE, width), bf16),
            dma((6,)), dma((6,)), dma((8,)), dma((8,)), dma((8,)), dma((8,)),
            dma((4,)), dma((4,)), dma((4,)), dma((4,)), dma((1,)), dma((1,)), dma,
        ],
        compiler_params=pltpu.CompilerParams(
            collective_id=collective_id, has_side_effects=True, vmem_limit_bytes=VMEM_LIMIT
        ),
    )(
        x, z, taps, conv_bias[None, :], xproj, dt_weight, dt_bias[None, :], rate, skip[None, :], weight
    )


def per_device(
    tokens,
    gain_mamba,
    in_weight,
    conv_weight,
    conv_bias,
    xproj_weight,
    dt_weight,
    dt_bias,
    a_rate,
    skip_d,
    out_weight,
    gain_moe,
    expert_ids,
    gate_weights,
    w_gate,
    w_up,
    w_down,
):
    rows, dim = tokens.shape
    n_seq = lax.axis_size("seq")
    n_exp = lax.axis_size("expert")
    xpart, zpart = project(tokens, gain_mamba, in_weight, 3)
    gated, mixer_weight = scan(
        xpart, zpart, conv_weight, conv_bias, xproj_weight, dt_weight, dt_bias, a_rate, skip_d, out_weight, 1
    )
    capacity = max(2, 4 * rows // n_seq)
    slots_all = n_seq * capacity
    flat_ids = expert_ids.reshape(-1)
    order = jnp.arange(flat_ids.shape[0], dtype=jnp.int32)
    same = (flat_ids[:, None] == flat_ids[None, :]) & (order[None, :] < order[:, None])
    slot = jnp.sum(same.astype(jnp.int32), axis=1)
    target = flat_ids * capacity + slot
    places = target[:, None] == jnp.arange(slots_all, dtype=jnp.int32)[None, :]
    eye = jnp.eye(4, dtype=jnp.float32)
    by_row = places.reshape(rows, TOP, n_seq, capacity)
    chosen = jnp.any(by_row, axis=1).astype(jnp.float32)
    place = jnp.einsum("rpi,qk->pqikr", chosen, eye).reshape(4 * slots_all, 4 * rows).astype(jnp.bfloat16)
    weighting = jnp.sum(
        jnp.where(by_row, gate_weights[:, :, None, None], 0.0), axis=1
    )
    weigh = (eye[:, None, None, :, None] * weighting[None, :, :, None, :]).reshape(4 * rows, 4 * slots_all)
    weigh_top = weigh.astype(jnp.bfloat16)
    weigh = jnp.stack([weigh_top, (weigh - weigh_top.astype(jnp.float32)).astype(jnp.bfloat16)])
    line = jnp.arange(4 * slots_all, dtype=jnp.int32)
    moved = (line // 4 % 4) * slots_all + line // 16 * 4 + line % 4
    back = (moved[:, None] == line[None, :]).astype(jnp.bfloat16)
    resid, pooled = mix(gated, mixer_weight, tokens, gain_moe, place, back.T, 4)
    pooled = pooled.reshape(n_exp * slots_all, dim)
    gate = jnp.dot(pooled, w_gate[0], preferred_element_type=jnp.float32)
    upper = jnp.dot(pooled, w_up[0], preferred_element_type=jnp.float32)
    act = (jax.nn.silu(gate) * upper).astype(jnp.bfloat16)
    terms = jnp.dot(act, w_down[0], preferred_element_type=jnp.float32).astype(jnp.bfloat16)
    return finish(terms.reshape(n_exp, slots_all, dim), resid, back, weigh, 5)


def solution(mesh):
    placed = (
        P(("seq", "expert"), None),
        P(),
        P(None, "seq", "expert"),
        P(None, "expert"),
        P("expert"),
        P("expert", None),
        P(None, "expert"),
        P("expert"),
        P(None, "expert"),
        P("expert"),
        P("expert", "seq"),
        P(),
        P(("seq", "expert"), None),
        P(("seq", "expert"), None),
        P("seq", None, "expert"),
        P("seq", None, "expert"),
        P("seq", "expert", None),
    )
    return jax.shard_map(
        per_device,
        mesh=mesh,
        in_specs=placed,
        out_specs=P(("seq", "expert"), None),
        check_vma=False,
    )
```

```python
import functools

import jax
import jax.numpy as jnp
from jax import lax
from jax.experimental import pallas as pl
from jax.experimental.pallas import tpu as pltpu
from jax.sharding import PartitionSpec as P

MESH = pl.DeviceIdType.MESH
VMEM_LIMIT = 56 * 2**20
PARTS = 2

STATE = 16
CONV = 4
RANK = 256
TOP = 2


def ring_of(axis_seq, kind):
    z, y = axis_seq // 4, axis_seq % 4
    if kind == 0:
        return y, lambda d: z * 4 + (y + d) % 4
    return z, lambda d: ((z + d) % 4) * 4 + y


def remote(src, dst, sems, index, target):
    return pltpu.make_async_remote_copy(
        src_ref=src,
        dst_ref=dst,
        send_sem=sems[0].at[index],
        recv_sem=sems[1].at[index],
        device_id=target,
        device_id_type=MESH,
    )


def greet(targets):
    barrier = pltpu.get_barrier_semaphore()
    for target in targets:
        pl.semaphore_signal(barrier, inc=1, device_id=target, device_id_type=MESH)
    pl.semaphore_wait(barrier, len(targets))


def expert_ring(e):
    return (e ^ 1, (e + 2) % 8, (e + 6) % 8)


def project_kernel(
    tok_ref, gain_ref, w_ref, x_ref, z_ref,
    n_ref, t_ref, g_ref, p_ref, relay_ref, in_ref,
    ws, wr, ts, tr, xs, xr, rs, rr, local_sems,
):
    s = lax.axis_index("seq")
    e = lax.axis_index("expert")
    at_y, along_y = ring_of(s, 0)
    at_z, along_z = ring_of(s, 1)
    sib, nxt, prv = expert_ring(e)
    gather = ((at_y, along_y), (at_z, along_z))
    reduce = ((at_z, along_z), (at_y, along_y))
    seq = lambda index: {"seq": index}
    exp = lambda index: {"expert": index}
    greet(
        [seq(along_y(d)) for d in (1, 2, 3)]
        + [seq(along_z(d)) for d in (1, 2, 3)]
        + [exp(sib), exp(nxt), exp(prv)]
    )
    half = w_ref.shape[1] // 2
    halves = (pl.ds(0, half), pl.ds(half, half))
    sent, own = [], []
    wide_cols = w_ref.shape[2] // PARTS
    cols_of = [pl.ds(c * wide_cols, wide_cols) for c in range(PARTS)]

    def open_part(c):
        for k, (at, along) in enumerate(gather):
            for m, (h, d) in enumerate(((0, 1), (1, 3), (1, 1), (0, 3))):
                copy = remote(
                    w_ref.at[k, halves[h], cols_of[c]],
                    g_ref.at[k, at, halves[h], cols_of[c]],
                    (ws, wr),
                    (k * PARTS + c) * 6 + m,
                    seq(along(d)),
                )
                copy.start()
                sent.append(copy)

    def land_part(c, k, m, o, h):
        ref = g_ref.at[k, (gather[k][0] + o) % 4, halves[h], cols_of[c]]
        remote(ref, ref, (ws, wr), (k * PARTS + c) * 6 + m, seq(gather[k][1](1))).wait_recv()
        return ref

    def pass_part(c):
        for k, (at, along) in enumerate(gather):
            for m, o, h, d in ((0, 3, 0, 1), (1, 1, 1, 3)):
                ref = land_part(c, k, m, o, h)
                copy = remote(ref, ref, (ws, wr), (k * PARTS + c) * 6 + 4 + m, seq(along(d)))
                copy.start()
                sent.append(copy)

    open_part(0)
    for k, (at, along) in enumerate(gather):
        copy = pltpu.make_async_copy(w_ref.at[k], g_ref.at[k, at], local_sems.at[k])
        copy.start()
        own.append(copy)
    wide = tok_ref[...].astype(jnp.float32)
    scale = lax.rsqrt(jnp.mean(wide * wide, axis=-1, keepdims=True) + 1e-05)
    normed = (wide * scale * gain_ref[...]).astype(jnp.bfloat16)
    for q in range(4):
        n_ref[0, q] = normed[:, q * 1024 : (q + 1) * 1024]
        for r in range(4):
            n_ref[1, q, :, r * 256 : (r + 1) * 256] = normed[:, (r * 4 + q) * 256 : (r * 4 + q + 1) * 256]
    mine = pl.ds(pl.multiple_of(e * 16, 16), 16)
    for k, (at, along) in enumerate(reduce):
        for d in (2, 1, 3):
            copy = remote(
                n_ref.at[k, (at + d) % 4], t_ref.at[k, at, mine], (ts, tr), k * 4 + d, seq(along(d))
            )
            copy.start()
            sent.append(copy)
        copy = pltpu.make_async_copy(n_ref.at[k, at], t_ref.at[k, at, mine], local_sems.at[2 + k])
        copy.start()
        own.append(copy)
    for copy in own:
        copy.wait()
    rows_of = lambda index: pl.ds(pl.multiple_of(index * 16, 16), 16)

    def pass_on(k, m, index, part, target):
        span = (slice(None), slice(0, 2), slice(2, 4))[part]
        block = t_ref.at[k, span, rows_of(index)]
        copy = remote(block, block, (xs, xr), k * 9 + m, exp(target))
        copy.start()
        sent.append(copy)

    def arrive(k, m, index, part):
        span = (slice(None), slice(0, 2), slice(2, 4))[part]
        block = t_ref.at[k, span, rows_of(index)]
        remote(block, block, (xs, xr), k * 9 + m, exp(sib)).wait_recv()

    for k, (at, along) in enumerate(reduce):
        for d in (1, 3, 2):
            remote(
                n_ref.at[k, at], t_ref.at[k, (at + 4 - d) % 4, mine], (ts, tr), k * 4 + d, seq(along(d))
            ).wait_recv()
        pass_on(k, 0, e, 0, nxt)
        pass_on(k, 1, e, 0, prv)
        pass_on(k, 2, e, 0, sib)
    pass_part(0)
    if PARTS > 1:
        open_part(1)
    far = (e + 4) % 8
    for k in range(2):
        arrive(k, 0, prv, 0)
        pass_on(k, 3, prv, 1, nxt)
        pass_on(k, 4, prv, 0, sib)
        arrive(k, 1, nxt, 0)
        pass_on(k, 5, nxt, 2, prv)
        pass_on(k, 6, nxt, 0, sib)
    for k in range(2):
        arrive(k, 3, far, 1)
        pass_on(k, 7, far, 1, sib)
        arrive(k, 5, far, 2)
        pass_on(k, 8, far, 2, sib)
    for k in range(2):
        arrive(k, 2, e ^ 1, 0)
        arrive(k, 4, prv ^ 1, 0)
        arrive(k, 6, nxt ^ 1, 0)
        arrive(k, 7, far ^ 1, 1)
        arrive(k, 8, far ^ 1, 2)
    top, low = pl.ds(0, 64), pl.ds(64, 64)
    outs = (x_ref, z_ref)

    def product(k, block, c, put):
        rows = t_ref[k, block]
        for at in range(c * wide_cols, (c + 1) * wide_cols, 256):
            cols = pl.ds(at, 256)
            total = jnp.zeros((rows.shape[0], 256), jnp.float32)
            for q in range(4):
                total = total + jnp.dot(
                    rows[:, q * 256 : (q + 1) * 256],
                    g_ref[k, q, :, cols],
                    preferred_element_type=jnp.float32,
                )
            put(cols, total)

    def push(k, c, m, src, dst, target):
        copy = remote(src, dst, (rs, rr), (k * PARTS + c) * 6 + m, seq(target))
        copy.start()
        sent.append(copy)

    def landed(k, c, m, dst):
        remote(dst, dst, (rs, rr), (k * PARTS + c) * 6 + m, seq(along_y(1))).wait_recv()

    def multiply(c):
        here = cols_of[c]
        for d in (2, 1, 3, 0):
            for k, (at, along) in enumerate(reduce):

                def put(cols, total, k=k, d=d):
                    if d:
                        p_ref[k, d - 1, :, cols] = total.astype(jnp.bfloat16)
                    else:
                        outs[k][:, cols] = total

                product(k, (at + d) % 4, c, put)
                if d == 2:
                    push(k, c, 0, p_ref.at[k, 1, top, here], relay_ref.at[k, 0, :, here], along(1))
                    push(k, c, 1, p_ref.at[k, 1, low, here], relay_ref.at[k, 1, :, here], along(3))
                if d == 1:
                    push(k, c, 2, p_ref.at[k, 0, low, here], in_ref.at[k, 0, low, here], along(1))
                if d == 3:
                    push(k, c, 3, p_ref.at[k, 2, top, here], in_ref.at[k, 1, top, here], along(3))

    def add_on_the_way(c):
        here = cols_of[c]
        for k, (at, along) in enumerate(reduce):
            for m, j, rows, side, d in ((0, 0, top, 0, 1), (1, 2, low, 1, 3)):
                landed(k, c, m, relay_ref.at[k, m, :, here])
                p_ref[k, j, rows, here] = (
                    p_ref[k, j, rows, here].astype(jnp.float32)
                    + relay_ref[k, m, :, here].astype(jnp.float32)
                ).astype(jnp.bfloat16)
                push(k, c, 4 + m, p_ref.at[k, j, rows, here], in_ref.at[k, side, rows, here], along(d))

    def close(c):
        here = cols_of[c]
        for k in range(2):
            landed(k, c, 2, in_ref.at[k, 0, low, here])
            landed(k, c, 3, in_ref.at[k, 1, top, here])
            landed(k, c, 4, in_ref.at[k, 0, top, here])
            landed(k, c, 5, in_ref.at[k, 1, low, here])
            outs[k][:, here] = outs[k][:, here] + (
                in_ref[k, 0, :, here].astype(jnp.float32) + in_ref[k, 1, :, here].astype(jnp.float32)
            )

    for c in range(PARTS):
        for k in range(2):
            for m, o, h in ((2, 3, 1), (3, 1, 0), (4, 2, 0), (5, 2, 1)):
                land_part(c, k, m, o, h)
        multiply(c)
        if c + 1 < PARTS:
            pass_part(c + 1)
        if c + 2 < PARTS:
            open_part(c + 2)
        add_on_the_way(c)
        if c:
            close(c - 1)
    close(PARTS - 1)
    for copy in sent:
        copy.wait_send()


def project(tokens, gain, weight, collective_id):
    width = weight.shape[2]
    out = jax.ShapeDtypeStruct((128, width), jnp.float32)
    dma = pltpu.SemaphoreType.DMA
    return pl.pallas_call(
        project_kernel,
        out_shape=(out, out),
        in_specs=[
            pl.BlockSpec(memory_space=pltpu.VMEM),
            pl.BlockSpec(memory_space=pltpu.VMEM),
            pl.BlockSpec(memory_space=pltpu.VMEM),
        ],
        out_specs=[pl.BlockSpec(memory_space=pltpu.VMEM)] * 2,
        scratch_shapes=[
            pltpu.VMEM((2, 4, 16, 1024), jnp.bfloat16),
            pltpu.VMEM((2, 4, 128, 1024), jnp.bfloat16),
            pltpu.VMEM((2, 4, 256, width), jnp.bfloat16),
            pltpu.VMEM((2, 3, 128, width), jnp.bfloat16),
            pltpu.VMEM((2, 2, 64, width), jnp.bfloat16),
            pltpu.VMEM((2, 2, 128, width), jnp.bfloat16),
            dma((12 * PARTS,)), dma((12 * PARTS,)), dma((8,)), dma((8,)), dma((18,)), dma((18,)),
            dma((12 * PARTS,)), dma((12 * PARTS,)),
            dma((4,)),
        ],
        compiler_params=pltpu.CompilerParams(
            collective_id=collective_id, has_side_effects=True, vmem_limit_bytes=VMEM_LIMIT
        ),
    )(tokens, gain[None, :], weight)


def mailbox(sems, sent):
    def send(i, src, dst, target):
        copy = remote(src, dst, sems, i, target)
        copy.start()
        sent.append(copy)

    def land(i, dst):
        remote(dst, dst, sems, i, {"expert": lax.axis_index("expert") ^ 1}).wait_recv()

    return send, land


def ring_gather_open(send, base, block, at, to):
    for m, (h, d) in enumerate(((0, 1), (1, 3), (1, 1), (0, 3))):
        send(base + m, block(at, h), block(at, h), to(d))


def ring_gather_pass(send, land, base, block, at, to):
    for m, h, o, d in ((0, 0, 3, 1), (1, 1, 1, 3)):
        ref = block((at + o) % 4, h)
        land(base + m, ref)
        send(base + 4 + m, ref, ref, to(d))


def expert_reduce(send, land, base, src, e, sib_ref, p_ref, relay_ref, in_ref):
    sib, nxt, prv = expert_ring(e)
    to = lambda index: {"expert": index}
    wide = lambda value: value.astype(jnp.float32)
    half = (pl.ds(0, 32), pl.ds(32, 32))
    for d in (2, 1, 3, 0):
        send(base + d, src(((e + 2 * d) % 8) ^ 1), sib_ref.at[d], to(sib))
    for d in (2, 1, 3):
        land(base + d, sib_ref.at[d])
        p_ref[d - 1] = (wide(src((e + 2 * d) % 8)[...]) + wide(sib_ref[d])).astype(jnp.bfloat16)
        if d == 2:
            send(base + 4, p_ref.at[1, half[0]], relay_ref.at[0], to(nxt))
            send(base + 5, p_ref.at[1, half[1]], relay_ref.at[1], to(prv))
        if d == 1:
            send(base + 6, p_ref.at[0, half[1]], in_ref.at[0, half[1]], to(nxt))
        if d == 3:
            send(base + 7, p_ref.at[2, half[0]], in_ref.at[1, half[0]], to(prv))
    land(base + 4, relay_ref.at[0])
    p_ref[0, half[0]] = (wide(p_ref[0, half[0]]) + wide(relay_ref[0])).astype(jnp.bfloat16)
    send(base + 8, p_ref.at[0, half[0]], in_ref.at[0, half[0]], to(nxt))
    land(base + 5, relay_ref.at[1])
    p_ref[2, half[1]] = (wide(p_ref[2, half[1]]) + wide(relay_ref[1])).astype(jnp.bfloat16)
    send(base + 9, p_ref.at[2, half[1]], in_ref.at[1, half[1]], to(prv))
    land(base + 0, sib_ref.at[0])
    total = wide(src(e)[...]) + wide(sib_ref[0])
    land(base + 6, in_ref.at[0, half[1]])
    land(base + 7, in_ref.at[1, half[0]])
    land(base + 8, in_ref.at[0, half[0]])
    land(base + 9, in_ref.at[1, half[1]])
    return total + (wide(in_ref[0]) + wide(in_ref[1]))


def swap_blocks(send, land, base, out_ref, got_ref, s):
    for d in (10, 5, 6, 7, 9, 11, 13, 14, 15, 8, 2, 1, 3, 4, 12):
        to = (s + d) % 16
        send(base + d, out_ref.at[to], got_ref.at[s], {"seq": to})
    got_ref[s] = out_ref[s]
    for d in range(1, 16):
        land(base + d, got_ref.at[(s + 16 - d) % 16])


def all_partners(s, e):
    return [{"seq": (s + d) % 16} for d in range(1, 16)] + [{"expert": i} for i in expert_ring(e)]


def routing(ids_ref, gates_ref):
    r_of = lax.broadcasted_iota(jnp.int32, (16, 16), 0)
    c_of = lax.broadcasted_iota(jnp.int32, (16, 16), 1)
    across = lambda col: jnp.sum(jnp.where(r_of == c_of, col, 0.0), axis=0, keepdims=True)
    upright = lambda row: jnp.sum(jnp.where(r_of == c_of, row, 0.0), axis=1, keepdims=True)
    line = [ids_ref[k : k + 1, :].astype(jnp.float32) for k in range(TOP)]
    column = [upright(row) for row in line]
    count = lambda hit: jnp.sum(jnp.where(hit, 1.0, 0.0), axis=1, keepdims=True)
    before, upto = c_of < r_of, c_of <= r_of
    slot = [
        count((column[0] == line[0]) & before) + count((column[0] == line[1]) & before),
        count((column[1] == line[0]) & upto) + count((column[1] == line[1]) & before),
    ]
    target = [column[k] * 4.0 + slot[k] for k in range(TOP)]
    m = lax.broadcasted_iota(jnp.int32, (256, 64), 0)
    n = lax.broadcasted_iota(jnp.int32, (256, 64), 1)
    place = m // 16 * 4 + m % 4
    hit = jnp.zeros((256, 64), jnp.float32)
    for k in range(TOP):
        wide = jnp.concatenate([across(target[k])] * 4, axis=1)
        hit = hit + jnp.where((place.astype(jnp.float32) == wide) & (m // 4 % 4 == n // 16), 1.0, 0.0)
    m = lax.broadcasted_iota(jnp.int32, (64, 256), 1)
    n = lax.broadcasted_iota(jnp.int32, (64, 256), 0)
    place = m // 16 * 4 + m % 4
    weigh = jnp.zeros((64, 256), jnp.float32)
    for k in range(TOP):
        tall = jnp.concatenate([target[k]] * 4, axis=0)
        gate = jnp.concatenate([upright(gates_ref[k : k + 1, :])] * 4, axis=0)
        weigh = weigh + jnp.where((place.astype(jnp.float32) == tall) & (m // 4 % 4 == n // 16), gate, 0.0)
    top = weigh.astype(jnp.bfloat16)
    return hit.astype(jnp.bfloat16), top, (weigh - top.astype(jnp.float32)).astype(jnp.bfloat16)


def reorder(flip):
    m = lax.broadcasted_iota(jnp.int32, (256, 256), flip)
    n = lax.broadcasted_iota(jnp.int32, (256, 256), 1 - flip)
    return jnp.where(m // 4 % 4 * 64 + m // 16 * 4 + m % 4 == n, 1.0, 0.0).astype(jnp.bfloat16)


def mix_kernel(
    gated_ref, w_ref, tok_ref, gain_ref, ids_ref, gates_ref, wg_hbm, wu_hbm, wd_hbm, o_ref,
    wg_ref, wu_ref, wd_ref, act_ref, pool_ref, part_ref, sib2_ref, p2_ref, relay2_ref, in2_ref, stack_ref,
    gg_ref, t_ref, sib_ref, p_ref, relay_ref, in_ref, u_ref, v_ref, n_ref, out_ref, got_ref, back_out_ref, back_got_ref, place_ref, order_ref, back_ref, weigh_ref,
    gs, gr, es, er, ys, yr, ds, dr, xs, xr, rs, rr, bs, br, fetch_sems,
):
    fetches = [
        pltpu.make_async_copy(src.at[0], dst, fetch_sems.at[i])
        for i, (src, dst) in enumerate(((wg_hbm, wg_ref), (wu_hbm, wu_ref), (wd_hbm, wd_ref)))
    ]
    for fetch in fetches:
        fetch.start()
    s = lax.axis_index("seq")
    e = lax.axis_index("expert")
    at, along = ring_of(s, 0)
    to = lambda d: {"seq": along(d)}
    greet(all_partners(s, e))
    sent = []
    gsend, gland = mailbox((gs, gr), sent)
    esend, eland = mailbox((es, er), sent)
    ysend, yland = mailbox((ys, yr), sent)
    dsend, dland = mailbox((ds, dr), sent)
    xsend, xland = mailbox((xs, xr), sent)
    rsend, rland = mailbox((rs, rr), sent)
    bsend, bland = mailbox((bs, br), sent)
    gg_ref[at] = gated_ref[...]
    span = (pl.ds(0, 64), pl.ds(64, 64))
    block = lambda i, h: gg_ref.at[i, span[h]]
    ring_gather_open(gsend, 0, block, at, to)

    place_ref[...], weigh_ref[0], weigh_ref[1] = routing(ids_ref, gates_ref)
    back_ref[...] = reorder(0)
    order_ref[...] = reorder(1)

    def product(y):
        def tile(q, carry):
            total = jnp.dot(gg_ref[y], w_ref[q], preferred_element_type=jnp.float32)
            rows = pl.ds(pl.multiple_of(y * 16, 16), 16)
            cols = pl.ds(pl.multiple_of(q * 256, 256), 256)
            t_ref[:, rows, cols] = total.astype(jnp.bfloat16).reshape(8, 16, 256)
            return carry

        lax.fori_loop(0, 4, tile, 0)

    product(at)
    ring_gather_pass(gsend, gland, 0, block, at, to)
    gland(2, block((at + 3) % 4, 1))
    product((at + 3) % 4)
    gland(3, block((at + 1) % 4, 0))
    product((at + 1) % 4)
    gland(4, block((at + 2) % 4, 0))
    gland(5, block((at + 2) % 4, 1))
    product((at + 2) % 4)
    total = expert_reduce(
        esend, eland, 0, lambda i: t_ref.at[i], e, sib_ref, p_ref, relay_ref, in_ref
    )
    for y in range(4):
        u_ref[y] = total[y * 16 : (y + 1) * 16].astype(jnp.bfloat16)
    for d in (2, 1, 3):
        ysend(d, u_ref.at[(at + d) % 4], v_ref.at[at], to(d))
    v_ref[at] = u_ref[at]
    for d in (1, 3, 2):
        yland(d, v_ref.at[(at + 4 - d) % 4])
    mixer = jnp.concatenate(
        [v_ref[y][:, z * 256 : (z + 1) * 256] for z in range(4) for y in range(4)], axis=1
    )
    resid = (tok_ref[...].astype(jnp.float32) + mixer.astype(jnp.float32)).astype(jnp.bfloat16)
    wide = resid.astype(jnp.float32)
    scale = lax.rsqrt(jnp.mean(wide * wide, axis=-1, keepdims=True) + 1e-05)
    normed = (wide * scale * gain_ref[...]).astype(jnp.bfloat16)
    for q in range(4):
        n_ref[q * 16 : (q + 1) * 16] = normed[:, q * 1024 : (q + 1) * 1024]
    out_ref[...] = (
        jnp.dot(place_ref[...], n_ref[...], preferred_element_type=jnp.float32)
        .astype(jnp.bfloat16)
        .reshape(16, 16, 1024)
    )
    swap_blocks(dsend, dland, 0, out_ref, got_ref, s)
    rows = jnp.dot(
        order_ref[...], got_ref[...].reshape(256, 1024), preferred_element_type=jnp.float32
    ).astype(jnp.bfloat16)
    for q in range(4):
        pool_ref[e, :, q * 1024 : (q + 1) * 1024] = rows[q * 64 : (q + 1) * 64]
    sib, nxt, prv = expert_ring(e)
    far = (e + 4) % 8
    chip = lambda d: (e // 2 + d) % 4
    to_e = lambda index: {"expert": index}
    f32 = lambda value: value.astype(jnp.float32)
    half = (pl.ds(0, 32), pl.ds(32, 32))

    def rows_of(index, h):
        return pool_ref.at[index] if h is None else pool_ref.at[index, half[h]]

    def pass_on(m, index, h, target):
        ref = rows_of(index, h)
        xsend(m, ref, ref, to_e(target))

    def experts(c):
        pair = pl.ds(c * 2, 2)
        rows = pool_ref[pair].reshape(128, 4096)

        def hidden(cols):
            gate = jnp.dot(rows, wg_ref[:, cols], preferred_element_type=jnp.float32)
            upper = jnp.dot(rows, wu_ref[:, cols], preferred_element_type=jnp.float32)
            act_ref[:, cols] = (gate / (1.0 + jnp.exp(-gate)) * upper).astype(jnp.bfloat16)

        def hidden_tile(i, carry):
            hidden(pl.ds(pl.multiple_of(i * 256, 256), 256))
            return carry

        lax.fori_loop(0, 3, hidden_tile, 0)
        hidden(pl.ds(768, 128))
        act = act_ref[...]

        def down_tile(i, carry):
            cols = pl.ds(pl.multiple_of(i * 512, 512), 512)
            total = jnp.dot(act, wd_ref[:, cols], preferred_element_type=jnp.float32)
            part_ref[pair, :, cols] = total.astype(jnp.bfloat16).reshape(2, 64, 512)
            return carry

        lax.fori_loop(0, 8, down_tile, 0)

    def offer(d):
        rsend(d, part_ref.at[((e + 2 * d) % 8) ^ 1], sib2_ref.at[d], to_e(sib))

    def pair_sum(d):
        rland(d, sib2_ref.at[d])
        return f32(part_ref[(e + 2 * d) % 8]) + f32(sib2_ref[d])

    pass_on(0, e, None, nxt)
    pass_on(1, e, None, prv)
    pass_on(2, e, None, sib)
    for fetch in fetches:
        fetch.wait()
    xland(2, rows_of(sib, None))
    experts(chip(0))
    offer(0)
    xland(0, rows_of(prv, None))
    pass_on(3, prv, 0, nxt)
    pass_on(4, prv, None, sib)
    xland(1, rows_of(nxt, None))
    pass_on(5, nxt, 1, prv)
    pass_on(6, nxt, None, sib)
    xland(6, rows_of(nxt ^ 1, None))
    experts(chip(1))
    offer(1)
    xland(3, rows_of(far, 0))
    pass_on(7, far, 0, sib)
    xland(5, rows_of(far, 1))
    pass_on(8, far, 1, sib)
    p2_ref[0] = pair_sum(1).astype(jnp.bfloat16)
    rsend(6, p2_ref.at[0, half[1]], in2_ref.at[0, half[1]], to_e(nxt))
    xland(7, rows_of(far ^ 1, 0))
    xland(8, rows_of(far ^ 1, 1))
    experts(chip(2))
    offer(2)
    xland(4, rows_of(prv ^ 1, None))
    p2_ref[1] = pair_sum(2).astype(jnp.bfloat16)
    rsend(4, p2_ref.at[1, half[0]], relay2_ref.at[0], to_e(nxt))
    rsend(5, p2_ref.at[1, half[1]], relay2_ref.at[1], to_e(prv))
    experts(chip(3))
    offer(3)
    rland(4, relay2_ref.at[0])
    p2_ref[0, half[0]] = (f32(p2_ref[0, half[0]]) + f32(relay2_ref[0])).astype(jnp.bfloat16)
    rsend(8, p2_ref.at[0, half[0]], in2_ref.at[0, half[0]], to_e(nxt))
    p2_ref[2] = pair_sum(3).astype(jnp.bfloat16)
    rsend(7, p2_ref.at[2, half[0]], in2_ref.at[1, half[0]], to_e(prv))
    rland(5, relay2_ref.at[1])
    p2_ref[2, half[1]] = (f32(p2_ref[2, half[1]]) + f32(relay2_ref[1])).astype(jnp.bfloat16)
    rsend(9, p2_ref.at[2, half[1]], in2_ref.at[1, half[1]], to_e(prv))
    total = pair_sum(0)
    rland(6, in2_ref.at[0, half[1]])
    rland(7, in2_ref.at[1, half[0]])
    rland(8, in2_ref.at[0, half[0]])
    rland(9, in2_ref.at[1, half[1]])
    total = (total + (f32(in2_ref[0]) + f32(in2_ref[1]))).astype(jnp.bfloat16)
    for q in range(4):
        stack_ref[q * 64 : (q + 1) * 64] = total[:, q * 1024 : (q + 1) * 1024]
    part_back = jnp.dot(back_ref[...], stack_ref[...], preferred_element_type=jnp.float32)
    back_out_ref[...] = part_back.astype(jnp.bfloat16).reshape(16, 16, 1024)
    swap_blocks(bsend, bland, 0, back_out_ref, back_got_ref, s)
    values = back_got_ref[...].reshape(256, 1024)
    moe = jnp.dot(weigh_ref[0], values, preferred_element_type=jnp.float32) + jnp.dot(
        weigh_ref[1], values, preferred_element_type=jnp.float32
    )
    for q in range(4):
        cols = slice(q * 1024, (q + 1) * 1024)
        o_ref[:, cols] = (f32(resid[:, cols]) + moe[q * 16 : (q + 1) * 16]).astype(jnp.bfloat16)
    for copy in sent:
        copy.wait_send()


def mix(gated, weight, tokens, gain, ids, gates, w_gate, w_up, w_down, collective_id):
    dma = pltpu.SemaphoreType.DMA
    bf16 = jnp.bfloat16
    whole = pl.BlockSpec(memory_space=pltpu.VMEM)
    return pl.pallas_call(
        mix_kernel,
        out_shape=jax.ShapeDtypeStruct((16, 4096), bf16),
        in_specs=[whole] * 6 + [pl.BlockSpec(memory_space=pl.ANY)] * 3,
        out_specs=whole,
        scratch_shapes=[
            pltpu.VMEM(w_gate.shape[1:], bf16),
            pltpu.VMEM(w_up.shape[1:], bf16),
            pltpu.VMEM(w_down.shape[1:], bf16),
            pltpu.VMEM((128, w_gate.shape[2]), bf16),
            pltpu.VMEM((8, 64, 4096), bf16),
            pltpu.VMEM((8, 64, 4096), bf16),
            pltpu.VMEM((4, 64, 4096), bf16),
            pltpu.VMEM((3, 64, 4096), bf16),
            pltpu.VMEM((2, 32, 4096), bf16),
            pltpu.VMEM((2, 64, 4096), bf16),
            pltpu.VMEM((256, 1024), bf16),
            pltpu.VMEM((4, 128, 1024), bf16),
            pltpu.VMEM((8, 64, 1024), bf16),
            pltpu.VMEM((4, 64, 1024), bf16),
            pltpu.VMEM((3, 64, 1024), bf16),
            pltpu.VMEM((2, 32, 1024), bf16),
            pltpu.VMEM((2, 64, 1024), bf16),
            pltpu.VMEM((4, 16, 1024), bf16),
            pltpu.VMEM((4, 16, 1024), bf16),
            pltpu.VMEM((64, 1024), bf16),
            pltpu.VMEM((16, 16, 1024), bf16),
            pltpu.VMEM((16, 16, 1024), bf16),
            pltpu.VMEM((16, 16, 1024), bf16),
            pltpu.VMEM((16, 16, 1024), bf16),
            pltpu.VMEM((256, 64), bf16),
            pltpu.VMEM((256, 256), bf16),
            pltpu.VMEM((256, 256), bf16),
            pltpu.VMEM((2, 64, 256), bf16),
            dma((6,)), dma((6,)), dma((10,)), dma((10,)), dma((4,)), dma((4,)),
            dma((16,)), dma((16,)), dma((9,)), dma((9,)), dma((10,)), dma((10,)), dma((16,)), dma((16,)), dma((3,)),
        ],
        compiler_params=pltpu.CompilerParams(
            collective_id=collective_id, has_side_effects=True, vmem_limit_bytes=VMEM_LIMIT
        ),
    )(gated, weight, tokens, gain[None, :], ids, gates, w_gate, w_up, w_down)


def lanes_of(value, width):
    return jnp.concatenate([value] * (width // 128), axis=1)


def split_sum(value):
    top = value.astype(jnp.bfloat16)
    low = (value - top.astype(jnp.float32)).astype(jnp.bfloat16)
    width = value.shape[1]
    return jnp.concatenate(
        [jnp.broadcast_to(top.astype(jnp.float32), (8, width)), jnp.broadcast_to(low.astype(jnp.float32), (8, width))],
        axis=0,
    ).astype(jnp.bfloat16)


def read_end(ref, index):
    final = ref[index, :STATE].astype(jnp.float32)
    rows = ref[index, STATE:].astype(jnp.float32)
    return final, rows[0:1] + rows[8:9]


def scan_kernel(
    x_ref, z_ref, taps_ref, cbias_ref, xproj_ref, dtw_ref, dtb_ref, a_ref, skip_ref, w_ref,
    out_ref, g_ref,
    pad_ref, inner_ref, part_ref, rbox_ref, proj_ref, b_ref, c_ref, step_ref, u_ref, ybox_ref, zbox_ref, zmsg_ref,
    ws, wr, as_, ar, bs, br, ys, yr, zs, zr, edge_s, edge_r, local_sem,
):
    s = lax.axis_index("seq")
    e = lax.axis_index("expert")
    at_y, along_y = ring_of(s, 0)
    at_z, along_z = ring_of(s, 1)
    tokens, width = x_ref.shape
    greet(
        [{"expert": (e + d) % 8} for d in range(1, 8)]
        + [{"seq": (s + 1) % 16}, {"seq": (s + 15) % 16}]
        + [{"seq": along_y(d)} for d in (1, 2, 3)]
        + [{"seq": along_z(d)} for d in (1, 2, 3)]
    )
    sent = []
    wsend, wland = mailbox((ws, wr), sent)
    asend, aland = mailbox((as_, ar), sent)
    bsend, bland = mailbox((bs, br), sent)
    ysend, yland = mailbox((ys, yr), sent)
    zsend, zland = mailbox((zs, zr), sent)
    esend, eland = mailbox((edge_s, edge_r), sent)
    esend(0, x_ref.at[pl.ds(tokens - 8, 8)], pad_ref.at[pl.ds(0, 8)], {"seq": (s + 1) % 16})
    own = pltpu.make_async_copy(w_ref, g_ref.at[at_z], local_sem)
    own.start()
    half = w_ref.shape[0] // 2
    span = (pl.ds(0, half), pl.ds(half, half))
    block = lambda i, h: g_ref.at[i, span[h]]
    to_z = lambda d: {"seq": along_z(d)}
    own.wait()
    ring_gather_open(wsend, 0, block, at_z, to_z)
    pad_ref[8:] = x_ref[...]
    eland(0, pad_ref.at[pl.ds(0, 8)])
    pad_ref[:8] = jnp.where(s > 0, pad_ref[:8], 0.0)
    part = jnp.zeros((tokens, xproj_ref.shape[0]), jnp.float32)
    for at in range(0, width, 256):
        cols = slice(at, at + 256)
        conv = jnp.broadcast_to(cbias_ref[:, cols], (tokens, 256))
        for tap in range(CONV):
            conv = conv + taps_ref[tap : tap + 1, cols] * pad_ref[5 + tap : 5 + tap + tokens, cols]
        inner = (conv / (1.0 + jnp.exp(-conv))).astype(jnp.bfloat16)
        inner_ref[:, cols] = inner
        part = part + lax.dot_general(
            inner, xproj_ref[:, cols], (((1,), (1,)), ((), ())), preferred_element_type=jnp.float32
        )
    part_ref[...] = part.astype(jnp.bfloat16).reshape(8, tokens // 8, part.shape[1])
    for d in (4, 5, 3, 2, 6, 1, 7):
        to = (e + d) % 8
        asend(d, part_ref.at[to], rbox_ref.at[e], {"expert": to})
    rbox_ref[e] = part_ref[e]
    for d in range(1, 8):
        aland(d, rbox_ref.at[(e + 8 - d) % 8])
    proj_ref[e] = jnp.sum(rbox_ref[...].astype(jnp.float32), axis=0)
    for d in (4, 5, 3, 2, 6, 1, 7):
        bsend(d, proj_ref.at[e], proj_ref.at[e], {"expert": (e + d) % 8})
    ring_gather_pass(wsend, wland, 0, block, at_z, to_z)
    for d in range(1, 8):
        bland(d, proj_ref.at[(e + 8 - d) % 8])
    low = proj_ref[:, :, :RANK].reshape(tokens, RANK).astype(jnp.bfloat16)
    for at in range(0, width, 256):
        cols = slice(at, at + 256)
        raw = jnp.dot(low, dtw_ref[:, cols], preferred_element_type=jnp.float32) + dtb_ref[:, cols]
        step = jnp.maximum(raw, 0.0) + jnp.log1p(jnp.exp(-jnp.abs(raw)))
        step_ref[:, cols] = step
        u_ref[:, cols] = step * inner_ref[:, cols].astype(jnp.float32)
    same = lax.broadcasted_iota(jnp.int32, (1, STATE, STATE), 1) == lax.broadcasted_iota(
        jnp.int32, (1, STATE, STATE), 2
    )

    def spread(i, carry):
        rows = pl.ds(pl.multiple_of(i * 16, 16), 16)
        for ref, at in ((b_ref, RANK), (c_ref, RANK + STATE)):
            values = proj_ref[i][:, at : at + STATE]
            column = jnp.sum(jnp.where(same, values[:, None, :], 0.0), axis=-1, keepdims=True)
            ref[rows] = jnp.broadcast_to(column, (16, STATE, 128))
        return carry

    lax.fori_loop(0, 8, spread, 0)
    rate = a_ref[...]

    def advance(state, step8, u8, r, t):
        decay = jnp.exp(-(step8[r : r + 1, :] * rate))
        return decay * state + lanes_of(b_ref[t], width) * u8[r : r + 1, :]

    def first(g, state):
        base = pl.multiple_of(g * 8, 8)
        step8 = step_ref[pl.ds(base, 8), :]
        u8 = u_ref[pl.ds(base, 8), :]
        for r in range(8):
            state = advance(state, step8, u8, r, base + r)
        return state

    final = lax.fori_loop(0, tokens // 8, first, jnp.zeros_like(rate))
    ybox_ref[at_y, :STATE] = final.astype(jnp.bfloat16)
    ybox_ref[at_y, STATE:] = split_sum(jnp.sum(step_ref[...], axis=0, keepdims=True))
    for d in (2, 1, 3):
        ysend(d, ybox_ref.at[at_y], ybox_ref.at[at_y], {"seq": along_y(d)})
    for d in (1, 3, 2):
        yland(d, ybox_ref.at[(at_y + 4 - d) % 4])
    plane = jnp.zeros_like(rate)
    total = jnp.zeros((1, width), jnp.float32)
    for y in range(4):
        end, summed = read_end(ybox_ref, y)
        plane = jnp.exp(-(summed * rate)) * plane + end
        total = total + summed
    zmsg_ref[:STATE] = plane.astype(jnp.bfloat16)
    zmsg_ref[STATE:] = split_sum(total)
    for d in (2, 1, 3):
        zsend(d, zmsg_ref, zbox_ref.at[at_z], to_z(d))
    zbox_ref[at_z] = zmsg_ref[...]
    for d in (1, 3, 2):
        zland(d, zbox_ref.at[(at_z + 4 - d) % 4])
    start = jnp.zeros_like(rate)
    for ref, at in ((zbox_ref, at_z), (ybox_ref, at_y)):
        for i in range(3):
            end, summed = read_end(ref, i)
            start = jnp.where(i < at, jnp.exp(-(summed * rate)) * start + end, start)

    def second(g, state):
        base = pl.multiple_of(g * 8, 8)
        step8 = step_ref[pl.ds(base, 8), :]
        u8 = u_ref[pl.ds(base, 8), :]
        rows = []
        for r in range(8):
            state = advance(state, step8, u8, r, base + r)
            rows.append(jnp.sum(lanes_of(c_ref[base + r], width) * state, axis=0, keepdims=True))
        u_ref[pl.ds(base, 8), :] = jnp.concatenate(rows, axis=0)
        return state

    lax.fori_loop(0, tokens // 8, second, start)
    for at in range(0, width, 256):
        cols = slice(at, at + 256)
        z = z_ref[:, cols]
        out_ref[:, cols] = (
            (u_ref[:, cols] + skip_ref[:, cols] * inner_ref[:, cols].astype(jnp.float32))
            * (z / (1.0 + jnp.exp(-z)))
        ).astype(jnp.bfloat16)
    for m, h, o in ((2, 1, 3), (3, 0, 1), (4, 0, 2), (5, 1, 2)):
        wland(m, block((at_z + o) % 4, h))
    for copy in sent:
        copy.wait_send()


def scan(x, z, taps, conv_bias, xproj, dt_weight, dt_bias, rate, skip, weight, collective_id):
    dma = pltpu.SemaphoreType.DMA
    tokens, width = x.shape
    bf16, f32 = jnp.bfloat16, jnp.float32
    return pl.pallas_call(
        scan_kernel,
        out_shape=(
            jax.ShapeDtypeStruct((tokens, width), bf16),
            jax.ShapeDtypeStruct((4, *weight.shape), bf16),
        ),
        in_specs=[pl.BlockSpec(memory_space=pltpu.VMEM)] * 10,
        out_specs=[pl.BlockSpec(memory_space=pltpu.VMEM)] * 2,
        scratch_shapes=[
            pltpu.VMEM((tokens + 8, width), f32),
            pltpu.VMEM((tokens, width), bf16),
            pltpu.VMEM((8, 16, xproj.shape[1]), bf16),
            pltpu.VMEM((8, 16, xproj.shape[1]), bf16),
            pltpu.VMEM((8, 16, xproj.shape[1]), f32),
            pltpu.VMEM((tokens, STATE, 128), f32),
            pltpu.VMEM((tokens, STATE, 128), f32),
            pltpu.VMEM((tokens, width), f32),
            pltpu.VMEM((tokens, width), f32),
            pltpu.VMEM((4, 2 * STATE, width), bf16),
            pltpu.VMEM((4, 2 * STATE, width), bf16),
            pltpu.VMEM((2 * STATE, width), bf16),
            dma((6,)), dma((6,)), dma((8,)), dma((8,)), dma((8,)), dma((8,)),
            dma((4,)), dma((4,)), dma((4,)), dma((4,)), dma((1,)), dma((1,)), dma,
        ],
        compiler_params=pltpu.CompilerParams(
            collective_id=collective_id, has_side_effects=True, vmem_limit_bytes=VMEM_LIMIT
        ),
    )(
        x, z, taps, conv_bias[None, :], xproj.T, dt_weight, dt_bias[None, :], rate, skip[None, :], weight
    )


def per_device(
    tokens,
    gain_mamba,
    in_weight,
    conv_weight,
    conv_bias,
    xproj_weight,
    dt_weight,
    dt_bias,
    a_rate,
    skip_d,
    out_weight,
    gain_moe,
    expert_ids,
    gate_weights,
    w_gate,
    w_up,
    w_down,
):
    xpart, zpart = project(tokens, gain_mamba, in_weight, 3)
    gated, mixer_weight = scan(
        xpart, zpart, conv_weight, conv_bias, xproj_weight, dt_weight, dt_bias, a_rate, skip_d, out_weight, 1
    )
    return mix(
        gated, mixer_weight, tokens, gain_moe, expert_ids.T, gate_weights.T, w_gate, w_up, w_down, 4
    )


def solution(mesh):
    placed = (
        P(("seq", "expert"), None),
        P(),
        P(None, "seq", "expert"),
        P(None, "expert"),
        P("expert"),
        P("expert", None),
        P(None, "expert"),
        P("expert"),
        P(None, "expert"),
        P("expert"),
        P("expert", "seq"),
        P(),
        P(("seq", "expert"), None),
        P(("seq", "expert"), None),
        P("seq", None, "expert"),
        P("seq", None, "expert"),
        P("seq", "expert", None),
    )
    return jax.shard_map(
        per_device,
        mesh=mesh,
        in_specs=placed,
        out_specs=P(("seq", "expert"), None),
        check_vma=False,
    )
```

```python
import functools

import jax
import jax.numpy as jnp
from jax import lax
from jax.experimental import pallas as pl
from jax.experimental.pallas import tpu as pltpu
from jax.sharding import PartitionSpec as P

MESH = pl.DeviceIdType.MESH
VMEM_LIMIT = 56 * 2**20
PARTS = 2

STATE = 16
CONV = 4
RANK = 256
TOP = 2


def ring_of(axis_seq, kind):
    z, y = axis_seq // 4, axis_seq % 4
    if kind == 0:
        return y, lambda d: z * 4 + (y + d) % 4
    return z, lambda d: ((z + d) % 4) * 4 + y


def remote(src, dst, sems, index, target):
    return pltpu.make_async_remote_copy(
        src_ref=src,
        dst_ref=dst,
        send_sem=sems[0].at[index],
        recv_sem=sems[1].at[index],
        device_id=target,
        device_id_type=MESH,
    )


def greet(targets):
    barrier = pltpu.get_barrier_semaphore()
    for target in targets:
        pl.semaphore_signal(barrier, inc=1, device_id=target, device_id_type=MESH)
    pl.semaphore_wait(barrier, len(targets))


def expert_ring(e):
    return (e ^ 1, (e + 2) % 8, (e + 6) % 8)


def project_kernel(
    tok_ref, gain_ref, w_ref, x_ref, z_ref,
    n_ref, t_ref, g_ref, p_ref, relay_ref, in_ref,
    ws, wr, ts, tr, xs, xr, rs, rr, local_sems,
):
    s = lax.axis_index("seq")
    e = lax.axis_index("expert")
    at_y, along_y = ring_of(s, 0)
    at_z, along_z = ring_of(s, 1)
    sib, nxt, prv = expert_ring(e)
    gather = ((at_y, along_y), (at_z, along_z))
    reduce = ((at_z, along_z), (at_y, along_y))
    seq = lambda index: {"seq": index}
    exp = lambda index: {"expert": index}
    greet(
        [seq(along_y(d)) for d in (1, 2, 3)]
        + [seq(along_z(d)) for d in (1, 2, 3)]
        + [exp(sib), exp(nxt), exp(prv)]
    )
    half = w_ref.shape[1] // 2
    halves = (pl.ds(0, half), pl.ds(half, half))
    sent, own = [], []
    wide_cols = w_ref.shape[2] // PARTS
    cols_of = [pl.ds(c * wide_cols, wide_cols) for c in range(PARTS)]

    def open_part(c):
        for k, (at, along) in enumerate(gather):
            for m, (h, d) in enumerate(((0, 1), (1, 3), (1, 1), (0, 3))):
                copy = remote(
                    w_ref.at[k, halves[h], cols_of[c]],
                    g_ref.at[k, at, halves[h], cols_of[c]],
                    (ws, wr),
                    (k * PARTS + c) * 6 + m,
                    seq(along(d)),
                )
                copy.start()
                sent.append(copy)

    def land_part(c, k, m, o, h):
        ref = g_ref.at[k, (gather[k][0] + o) % 4, halves[h], cols_of[c]]
        remote(ref, ref, (ws, wr), (k * PARTS + c) * 6 + m, seq(gather[k][1](1))).wait_recv()
        return ref

    def pass_part(c):
        for k, (at, along) in enumerate(gather):
            for m, o, h, d in ((0, 3, 0, 1), (1, 1, 1, 3)):
                ref = land_part(c, k, m, o, h)
                copy = remote(ref, ref, (ws, wr), (k * PARTS + c) * 6 + 4 + m, seq(along(d)))
                copy.start()
                sent.append(copy)

    open_part(0)
    for k, (at, along) in enumerate(gather):
        copy = pltpu.make_async_copy(w_ref.at[k], g_ref.at[k, at], local_sems.at[k])
        copy.start()
        own.append(copy)
    wide = tok_ref[...].astype(jnp.float32)
    scale = lax.rsqrt(jnp.mean(wide * wide, axis=-1, keepdims=True) + 1e-05)
    normed = (wide * scale * gain_ref[...]).astype(jnp.bfloat16)
    for q in range(4):
        n_ref[0, q] = normed[:, q * 1024 : (q + 1) * 1024]
        for r in range(4):
            n_ref[1, q, :, r * 256 : (r + 1) * 256] = normed[:, (r * 4 + q) * 256 : (r * 4 + q + 1) * 256]
    mine = pl.ds(pl.multiple_of(e * 16, 16), 16)
    for k, (at, along) in enumerate(reduce):
        for d in (2, 1, 3):
            copy = remote(
                n_ref.at[k, (at + d) % 4], t_ref.at[k, at, mine], (ts, tr), k * 4 + d, seq(along(d))
            )
            copy.start()
            sent.append(copy)
        copy = pltpu.make_async_copy(n_ref.at[k, at], t_ref.at[k, at, mine], local_sems.at[2 + k])
        copy.start()
        own.append(copy)
    for copy in own:
        copy.wait()
    rows_of = lambda index: pl.ds(pl.multiple_of(index * 16, 16), 16)

    def pass_on(k, m, index, part, target):
        span = (slice(None), slice(0, 2), slice(2, 4))[part]
        block = t_ref.at[k, span, rows_of(index)]
        copy = remote(block, block, (xs, xr), k * 9 + m, exp(target))
        copy.start()
        sent.append(copy)

    def arrive(k, m, index, part):
        span = (slice(None), slice(0, 2), slice(2, 4))[part]
        block = t_ref.at[k, span, rows_of(index)]
        remote(block, block, (xs, xr), k * 9 + m, exp(sib)).wait_recv()

    for k, (at, along) in enumerate(reduce):
        for d in (1, 3, 2):
            remote(
                n_ref.at[k, at], t_ref.at[k, (at + 4 - d) % 4, mine], (ts, tr), k * 4 + d, seq(along(d))
            ).wait_recv()
        pass_on(k, 0, e, 0, nxt)
        pass_on(k, 1, e, 0, prv)
        pass_on(k, 2, e, 0, sib)
    pass_part(0)
    if PARTS > 1:
        open_part(1)
    far = (e + 4) % 8
    for k in range(2):
        arrive(k, 0, prv, 0)
        pass_on(k, 3, prv, 1, nxt)
        pass_on(k, 4, prv, 0, sib)
        arrive(k, 1, nxt, 0)
        pass_on(k, 5, nxt, 2, prv)
        pass_on(k, 6, nxt, 0, sib)
    for k in range(2):
        arrive(k, 3, far, 1)
        pass_on(k, 7, far, 1, sib)
        arrive(k, 5, far, 2)
        pass_on(k, 8, far, 2, sib)
    for k in range(2):
        arrive(k, 2, e ^ 1, 0)
        arrive(k, 4, prv ^ 1, 0)
        arrive(k, 6, nxt ^ 1, 0)
        arrive(k, 7, far ^ 1, 1)
        arrive(k, 8, far ^ 1, 2)
    top, low = pl.ds(0, 64), pl.ds(64, 64)
    outs = (x_ref, z_ref)

    def product(k, block, c, put):
        rows = t_ref[k, block]
        for at in range(c * wide_cols, (c + 1) * wide_cols, 256):
            cols = pl.ds(at, 256)
            total = jnp.zeros((rows.shape[0], 256), jnp.float32)
            for q in range(4):
                total = total + jnp.dot(
                    rows[:, q * 256 : (q + 1) * 256],
                    g_ref[k, q, :, cols],
                    preferred_element_type=jnp.float32,
                )
            put(cols, total)

    def push(k, c, m, src, dst, target):
        copy = remote(src, dst, (rs, rr), (k * PARTS + c) * 6 + m, seq(target))
        copy.start()
        sent.append(copy)

    def landed(k, c, m, dst):
        remote(dst, dst, (rs, rr), (k * PARTS + c) * 6 + m, seq(along_y(1))).wait_recv()

    def multiply(c):
        here = cols_of[c]
        for d in (2, 1, 3, 0):
            for k, (at, along) in enumerate(reduce):

                def put(cols, total, k=k, d=d):
                    if d:
                        p_ref[k, d - 1, :, cols] = total.astype(jnp.bfloat16)
                    else:
                        outs[k][:, cols] = total

                product(k, (at + d) % 4, c, put)
                if d == 2:
                    push(k, c, 0, p_ref.at[k, 1, top, here], relay_ref.at[k, 0, :, here], along(1))
                    push(k, c, 1, p_ref.at[k, 1, low, here], relay_ref.at[k, 1, :, here], along(3))
                if d == 1:
                    push(k, c, 2, p_ref.at[k, 0, low, here], in_ref.at[k, 0, low, here], along(1))
                if d == 3:
                    push(k, c, 3, p_ref.at[k, 2, top, here], in_ref.at[k, 1, top, here], along(3))

    def add_on_the_way(c):
        here = cols_of[c]
        for k, (at, along) in enumerate(reduce):
            for m, j, rows, side, d in ((0, 0, top, 0, 1), (1, 2, low, 1, 3)):
                landed(k, c, m, relay_ref.at[k, m, :, here])
                p_ref[k, j, rows, here] = (
                    p_ref[k, j, rows, here].astype(jnp.float32)
                    + relay_ref[k, m, :, here].astype(jnp.float32)
                ).astype(jnp.bfloat16)
                push(k, c, 4 + m, p_ref.at[k, j, rows, here], in_ref.at[k, side, rows, here], along(d))

    def close(c):
        here = cols_of[c]
        for k in range(2):
            landed(k, c, 2, in_ref.at[k, 0, low, here])
            landed(k, c, 3, in_ref.at[k, 1, top, here])
            landed(k, c, 4, in_ref.at[k, 0, top, here])
            landed(k, c, 5, in_ref.at[k, 1, low, here])
            outs[k][:, here] = outs[k][:, here] + (
                in_ref[k, 0, :, here].astype(jnp.float32) + in_ref[k, 1, :, here].astype(jnp.float32)
            )

    for c in range(PARTS):
        for k in range(2):
            for m, o, h in ((2, 3, 1), (3, 1, 0), (4, 2, 0), (5, 2, 1)):
                land_part(c, k, m, o, h)
        multiply(c)
        if c + 1 < PARTS:
            pass_part(c + 1)
        if c + 2 < PARTS:
            open_part(c + 2)
        add_on_the_way(c)
        if c:
            close(c - 1)
    close(PARTS - 1)
    for copy in sent:
        copy.wait_send()


def project(tokens, gain, weight, collective_id):
    width = weight.shape[2]
    out = jax.ShapeDtypeStruct((128, width), jnp.float32)
    dma = pltpu.SemaphoreType.DMA
    return pl.pallas_call(
        project_kernel,
        out_shape=(out, out),
        in_specs=[
            pl.BlockSpec(memory_space=pltpu.VMEM),
            pl.BlockSpec(memory_space=pltpu.VMEM),
            pl.BlockSpec(memory_space=pltpu.VMEM),
        ],
        out_specs=[pl.BlockSpec(memory_space=pltpu.VMEM)] * 2,
        scratch_shapes=[
            pltpu.VMEM((2, 4, 16, 1024), jnp.bfloat16),
            pltpu.VMEM((2, 4, 128, 1024), jnp.bfloat16),
            pltpu.VMEM((2, 4, 256, width), jnp.bfloat16),
            pltpu.VMEM((2, 3, 128, width), jnp.bfloat16),
            pltpu.VMEM((2, 2, 64, width), jnp.bfloat16),
            pltpu.VMEM((2, 2, 128, width), jnp.bfloat16),
            dma((12 * PARTS,)), dma((12 * PARTS,)), dma((8,)), dma((8,)), dma((18,)), dma((18,)),
            dma((12 * PARTS,)), dma((12 * PARTS,)),
            dma((4,)),
        ],
        compiler_params=pltpu.CompilerParams(
            collective_id=collective_id, has_side_effects=True, vmem_limit_bytes=VMEM_LIMIT
        ),
    )(tokens, gain[None, :], weight)


def mailbox(sems, sent):
    def send(i, src, dst, target):
        copy = remote(src, dst, sems, i, target)
        copy.start()
        sent.append(copy)

    def land(i, dst):
        remote(dst, dst, sems, i, {"expert": lax.axis_index("expert") ^ 1}).wait_recv()

    return send, land


def ring_gather_open(send, base, block, at, to):
    for m, (h, d) in enumerate(((0, 1), (1, 3), (1, 1), (0, 3))):
        send(base + m, block(at, h), block(at, h), to(d))


def ring_gather_pass(send, land, base, block, at, to):
    for m, h, o, d in ((0, 0, 3, 1), (1, 1, 1, 3)):
        ref = block((at + o) % 4, h)
        land(base + m, ref)
        send(base + 4 + m, ref, ref, to(d))


def expert_reduce(send, land, base, src, e, sib_ref, p_ref, relay_ref, in_ref):
    sib, nxt, prv = expert_ring(e)
    to = lambda index: {"expert": index}
    wide = lambda value: value.astype(jnp.float32)
    half = (pl.ds(0, 32), pl.ds(32, 32))
    for d in (2, 1, 3, 0):
        send(base + d, src(((e + 2 * d) % 8) ^ 1), sib_ref.at[d], to(sib))
    for d in (2, 1, 3):
        land(base + d, sib_ref.at[d])
        p_ref[d - 1] = (wide(src((e + 2 * d) % 8)[...]) + wide(sib_ref[d])).astype(jnp.bfloat16)
        if d == 2:
            send(base + 4, p_ref.at[1, half[0]], relay_ref.at[0], to(nxt))
            send(base + 5, p_ref.at[1, half[1]], relay_ref.at[1], to(prv))
        if d == 1:
            send(base + 6, p_ref.at[0, half[1]], in_ref.at[0, half[1]], to(nxt))
        if d == 3:
            send(base + 7, p_ref.at[2, half[0]], in_ref.at[1, half[0]], to(prv))
    land(base + 4, relay_ref.at[0])
    p_ref[0, half[0]] = (wide(p_ref[0, half[0]]) + wide(relay_ref[0])).astype(jnp.bfloat16)
    send(base + 8, p_ref.at[0, half[0]], in_ref.at[0, half[0]], to(nxt))
    land(base + 5, relay_ref.at[1])
    p_ref[2, half[1]] = (wide(p_ref[2, half[1]]) + wide(relay_ref[1])).astype(jnp.bfloat16)
    send(base + 9, p_ref.at[2, half[1]], in_ref.at[1, half[1]], to(prv))
    land(base + 0, sib_ref.at[0])
    total = wide(src(e)[...]) + wide(sib_ref[0])
    land(base + 6, in_ref.at[0, half[1]])
    land(base + 7, in_ref.at[1, half[0]])
    land(base + 8, in_ref.at[0, half[0]])
    land(base + 9, in_ref.at[1, half[1]])
    return total + (wide(in_ref[0]) + wide(in_ref[1]))


def swap_send(send, base, v, out_ref, got_ref, s):
    cols = pl.ds(v * 512, 512)
    for d in (10, 5, 6, 7, 9, 11, 13, 14, 15, 8, 2, 1, 3, 4, 12):
        to = (s + d) % 16
        send(base + v * 16 + d, out_ref.at[to, :, cols], got_ref.at[s, :, cols], {"seq": to})
    got_ref[s, :, cols] = out_ref[s, :, cols]


def swap_land(land, base, v, got_ref, s):
    for d in range(1, 16):
        land(base + v * 16 + d, got_ref.at[(s + 16 - d) % 16, :, pl.ds(v * 512, 512)])


def all_partners(s, e):
    return [{"seq": (s + d) % 16} for d in range(1, 16)] + [{"expert": i} for i in expert_ring(e)]


def routing(ids_ref, gates_ref):
    r_of = lax.broadcasted_iota(jnp.int32, (16, 16), 0)
    c_of = lax.broadcasted_iota(jnp.int32, (16, 16), 1)
    across = lambda col: jnp.sum(jnp.where(r_of == c_of, col, 0.0), axis=0, keepdims=True)
    upright = lambda row: jnp.sum(jnp.where(r_of == c_of, row, 0.0), axis=1, keepdims=True)
    line = [ids_ref[k : k + 1, :].astype(jnp.float32) for k in range(TOP)]
    column = [upright(row) for row in line]
    count = lambda hit: jnp.sum(jnp.where(hit, 1.0, 0.0), axis=1, keepdims=True)
    before, upto = c_of < r_of, c_of <= r_of
    slot = [
        count((column[0] == line[0]) & before) + count((column[0] == line[1]) & before),
        count((column[1] == line[0]) & upto) + count((column[1] == line[1]) & before),
    ]
    target = [column[k] * 4.0 + slot[k] for k in range(TOP)]
    m = lax.broadcasted_iota(jnp.int32, (256, 64), 0)
    n = lax.broadcasted_iota(jnp.int32, (256, 64), 1)
    place = m // 16 * 4 + m % 4
    hit = jnp.zeros((256, 64), jnp.float32)
    for k in range(TOP):
        wide = jnp.concatenate([across(target[k])] * 4, axis=1)
        hit = hit + jnp.where((place.astype(jnp.float32) == wide) & (m // 4 % 4 == n // 16), 1.0, 0.0)
    m = lax.broadcasted_iota(jnp.int32, (64, 256), 1)
    n = lax.broadcasted_iota(jnp.int32, (64, 256), 0)
    place = m // 16 * 4 + m % 4
    weigh = jnp.zeros((64, 256), jnp.float32)
    for k in range(TOP):
        tall = jnp.concatenate([target[k]] * 4, axis=0)
        gate = jnp.concatenate([upright(gates_ref[k : k + 1, :])] * 4, axis=0)
        weigh = weigh + jnp.where((place.astype(jnp.float32) == tall) & (m // 4 % 4 == n // 16), gate, 0.0)
    top = weigh.astype(jnp.bfloat16)
    return hit.astype(jnp.bfloat16), top, (weigh - top.astype(jnp.float32)).astype(jnp.bfloat16)


def reorder(flip):
    m = lax.broadcasted_iota(jnp.int32, (256, 256), flip)
    n = lax.broadcasted_iota(jnp.int32, (256, 256), 1 - flip)
    return jnp.where(m // 4 % 4 * 64 + m // 16 * 4 + m % 4 == n, 1.0, 0.0).astype(jnp.bfloat16)


def mix_kernel(
    gated_ref, w_ref, tok_ref, gain_ref, ids_ref, gates_ref, wg_hbm, wu_hbm, wd_hbm, o_ref,
    wg_ref, wu_ref, wd_ref, act_ref, pool_ref, part_ref, sib2_ref, p2_ref, relay2_ref, in2_ref, stack_ref,
    gg_ref, t_ref, sib_ref, p_ref, relay_ref, in_ref, u_ref, v_ref, n_ref, out_ref, got_ref, back_out_ref, back_got_ref, place_ref, order_ref, back_ref, weigh_ref,
    gs, gr, es, er, ys, yr, ds, dr, xs, xr, rs, rr, bs, br, fetch_sems,
):
    fetches = [
        pltpu.make_async_copy(src.at[0], dst, fetch_sems.at[i])
        for i, (src, dst) in enumerate(((wg_hbm, wg_ref), (wu_hbm, wu_ref), (wd_hbm, wd_ref)))
    ]
    for fetch in fetches:
        fetch.start()
    s = lax.axis_index("seq")
    e = lax.axis_index("expert")
    at, along = ring_of(s, 0)
    to = lambda d: {"seq": along(d)}
    greet(all_partners(s, e))
    sent = []
    gsend, gland = mailbox((gs, gr), sent)
    esend, eland = mailbox((es, er), sent)
    ysend, yland = mailbox((ys, yr), sent)
    dsend, dland = mailbox((ds, dr), sent)
    xsend, xland = mailbox((xs, xr), sent)
    rsend, rland = mailbox((rs, rr), sent)
    bsend, bland = mailbox((bs, br), sent)
    gg_ref[at] = gated_ref[...]
    span = (pl.ds(0, 64), pl.ds(64, 64))
    block = lambda i, h: gg_ref.at[i, span[h]]
    ring_gather_open(gsend, 0, block, at, to)

    place_ref[...], weigh_ref[0], weigh_ref[1] = routing(ids_ref, gates_ref)
    back_ref[...] = reorder(0)
    order_ref[...] = reorder(1)

    def product(y):
        def tile(q, carry):
            total = jnp.dot(gg_ref[y], w_ref[q], preferred_element_type=jnp.float32)
            rows = pl.ds(pl.multiple_of(y * 16, 16), 16)
            cols = pl.ds(pl.multiple_of(q * 256, 256), 256)
            t_ref[:, rows, cols] = total.astype(jnp.bfloat16).reshape(8, 16, 256)
            return carry

        lax.fori_loop(0, 4, tile, 0)

    product(at)
    ring_gather_pass(gsend, gland, 0, block, at, to)
    gland(2, block((at + 3) % 4, 1))
    product((at + 3) % 4)
    gland(3, block((at + 1) % 4, 0))
    product((at + 1) % 4)
    gland(4, block((at + 2) % 4, 0))
    gland(5, block((at + 2) % 4, 1))
    product((at + 2) % 4)
    total = expert_reduce(
        esend, eland, 0, lambda i: t_ref.at[i], e, sib_ref, p_ref, relay_ref, in_ref
    )
    for y in range(4):
        u_ref[y] = total[y * 16 : (y + 1) * 16].astype(jnp.bfloat16)
    for d in (2, 1, 3):
        ysend(d, u_ref.at[(at + d) % 4], v_ref.at[at], to(d))
    v_ref[at] = u_ref[at]
    for d in (1, 3, 2):
        yland(d, v_ref.at[(at + 4 - d) % 4])
    mixer = jnp.concatenate(
        [v_ref[y][:, z * 256 : (z + 1) * 256] for z in range(4) for y in range(4)], axis=1
    )
    resid = (tok_ref[...].astype(jnp.float32) + mixer.astype(jnp.float32)).astype(jnp.bfloat16)
    wide = resid.astype(jnp.float32)
    scale = lax.rsqrt(jnp.mean(wide * wide, axis=-1, keepdims=True) + 1e-05)
    normed = (wide * scale * gain_ref[...]).astype(jnp.bfloat16)
    for q in range(4):
        for v in range(2):
            at_col = v * 2048 + q * 512
            n_ref[q * 16 : (q + 1) * 16, v * 512 : (v + 1) * 512] = normed[:, at_col : at_col + 512]
    for v in range(2):
        cols = slice(v * 512, (v + 1) * 512)
        placed = jnp.dot(place_ref[...], n_ref[:, cols], preferred_element_type=jnp.float32)
        out_ref[:, :, cols] = placed.astype(jnp.bfloat16).reshape(16, 16, 512)
        swap_send(dsend, 0, v, out_ref, got_ref, s)
    sib, nxt, prv = expert_ring(e)
    far = (e + 4) % 8
    chip = lambda d: (e // 2 + d) % 4
    to_e = lambda index: {"expert": index}
    f32 = lambda value: value.astype(jnp.float32)
    half = (pl.ds(0, 32), pl.ds(32, 32))

    wide_cols = (pl.ds(0, 2048), pl.ds(2048, 2048))

    def rows_of(index, h, v):
        return pool_ref.at[index, slice(None) if h is None else half[h], wide_cols[v]]

    def xarrive(m, index, h, v):
        xland(v * 9 + m, rows_of(index, h, v))

    def experts(d):
        c = chip(d)
        pair = pl.ds(c * 2, 2)
        rows = pool_ref[pair].reshape(128, 4096)

        def hidden(cols):
            gate = jnp.dot(rows, wg_ref[:, cols], preferred_element_type=jnp.float32)
            upper = jnp.dot(rows, wu_ref[:, cols], preferred_element_type=jnp.float32)
            act_ref[:, cols] = (gate / (1.0 + jnp.exp(-gate)) * upper).astype(jnp.bfloat16)

        def hidden_tile(i, carry):
            hidden(pl.ds(pl.multiple_of(i * 256, 256), 256))
            return carry

        lax.fori_loop(0, 3, hidden_tile, 0)
        hidden(pl.ds(768, 128))
        act = act_ref[...]

        def down_tile(i, carry):
            cols = pl.ds(pl.multiple_of(i * 512, 512), 512)
            total = jnp.dot(act, wd_ref[:, cols], preferred_element_type=jnp.float32)
            part_ref[pair, :, cols] = total.astype(jnp.bfloat16).reshape(2, 64, 512)
            return carry

        for v in range(2):
            lax.fori_loop(v * 4, v * 4 + 4, down_tile, 0)
            offered = wide_cols[v]
            rsend(
                v * 10 + d, part_ref.at[((e + 2 * d) % 8) ^ 1, :, offered], sib2_ref.at[d, :, offered], to_e(sib)
            )

    def pair_sum(d, v):
        cols = wide_cols[v]
        rland(v * 10 + d, sib2_ref.at[d, :, cols])
        return f32(part_ref[(e + 2 * d) % 8, :, cols]) + f32(sib2_ref[d, :, cols])

    def inbox(side, h, v):
        return in2_ref.at[side, half[h], wide_cols[v]]

    def add_relay(m, j, h, v):
        cols = wide_cols[v]
        rland(v * 10 + 4 + m, relay2_ref.at[m, :, cols])
        p2_ref[j, half[h], cols] = (f32(p2_ref[j, half[h], cols]) + f32(relay2_ref[m, :, cols])).astype(jnp.bfloat16)

    for v in range(2):
        swap_land(dland, 0, v, got_ref, s)
        cols = slice(v * 512, (v + 1) * 512)
        rows = jnp.dot(
            order_ref[...], got_ref[:, :, cols].reshape(256, 512), preferred_element_type=jnp.float32
        ).astype(jnp.bfloat16)
        for q in range(4):
            at_col = v * 2048 + q * 512
            pool_ref[e, :, at_col : at_col + 512] = rows[q * 64 : (q + 1) * 64]
        for m, target in ((0, nxt), (1, prv), (2, sib)):
            ref = rows_of(e, None, v)
            xsend(v * 9 + m, ref, ref, to_e(target))
    for fetch in fetches:
        fetch.wait()
    for v in range(2):
        xarrive(2, sib, None, v)
    experts(0)
    for v in range(2):
        xarrive(0, prv, None, v)
        ref = rows_of(prv, 0, v)
        xsend(v * 9 + 3, ref, ref, to_e(nxt))
        ref = rows_of(prv, None, v)
        xsend(v * 9 + 4, ref, ref, to_e(sib))
        xarrive(1, nxt, None, v)
        ref = rows_of(nxt, 1, v)
        xsend(v * 9 + 5, ref, ref, to_e(prv))
        ref = rows_of(nxt, None, v)
        xsend(v * 9 + 6, ref, ref, to_e(sib))
    for v in range(2):
        xarrive(6, nxt ^ 1, None, v)
    experts(1)
    for v in range(2):
        xarrive(3, far, 0, v)
        ref = rows_of(far, 0, v)
        xsend(v * 9 + 7, ref, ref, to_e(sib))
        xarrive(5, far, 1, v)
        ref = rows_of(far, 1, v)
        xsend(v * 9 + 8, ref, ref, to_e(sib))
    for v in range(2):
        p2_ref[0, :, wide_cols[v]] = pair_sum(1, v).astype(jnp.bfloat16)
        rsend(v * 10 + 6, p2_ref.at[0, half[1], wide_cols[v]], inbox(0, 1, v), to_e(nxt))
    for v in range(2):
        xarrive(7, far ^ 1, 0, v)
        xarrive(8, far ^ 1, 1, v)
    experts(2)
    for v in range(2):
        cols = wide_cols[v]
        p2_ref[1, :, cols] = pair_sum(2, v).astype(jnp.bfloat16)
        rsend(v * 10 + 4, p2_ref.at[1, half[0], cols], relay2_ref.at[0, :, cols], to_e(nxt))
        rsend(v * 10 + 5, p2_ref.at[1, half[1], cols], relay2_ref.at[1, :, cols], to_e(prv))
    for v in range(2):
        xarrive(4, prv ^ 1, None, v)
    experts(3)
    for v in range(2):
        cols = wide_cols[v]
        add_relay(0, 0, 0, v)
        rsend(v * 10 + 8, p2_ref.at[0, half[0], cols], inbox(0, 0, v), to_e(nxt))
        p2_ref[2, :, cols] = pair_sum(3, v).astype(jnp.bfloat16)
        rsend(v * 10 + 7, p2_ref.at[2, half[0], cols], inbox(1, 0, v), to_e(prv))
        add_relay(1, 2, 1, v)
        rsend(v * 10 + 9, p2_ref.at[2, half[1], cols], inbox(1, 1, v), to_e(prv))
    for v in range(2):
        cols = wide_cols[v]
        total = pair_sum(0, v)
        for m, side, h in ((6, 0, 1), (7, 1, 0), (8, 0, 0), (9, 1, 1)):
            rland(v * 10 + m, inbox(side, h, v))
        total = (total + (f32(in2_ref[0, :, cols]) + f32(in2_ref[1, :, cols]))).astype(jnp.bfloat16)
        for q in range(4):
            stack_ref[q * 64 : (q + 1) * 64, v * 512 : (v + 1) * 512] = total[:, q * 512 : (q + 1) * 512]
        part_back = jnp.dot(
            back_ref[...], stack_ref[:, v * 512 : (v + 1) * 512], preferred_element_type=jnp.float32
        )
        back_out_ref[:, :, v * 512 : (v + 1) * 512] = part_back.astype(jnp.bfloat16).reshape(16, 16, 512)
        swap_send(bsend, 0, v, back_out_ref, back_got_ref, s)
    for v in range(2):
        swap_land(bland, 0, v, back_got_ref, s)
        values = back_got_ref[:, :, v * 512 : (v + 1) * 512].reshape(256, 512)
        moe = jnp.dot(weigh_ref[0], values, preferred_element_type=jnp.float32) + jnp.dot(
            weigh_ref[1], values, preferred_element_type=jnp.float32
        )
        for q in range(4):
            cols = slice(v * 2048 + q * 512, v * 2048 + (q + 1) * 512)
            o_ref[:, cols] = (f32(resid[:, cols]) + moe[q * 16 : (q + 1) * 16]).astype(jnp.bfloat16)
    for copy in sent:
        copy.wait_send()


def mix(gated, weight, tokens, gain, ids, gates, w_gate, w_up, w_down, collective_id):
    dma = pltpu.SemaphoreType.DMA
    bf16 = jnp.bfloat16
    whole = pl.BlockSpec(memory_space=pltpu.VMEM)
    return pl.pallas_call(
        mix_kernel,
        out_shape=jax.ShapeDtypeStruct((16, 4096), bf16),
        in_specs=[whole] * 6 + [pl.BlockSpec(memory_space=pl.ANY)] * 3,
        out_specs=whole,
        scratch_shapes=[
            pltpu.VMEM(w_gate.shape[1:], bf16),
            pltpu.VMEM(w_up.shape[1:], bf16),
            pltpu.VMEM(w_down.shape[1:], bf16),
            pltpu.VMEM((128, w_gate.shape[2]), bf16),
            pltpu.VMEM((8, 64, 4096), bf16),
            pltpu.VMEM((8, 64, 4096), bf16),
            pltpu.VMEM((4, 64, 4096), bf16),
            pltpu.VMEM((3, 64, 4096), bf16),
            pltpu.VMEM((2, 32, 4096), bf16),
            pltpu.VMEM((2, 64, 4096), bf16),
            pltpu.VMEM((256, 1024), bf16),
            pltpu.VMEM((4, 128, 1024), bf16),
            pltpu.VMEM((8, 64, 1024), bf16),
            pltpu.VMEM((4, 64, 1024), bf16),
            pltpu.VMEM((3, 64, 1024), bf16),
            pltpu.VMEM((2, 32, 1024), bf16),
            pltpu.VMEM((2, 64, 1024), bf16),
            pltpu.VMEM((4, 16, 1024), bf16),
            pltpu.VMEM((4, 16, 1024), bf16),
            pltpu.VMEM((64, 1024), bf16),
            pltpu.VMEM((16, 16, 1024), bf16),
            pltpu.VMEM((16, 16, 1024), bf16),
            pltpu.VMEM((16, 16, 1024), bf16),
            pltpu.VMEM((16, 16, 1024), bf16),
            pltpu.VMEM((256, 64), bf16),
            pltpu.VMEM((256, 256), bf16),
            pltpu.VMEM((256, 256), bf16),
            pltpu.VMEM((2, 64, 256), bf16),
            dma((6,)), dma((6,)), dma((10,)), dma((10,)), dma((4,)), dma((4,)),
            dma((32,)), dma((32,)), dma((18,)), dma((18,)), dma((20,)), dma((20,)), dma((32,)), dma((32,)), dma((3,)),
        ],
        compiler_params=pltpu.CompilerParams(
            collective_id=collective_id, has_side_effects=True, vmem_limit_bytes=VMEM_LIMIT
        ),
    )(gated, weight, tokens, gain[None, :], ids, gates, w_gate, w_up, w_down)


def lanes_of(value, width):
    return jnp.concatenate([value] * (width // 128), axis=1)


def split_sum(value):
    top = value.astype(jnp.bfloat16)
    low = (value - top.astype(jnp.float32)).astype(jnp.bfloat16)
    width = value.shape[1]
    return jnp.concatenate(
        [jnp.broadcast_to(top.astype(jnp.float32), (8, width)), jnp.broadcast_to(low.astype(jnp.float32), (8, width))],
        axis=0,
    ).astype(jnp.bfloat16)


def read_end(ref, index):
    final = ref[index, :STATE].astype(jnp.float32)
    rows = ref[index, STATE:].astype(jnp.float32)
    return final, rows[0:1] + rows[8:9]


def scan_kernel(
    x_ref, z_ref, taps_ref, cbias_ref, xproj_ref, dtw_ref, dtb_ref, a_ref, skip_ref, w_ref,
    out_ref, g_ref,
    pad_ref, inner_ref, part_ref, rbox_ref, proj_ref, b_ref, c_ref, step_ref, u_ref, ybox_ref, zbox_ref, zmsg_ref,
    ws, wr, as_, ar, bs, br, ys, yr, zs, zr, edge_s, edge_r, local_sem,
):
    s = lax.axis_index("seq")
    e = lax.axis_index("expert")
    at_y, along_y = ring_of(s, 0)
    at_z, along_z = ring_of(s, 1)
    tokens, width = x_ref.shape
    greet(
        [{"expert": (e + d) % 8} for d in range(1, 8)]
        + [{"seq": (s + 1) % 16}, {"seq": (s + 15) % 16}]
        + [{"seq": along_y(d)} for d in (1, 2, 3)]
        + [{"seq": along_z(d)} for d in (1, 2, 3)]
    )
    sent = []
    wsend, wland = mailbox((ws, wr), sent)
    asend, aland = mailbox((as_, ar), sent)
    bsend, bland = mailbox((bs, br), sent)
    ysend, yland = mailbox((ys, yr), sent)
    zsend, zland = mailbox((zs, zr), sent)
    esend, eland = mailbox((edge_s, edge_r), sent)
    esend(0, x_ref.at[pl.ds(tokens - 8, 8)], pad_ref.at[pl.ds(0, 8)], {"seq": (s + 1) % 16})
    own = pltpu.make_async_copy(w_ref, g_ref.at[at_z], local_sem)
    own.start()
    half = w_ref.shape[0] // 2
    span = (pl.ds(0, half), pl.ds(half, half))
    block = lambda i, h: g_ref.at[i, span[h]]
    to_z = lambda d: {"seq": along_z(d)}
    own.wait()
    ring_gather_open(wsend, 0, block, at_z, to_z)
    pad_ref[8:] = x_ref[...]
    eland(0, pad_ref.at[pl.ds(0, 8)])
    pad_ref[:8] = jnp.where(s > 0, pad_ref[:8], 0.0)
    part = jnp.zeros((tokens, xproj_ref.shape[0]), jnp.float32)
    for at in range(0, width, 256):
        cols = slice(at, at + 256)
        conv = jnp.broadcast_to(cbias_ref[:, cols], (tokens, 256))
        for tap in range(CONV):
            conv = conv + taps_ref[tap : tap + 1, cols] * pad_ref[5 + tap : 5 + tap + tokens, cols]
        inner = (conv / (1.0 + jnp.exp(-conv))).astype(jnp.bfloat16)
        inner_ref[:, cols] = inner
        part = part + lax.dot_general(
            inner, xproj_ref[:, cols], (((1,), (1,)), ((), ())), preferred_element_type=jnp.float32
        )
    part_ref[...] = part.astype(jnp.bfloat16).reshape(8, tokens // 8, part.shape[1])
    for d in (4, 5, 3, 2, 6, 1, 7):
        to = (e + d) % 8
        asend(d, part_ref.at[to], rbox_ref.at[e], {"expert": to})
    rbox_ref[e] = part_ref[e]
    for d in range(1, 8):
        aland(d, rbox_ref.at[(e + 8 - d) % 8])
    proj_ref[e] = jnp.sum(rbox_ref[...].astype(jnp.float32), axis=0)
    for d in (4, 5, 3, 2, 6, 1, 7):
        bsend(d, proj_ref.at[e], proj_ref.at[e], {"expert": (e + d) % 8})
    ring_gather_pass(wsend, wland, 0, block, at_z, to_z)
    for d in range(1, 8):
        bland(d, proj_ref.at[(e + 8 - d) % 8])
    low = proj_ref[:, :, :RANK].reshape(tokens, RANK).astype(jnp.bfloat16)
    for at in range(0, width, 256):
        cols = slice(at, at + 256)
        raw = jnp.dot(low, dtw_ref[:, cols], preferred_element_type=jnp.float32) + dtb_ref[:, cols]
        step = jnp.maximum(raw, 0.0) + jnp.log1p(jnp.exp(-jnp.abs(raw)))
        step_ref[:, cols] = step
        u_ref[:, cols] = step * inner_ref[:, cols].astype(jnp.float32)
    same = lax.broadcasted_iota(jnp.int32, (1, STATE, STATE), 1) == lax.broadcasted_iota(
        jnp.int32, (1, STATE, STATE), 2
    )

    def spread(i, carry):
        rows = pl.ds(pl.multiple_of(i * 16, 16), 16)
        for ref, at in ((b_ref, RANK), (c_ref, RANK + STATE)):
            values = proj_ref[i][:, at : at + STATE]
            column = jnp.sum(jnp.where(same, values[:, None, :], 0.0), axis=-1, keepdims=True)
            ref[rows] = jnp.broadcast_to(column, (16, STATE, 128))
        return carry

    lax.fori_loop(0, 8, spread, 0)
    rate = a_ref[...]

    def advance(state, step8, u8, r, t):
        decay = jnp.exp(-(step8[r : r + 1, :] * rate))
        return decay * state + lanes_of(b_ref[t], width) * u8[r : r + 1, :]

    def first(g, state):
        base = pl.multiple_of(g * 8, 8)
        step8 = step_ref[pl.ds(base, 8), :]
        u8 = u_ref[pl.ds(base, 8), :]
        for r in range(8):
            state = advance(state, step8, u8, r, base + r)
        return state

    final = lax.fori_loop(0, tokens // 8, first, jnp.zeros_like(rate))
    ybox_ref[at_y, :STATE] = final.astype(jnp.bfloat16)
    ybox_ref[at_y, STATE:] = split_sum(jnp.sum(step_ref[...], axis=0, keepdims=True))
    for d in (2, 1, 3):
        ysend(d, ybox_ref.at[at_y], ybox_ref.at[at_y], {"seq": along_y(d)})
    for d in (1, 3, 2):
        yland(d, ybox_ref.at[(at_y + 4 - d) % 4])
    plane = jnp.zeros_like(rate)
    total = jnp.zeros((1, width), jnp.float32)
    for y in range(4):
        end, summed = read_end(ybox_ref, y)
        plane = jnp.exp(-(summed * rate)) * plane + end
        total = total + summed
    zmsg_ref[:STATE] = plane.astype(jnp.bfloat16)
    zmsg_ref[STATE:] = split_sum(total)
    for d in (2, 1, 3):
        zsend(d, zmsg_ref, zbox_ref.at[at_z], to_z(d))
    zbox_ref[at_z] = zmsg_ref[...]
    for d in (1, 3, 2):
        zland(d, zbox_ref.at[(at_z + 4 - d) % 4])
    start = jnp.zeros_like(rate)
    for ref, at in ((zbox_ref, at_z), (ybox_ref, at_y)):
        for i in range(3):
            end, summed = read_end(ref, i)
            start = jnp.where(i < at, jnp.exp(-(summed * rate)) * start + end, start)

    def second(g, state):
        base = pl.multiple_of(g * 8, 8)
        step8 = step_ref[pl.ds(base, 8), :]
        u8 = u_ref[pl.ds(base, 8), :]
        rows = []
        for r in range(8):
            state = advance(state, step8, u8, r, base + r)
            rows.append(jnp.sum(lanes_of(c_ref[base + r], width) * state, axis=0, keepdims=True))
        u_ref[pl.ds(base, 8), :] = jnp.concatenate(rows, axis=0)
        return state

    lax.fori_loop(0, tokens // 8, second, start)
    for at in range(0, width, 256):
        cols = slice(at, at + 256)
        z = z_ref[:, cols]
        out_ref[:, cols] = (
            (u_ref[:, cols] + skip_ref[:, cols] * inner_ref[:, cols].astype(jnp.float32))
            * (z / (1.0 + jnp.exp(-z)))
        ).astype(jnp.bfloat16)
    for m, h, o in ((2, 1, 3), (3, 0, 1), (4, 0, 2), (5, 1, 2)):
        wland(m, block((at_z + o) % 4, h))
    for copy in sent:
        copy.wait_send()


def scan(x, z, taps, conv_bias, xproj, dt_weight, dt_bias, rate, skip, weight, collective_id):
    dma = pltpu.SemaphoreType.DMA
    tokens, width = x.shape
    bf16, f32 = jnp.bfloat16, jnp.float32
    return pl.pallas_call(
        scan_kernel,
        out_shape=(
            jax.ShapeDtypeStruct((tokens, width), bf16),
            jax.ShapeDtypeStruct((4, *weight.shape), bf16),
        ),
        in_specs=[pl.BlockSpec(memory_space=pltpu.VMEM)] * 10,
        out_specs=[pl.BlockSpec(memory_space=pltpu.VMEM)] * 2,
        scratch_shapes=[
            pltpu.VMEM((tokens + 8, width), f32),
            pltpu.VMEM((tokens, width), bf16),
            pltpu.VMEM((8, 16, xproj.shape[1]), bf16),
            pltpu.VMEM((8, 16, xproj.shape[1]), bf16),
            pltpu.VMEM((8, 16, xproj.shape[1]), f32),
            pltpu.VMEM((tokens, STATE, 128), f32),
            pltpu.VMEM((tokens, STATE, 128), f32),
            pltpu.VMEM((tokens, width), f32),
            pltpu.VMEM((tokens, width), f32),
            pltpu.VMEM((4, 2 * STATE, width), bf16),
            pltpu.VMEM((4, 2 * STATE, width), bf16),
            pltpu.VMEM((2 * STATE, width), bf16),
            dma((6,)), dma((6,)), dma((8,)), dma((8,)), dma((8,)), dma((8,)),
            dma((4,)), dma((4,)), dma((4,)), dma((4,)), dma((1,)), dma((1,)), dma,
        ],
        compiler_params=pltpu.CompilerParams(
            collective_id=collective_id, has_side_effects=True, vmem_limit_bytes=VMEM_LIMIT
        ),
    )(
        x, z, taps, conv_bias[None, :], xproj.T, dt_weight, dt_bias[None, :], rate, skip[None, :], weight
    )


def per_device(
    tokens,
    gain_mamba,
    in_weight,
    conv_weight,
    conv_bias,
    xproj_weight,
    dt_weight,
    dt_bias,
    a_rate,
    skip_d,
    out_weight,
    gain_moe,
    expert_ids,
    gate_weights,
    w_gate,
    w_up,
    w_down,
):
    xpart, zpart = project(tokens, gain_mamba, in_weight, 3)
    gated, mixer_weight = scan(
        xpart, zpart, conv_weight, conv_bias, xproj_weight, dt_weight, dt_bias, a_rate, skip_d, out_weight, 1
    )
    return mix(
        gated, mixer_weight, tokens, gain_moe, expert_ids.T, gate_weights.T, w_gate, w_up, w_down, 4
    )


def solution(mesh):
    placed = (
        P(("seq", "expert"), None),
        P(),
        P(None, "seq", "expert"),
        P(None, "expert"),
        P("expert"),
        P("expert", None),
        P(None, "expert"),
        P("expert"),
        P(None, "expert"),
        P("expert"),
        P("expert", "seq"),
        P(),
        P(("seq", "expert"), None),
        P(("seq", "expert"), None),
        P("seq", None, "expert"),
        P("seq", None, "expert"),
        P("seq", "expert", None),
    )
    return jax.shard_map(
        per_device,
        mesh=mesh,
        in_specs=placed,
        out_specs=P(("seq", "expert"), None),
        check_vma=False,
    )
```

```python
import functools

import jax
import jax.numpy as jnp
from jax import lax
from jax.experimental import pallas as pl
from jax.experimental.pallas import tpu as pltpu
from jax.sharding import PartitionSpec as P

MESH = pl.DeviceIdType.MESH
VMEM_LIMIT = 56 * 2**20
PARTS = 2

STATE = 16
CONV = 4
RANK = 256
TOP = 2


def ring_of(axis_seq, kind):
    z, y = axis_seq // 4, axis_seq % 4
    if kind == 0:
        return y, lambda d: z * 4 + (y + d) % 4
    return z, lambda d: ((z + d) % 4) * 4 + y


def remote(src, dst, sems, index, target):
    return pltpu.make_async_remote_copy(
        src_ref=src,
        dst_ref=dst,
        send_sem=sems[0].at[index],
        recv_sem=sems[1].at[index],
        device_id=target,
        device_id_type=MESH,
    )


def greet(targets, meanwhile=lambda: None):
    barrier = pltpu.get_barrier_semaphore()
    for target in targets:
        pl.semaphore_signal(barrier, inc=1, device_id=target, device_id_type=MESH)
    meanwhile()
    pl.semaphore_wait(barrier, len(targets))


def expert_ring(e):
    return (e ^ 1, (e + 2) % 8, (e + 6) % 8)


def project_kernel(
    tok_ref, gain_ref, w_ref, x_ref, z_ref,
    n_ref, t_ref, g_ref, p_ref, relay_ref, in_ref,
    ws, wr, ts, tr, xs, xr, rs, rr, local_sems,
):
    s = lax.axis_index("seq")
    e = lax.axis_index("expert")
    at_y, along_y = ring_of(s, 0)
    at_z, along_z = ring_of(s, 1)
    sib, nxt, prv = expert_ring(e)
    gather = ((at_y, along_y), (at_z, along_z))
    reduce = ((at_z, along_z), (at_y, along_y))
    seq = lambda index: {"seq": index}
    exp = lambda index: {"expert": index}

    def normalise():
        wide = tok_ref[...].astype(jnp.float32)
        scale = lax.rsqrt(jnp.mean(wide * wide, axis=-1, keepdims=True) + 1e-05)
        normed = (wide * scale * gain_ref[...]).astype(jnp.bfloat16)
        for q in range(4):
            n_ref[0, q] = normed[:, q * 1024 : (q + 1) * 1024]
            for r in range(4):
                n_ref[1, q, :, r * 256 : (r + 1) * 256] = normed[:, (r * 4 + q) * 256 : (r * 4 + q + 1) * 256]

    greet(
        [seq(along_y(d)) for d in (1, 2, 3)]
        + [seq(along_z(d)) for d in (1, 2, 3)]
        + [exp(sib), exp(nxt), exp(prv)],
        normalise,
    )
    half = w_ref.shape[1] // 2
    halves = (pl.ds(0, half), pl.ds(half, half))
    sent, own = [], []
    wide_cols = w_ref.shape[2] // PARTS
    cols_of = [pl.ds(c * wide_cols, wide_cols) for c in range(PARTS)]

    def open_part(c):
        for k, (at, along) in enumerate(gather):
            for m, (h, d) in enumerate(((0, 1), (1, 3), (1, 1), (0, 3))):
                copy = remote(
                    w_ref.at[k, halves[h], cols_of[c]],
                    g_ref.at[k, at, halves[h], cols_of[c]],
                    (ws, wr),
                    (k * PARTS + c) * 6 + m,
                    seq(along(d)),
                )
                copy.start()
                sent.append(copy)

    def land_part(c, k, m, o, h):
        ref = g_ref.at[k, (gather[k][0] + o) % 4, halves[h], cols_of[c]]
        remote(ref, ref, (ws, wr), (k * PARTS + c) * 6 + m, seq(gather[k][1](1))).wait_recv()
        return ref

    def pass_part(c):
        for k, (at, along) in enumerate(gather):
            for m, o, h, d in ((0, 3, 0, 1), (1, 1, 1, 3)):
                ref = land_part(c, k, m, o, h)
                copy = remote(ref, ref, (ws, wr), (k * PARTS + c) * 6 + 4 + m, seq(along(d)))
                copy.start()
                sent.append(copy)

    open_part(0)
    for k, (at, along) in enumerate(gather):
        copy = pltpu.make_async_copy(w_ref.at[k], g_ref.at[k, at], local_sems.at[k])
        copy.start()
        own.append(copy)
    mine = pl.ds(pl.multiple_of(e * 16, 16), 16)
    for k, (at, along) in enumerate(reduce):
        for d in (2, 1, 3):
            copy = remote(
                n_ref.at[k, (at + d) % 4], t_ref.at[k, at, mine], (ts, tr), k * 4 + d, seq(along(d))
            )
            copy.start()
            sent.append(copy)
        copy = pltpu.make_async_copy(n_ref.at[k, at], t_ref.at[k, at, mine], local_sems.at[2 + k])
        copy.start()
        own.append(copy)
    for copy in own:
        copy.wait()
    rows_of = lambda index: pl.ds(pl.multiple_of(index * 16, 16), 16)

    def pass_on(k, m, index, part, target):
        span = (slice(None), slice(0, 2), slice(2, 4))[part]
        block = t_ref.at[k, span, rows_of(index)]
        copy = remote(block, block, (xs, xr), k * 9 + m, exp(target))
        copy.start()
        sent.append(copy)

    def arrive(k, m, index, part):
        span = (slice(None), slice(0, 2), slice(2, 4))[part]
        block = t_ref.at[k, span, rows_of(index)]
        remote(block, block, (xs, xr), k * 9 + m, exp(sib)).wait_recv()

    for k, (at, along) in enumerate(reduce):
        for d in (1, 3, 2):
            remote(
                n_ref.at[k, at], t_ref.at[k, (at + 4 - d) % 4, mine], (ts, tr), k * 4 + d, seq(along(d))
            ).wait_recv()
        pass_on(k, 0, e, 0, nxt)
        pass_on(k, 1, e, 0, prv)
        pass_on(k, 2, e, 0, sib)
    pass_part(0)
    if PARTS > 1:
        open_part(1)
    far = (e + 4) % 8
    for k in range(2):
        arrive(k, 0, prv, 0)
        pass_on(k, 3, prv, 1, nxt)
        pass_on(k, 4, prv, 0, sib)
        arrive(k, 1, nxt, 0)
        pass_on(k, 5, nxt, 2, prv)
        pass_on(k, 6, nxt, 0, sib)
    if PARTS > 1:
        pass_part(1)
    for k in range(2):
        arrive(k, 3, far, 1)
        pass_on(k, 7, far, 1, sib)
        arrive(k, 5, far, 2)
        pass_on(k, 8, far, 2, sib)
    for k in range(2):
        arrive(k, 2, e ^ 1, 0)
        arrive(k, 4, prv ^ 1, 0)
        arrive(k, 6, nxt ^ 1, 0)
        arrive(k, 7, far ^ 1, 1)
        arrive(k, 8, far ^ 1, 2)
    top, low = pl.ds(0, 64), pl.ds(64, 64)
    outs = (x_ref, z_ref)

    def product(k, block, c, put):
        rows = t_ref[k, block]
        for at in range(c * wide_cols, (c + 1) * wide_cols, 256):
            cols = pl.ds(at, 256)
            total = jnp.zeros((rows.shape[0], 256), jnp.float32)
            for q in range(4):
                total = total + jnp.dot(
                    rows[:, q * 256 : (q + 1) * 256],
                    g_ref[k, q, :, cols],
                    preferred_element_type=jnp.float32,
                )
            put(cols, total)

    def push(k, c, m, src, dst, target):
        copy = remote(src, dst, (rs, rr), (k * PARTS + c) * 6 + m, seq(target))
        copy.start()
        sent.append(copy)

    def landed(k, c, m, dst):
        remote(dst, dst, (rs, rr), (k * PARTS + c) * 6 + m, seq(along_y(1))).wait_recv()

    def multiply(c):
        here = cols_of[c]
        for d in (2, 1, 3, 0):
            for k, (at, along) in enumerate(reduce):

                def put(cols, total, k=k, d=d):
                    if d:
                        p_ref[k, d - 1, :, cols] = total.astype(jnp.bfloat16)
                    else:
                        outs[k][:, cols] = total

                product(k, (at + d) % 4, c, put)
                if d == 2:
                    push(k, c, 0, p_ref.at[k, 1, top, here], relay_ref.at[k, 0, :, here], along(1))
                    push(k, c, 1, p_ref.at[k, 1, low, here], relay_ref.at[k, 1, :, here], along(3))
                if d == 1:
                    push(k, c, 2, p_ref.at[k, 0, low, here], in_ref.at[k, 0, low, here], along(1))
                if d == 3:
                    push(k, c, 3, p_ref.at[k, 2, top, here], in_ref.at[k, 1, top, here], along(3))

    def add_on_the_way(c):
        here = cols_of[c]
        for k, (at, along) in enumerate(reduce):
            for m, j, rows, side, d in ((0, 0, top, 0, 1), (1, 2, low, 1, 3)):
                landed(k, c, m, relay_ref.at[k, m, :, here])
                p_ref[k, j, rows, here] = (
                    p_ref[k, j, rows, here].astype(jnp.float32)
                    + relay_ref[k, m, :, here].astype(jnp.float32)
                ).astype(jnp.bfloat16)
                push(k, c, 4 + m, p_ref.at[k, j, rows, here], in_ref.at[k, side, rows, here], along(d))

    def close(c):
        here = cols_of[c]
        for k in range(2):
            landed(k, c, 2, in_ref.at[k, 0, low, here])
            landed(k, c, 3, in_ref.at[k, 1, top, here])
            landed(k, c, 4, in_ref.at[k, 0, top, here])
            landed(k, c, 5, in_ref.at[k, 1, low, here])
            outs[k][:, here] = outs[k][:, here] + (
                in_ref[k, 0, :, here].astype(jnp.float32) + in_ref[k, 1, :, here].astype(jnp.float32)
            )

    for c in range(PARTS):
        for k in range(2):
            for m, o, h in ((2, 3, 1), (3, 1, 0), (4, 2, 0), (5, 2, 1)):
                land_part(c, k, m, o, h)
        multiply(c)
        if 0 < c < PARTS - 1:
            pass_part(c + 1)
        if c + 2 < PARTS:
            open_part(c + 2)
        add_on_the_way(c)
        if c:
            close(c - 1)
    close(PARTS - 1)
    for copy in sent:
        copy.wait_send()


def project(tokens, gain, weight, collective_id):
    width = weight.shape[2]
    out = jax.ShapeDtypeStruct((128, width), jnp.float32)
    dma = pltpu.SemaphoreType.DMA
    return pl.pallas_call(
        project_kernel,
        out_shape=(out, out),
        in_specs=[
            pl.BlockSpec(memory_space=pltpu.VMEM),
            pl.BlockSpec(memory_space=pltpu.VMEM),
            pl.BlockSpec(memory_space=pltpu.VMEM),
        ],
        out_specs=[pl.BlockSpec(memory_space=pltpu.VMEM)] * 2,
        scratch_shapes=[
            pltpu.VMEM((2, 4, 16, 1024), jnp.bfloat16),
            pltpu.VMEM((2, 4, 128, 1024), jnp.bfloat16),
            pltpu.VMEM((2, 4, 256, width), jnp.bfloat16),
            pltpu.VMEM((2, 3, 128, width), jnp.bfloat16),
            pltpu.VMEM((2, 2, 64, width), jnp.bfloat16),
            pltpu.VMEM((2, 2, 128, width), jnp.bfloat16),
            dma((12 * PARTS,)), dma((12 * PARTS,)), dma((8,)), dma((8,)), dma((18,)), dma((18,)),
            dma((12 * PARTS,)), dma((12 * PARTS,)),
            dma((4,)),
        ],
        compiler_params=pltpu.CompilerParams(
            collective_id=collective_id, has_side_effects=True, vmem_limit_bytes=VMEM_LIMIT
        ),
    )(tokens, gain[None, :], weight)


def mailbox(sems, sent):
    def send(i, src, dst, target):
        copy = remote(src, dst, sems, i, target)
        copy.start()
        sent.append(copy)

    def land(i, dst):
        remote(dst, dst, sems, i, {"expert": lax.axis_index("expert") ^ 1}).wait_recv()

    return send, land


def ring_gather_open(send, base, block, at, to):
    for m, (h, d) in enumerate(((0, 1), (1, 3), (1, 1), (0, 3))):
        send(base + m, block(at, h), block(at, h), to(d))


def ring_gather_pass(send, land, base, block, at, to):
    for m, h, o, d in ((0, 0, 3, 1), (1, 1, 1, 3)):
        ref = block((at + o) % 4, h)
        land(base + m, ref)
        send(base + 4 + m, ref, ref, to(d))


def expert_reduce(send, land, base, src, e, sib_ref, p_ref, relay_ref, in_ref):
    sib, nxt, prv = expert_ring(e)
    to = lambda index: {"expert": index}
    wide = lambda value: value.astype(jnp.float32)
    half = (pl.ds(0, 32), pl.ds(32, 32))
    for d in (2, 1, 3, 0):
        send(base + d, src(((e + 2 * d) % 8) ^ 1), sib_ref.at[d], to(sib))
    for d in (2, 1, 3):
        land(base + d, sib_ref.at[d])
        p_ref[d - 1] = (wide(src((e + 2 * d) % 8)[...]) + wide(sib_ref[d])).astype(jnp.bfloat16)
        if d == 2:
            send(base + 4, p_ref.at[1, half[0]], relay_ref.at[0], to(nxt))
            send(base + 5, p_ref.at[1, half[1]], relay_ref.at[1], to(prv))
        if d == 1:
            send(base + 6, p_ref.at[0, half[1]], in_ref.at[0, half[1]], to(nxt))
        if d == 3:
            send(base + 7, p_ref.at[2, half[0]], in_ref.at[1, half[0]], to(prv))
    land(base + 4, relay_ref.at[0])
    p_ref[0, half[0]] = (wide(p_ref[0, half[0]]) + wide(relay_ref[0])).astype(jnp.bfloat16)
    send(base + 8, p_ref.at[0, half[0]], in_ref.at[0, half[0]], to(nxt))
    land(base + 5, relay_ref.at[1])
    p_ref[2, half[1]] = (wide(p_ref[2, half[1]]) + wide(relay_ref[1])).astype(jnp.bfloat16)
    send(base + 9, p_ref.at[2, half[1]], in_ref.at[1, half[1]], to(prv))
    land(base + 0, sib_ref.at[0])
    total = wide(src(e)[...]) + wide(sib_ref[0])
    land(base + 6, in_ref.at[0, half[1]])
    land(base + 7, in_ref.at[1, half[0]])
    land(base + 8, in_ref.at[0, half[0]])
    land(base + 9, in_ref.at[1, half[1]])
    return total + (wide(in_ref[0]) + wide(in_ref[1]))


def swap_send(send, base, v, out_ref, got_ref, s):
    cols = pl.ds(v * 512, 512)
    for d in (10, 5, 6, 7, 9, 11, 13, 14, 15, 8, 2, 1, 3, 4, 12):
        to = (s + d) % 16
        send(base + v * 16 + d, out_ref.at[to, :, cols], got_ref.at[s, :, cols], {"seq": to})
    got_ref[s, :, cols] = out_ref[s, :, cols]


def swap_land(land, base, v, got_ref, s):
    for d in range(1, 16):
        land(base + v * 16 + d, got_ref.at[(s + 16 - d) % 16, :, pl.ds(v * 512, 512)])


def all_partners(s, e):
    return [{"seq": (s + d) % 16} for d in range(1, 16)] + [{"expert": i} for i in expert_ring(e)]


def routing(ids_ref, gates_ref):
    r_of = lax.broadcasted_iota(jnp.int32, (16, 16), 0)
    c_of = lax.broadcasted_iota(jnp.int32, (16, 16), 1)
    across = lambda col: jnp.sum(jnp.where(r_of == c_of, col, 0.0), axis=0, keepdims=True)
    upright = lambda row: jnp.sum(jnp.where(r_of == c_of, row, 0.0), axis=1, keepdims=True)
    line = [ids_ref[k : k + 1, :].astype(jnp.float32) for k in range(TOP)]
    column = [upright(row) for row in line]
    count = lambda hit: jnp.sum(jnp.where(hit, 1.0, 0.0), axis=1, keepdims=True)
    before, upto = c_of < r_of, c_of <= r_of
    slot = [
        count((column[0] == line[0]) & before) + count((column[0] == line[1]) & before),
        count((column[1] == line[0]) & upto) + count((column[1] == line[1]) & before),
    ]
    target = [column[k] * 4.0 + slot[k] for k in range(TOP)]
    m = lax.broadcasted_iota(jnp.int32, (256, 64), 0)
    n = lax.broadcasted_iota(jnp.int32, (256, 64), 1)
    place = m // 16 * 4 + m % 4
    hit = jnp.zeros((256, 64), jnp.float32)
    for k in range(TOP):
        wide = jnp.concatenate([across(target[k])] * 4, axis=1)
        hit = hit + jnp.where((place.astype(jnp.float32) == wide) & (m // 4 % 4 == n // 16), 1.0, 0.0)
    m = lax.broadcasted_iota(jnp.int32, (64, 256), 1)
    n = lax.broadcasted_iota(jnp.int32, (64, 256), 0)
    place = m // 16 * 4 + m % 4
    weigh = jnp.zeros((64, 256), jnp.float32)
    for k in range(TOP):
        tall = jnp.concatenate([target[k]] * 4, axis=0)
        gate = jnp.concatenate([upright(gates_ref[k : k + 1, :])] * 4, axis=0)
        weigh = weigh + jnp.where((place.astype(jnp.float32) == tall) & (m // 4 % 4 == n // 16), gate, 0.0)
    top = weigh.astype(jnp.bfloat16)
    return hit.astype(jnp.bfloat16), top, (weigh - top.astype(jnp.float32)).astype(jnp.bfloat16)


def reorder(flip):
    m = lax.broadcasted_iota(jnp.int32, (256, 256), flip)
    n = lax.broadcasted_iota(jnp.int32, (256, 256), 1 - flip)
    return jnp.where(m // 4 % 4 * 64 + m // 16 * 4 + m % 4 == n, 1.0, 0.0).astype(jnp.bfloat16)


def mix_kernel(
    gated_ref, w_ref, tok_ref, gain_ref, ids_ref, gates_ref, wg_hbm, wu_hbm, wd_hbm, o_ref,
    wg_ref, wu_ref, wd_ref, act_ref, pool_ref, part_ref, sib2_ref, p2_ref, relay2_ref, in2_ref, stack_ref,
    gg_ref, t_ref, sib_ref, p_ref, relay_ref, in_ref, u_ref, v_ref, n_ref, out_ref, got_ref, back_out_ref, back_got_ref, place_ref, order_ref, back_ref, weigh_ref,
    gs, gr, es, er, ys, yr, ds, dr, xs, xr, rs, rr, bs, br, fetch_sems,
):
    fetches = [
        pltpu.make_async_copy(src.at[0], dst, fetch_sems.at[i])
        for i, (src, dst) in enumerate(((wg_hbm, wg_ref), (wu_hbm, wu_ref), (wd_hbm, wd_ref)))
    ]
    for fetch in fetches:
        fetch.start()
    s = lax.axis_index("seq")
    e = lax.axis_index("expert")
    at, along = ring_of(s, 0)
    to = lambda d: {"seq": along(d)}
    greet(all_partners(s, e))
    sent = []
    gsend, gland = mailbox((gs, gr), sent)
    esend, eland = mailbox((es, er), sent)
    ysend, yland = mailbox((ys, yr), sent)
    dsend, dland = mailbox((ds, dr), sent)
    xsend, xland = mailbox((xs, xr), sent)
    rsend, rland = mailbox((rs, rr), sent)
    bsend, bland = mailbox((bs, br), sent)
    gg_ref[at] = gated_ref[...]
    span = (pl.ds(0, 64), pl.ds(64, 64))
    block = lambda i, h: gg_ref.at[i, span[h]]
    ring_gather_open(gsend, 0, block, at, to)

    place_ref[...], weigh_ref[0], weigh_ref[1] = routing(ids_ref, gates_ref)
    back_ref[...] = reorder(0)
    order_ref[...] = reorder(1)

    def product(y):
        def tile(q, carry):
            total = jnp.dot(gg_ref[y], w_ref[q], preferred_element_type=jnp.float32)
            rows = pl.ds(pl.multiple_of(y * 16, 16), 16)
            cols = pl.ds(pl.multiple_of(q * 256, 256), 256)
            t_ref[:, rows, cols] = total.astype(jnp.bfloat16).reshape(8, 16, 256)
            return carry

        lax.fori_loop(0, 4, tile, 0)

    product(at)
    ring_gather_pass(gsend, gland, 0, block, at, to)
    gland(2, block((at + 3) % 4, 1))
    product((at + 3) % 4)
    gland(3, block((at + 1) % 4, 0))
    product((at + 1) % 4)
    gland(4, block((at + 2) % 4, 0))
    gland(5, block((at + 2) % 4, 1))
    product((at + 2) % 4)
    total = expert_reduce(
        esend, eland, 0, lambda i: t_ref.at[i], e, sib_ref, p_ref, relay_ref, in_ref
    )
    for y in range(4):
        u_ref[y] = total[y * 16 : (y + 1) * 16].astype(jnp.bfloat16)
    for d in (2, 1, 3):
        ysend(d, u_ref.at[(at + d) % 4], v_ref.at[at], to(d))
    v_ref[at] = u_ref[at]
    for d in (1, 3, 2):
        yland(d, v_ref.at[(at + 4 - d) % 4])
    mixer = jnp.concatenate(
        [v_ref[y][:, z * 256 : (z + 1) * 256] for z in range(4) for y in range(4)], axis=1
    )
    resid = (tok_ref[...].astype(jnp.float32) + mixer.astype(jnp.float32)).astype(jnp.bfloat16)
    wide = resid.astype(jnp.float32)
    scale = lax.rsqrt(jnp.mean(wide * wide, axis=-1, keepdims=True) + 1e-05)
    normed = (wide * scale * gain_ref[...]).astype(jnp.bfloat16)
    for q in range(4):
        for v in range(2):
            at_col = v * 2048 + q * 512
            n_ref[q * 16 : (q + 1) * 16, v * 512 : (v + 1) * 512] = normed[:, at_col : at_col + 512]
    for v in range(2):
        cols = slice(v * 512, (v + 1) * 512)
        placed = jnp.dot(place_ref[...], n_ref[:, cols], preferred_element_type=jnp.float32)
        out_ref[:, :, cols] = placed.astype(jnp.bfloat16).reshape(16, 16, 512)
        swap_send(dsend, 0, v, out_ref, got_ref, s)
    sib, nxt, prv = expert_ring(e)
    far = (e + 4) % 8
    chip = lambda d: (e // 2 + d) % 4
    to_e = lambda index: {"expert": index}
    f32 = lambda value: value.astype(jnp.float32)
    half = (pl.ds(0, 32), pl.ds(32, 32))

    wide_cols = (pl.ds(0, 2048), pl.ds(2048, 2048))

    def rows_of(index, h, v):
        return pool_ref.at[index, slice(None) if h is None else half[h], wide_cols[v]]

    def xarrive(m, index, h, v):
        xland(v * 9 + m, rows_of(index, h, v))

    def experts(d):
        c = chip(d)
        pair = pl.ds(c * 2, 2)
        rows = pool_ref[pair].reshape(128, 4096)

        def hidden(cols):
            gate = jnp.dot(rows, wg_ref[:, cols], preferred_element_type=jnp.float32)
            upper = jnp.dot(rows, wu_ref[:, cols], preferred_element_type=jnp.float32)
            act_ref[:, cols] = (gate / (1.0 + jnp.exp(-gate)) * upper).astype(jnp.bfloat16)

        def hidden_tile(i, carry):
            hidden(pl.ds(pl.multiple_of(i * 256, 256), 256))
            return carry

        lax.fori_loop(0, 3, hidden_tile, 0)
        hidden(pl.ds(768, 128))
        act = act_ref[...]

        def down_tile(i, carry):
            cols = pl.ds(pl.multiple_of(i * 512, 512), 512)
            total = jnp.dot(act, wd_ref[:, cols], preferred_element_type=jnp.float32)
            part_ref[pair, :, cols] = total.astype(jnp.bfloat16).reshape(2, 64, 512)
            return carry

        for v in range(2):
            lax.fori_loop(v * 4, v * 4 + 4, down_tile, 0)
            offered = wide_cols[v]
            rsend(
                v * 10 + d, part_ref.at[((e + 2 * d) % 8) ^ 1, :, offered], sib2_ref.at[d, :, offered], to_e(sib)
            )

    def pair_sum(d, v):
        cols = wide_cols[v]
        rland(v * 10 + d, sib2_ref.at[d, :, cols])
        return f32(part_ref[(e + 2 * d) % 8, :, cols]) + f32(sib2_ref[d, :, cols])

    def inbox(side, h, v):
        return in2_ref.at[side, half[h], wide_cols[v]]

    def add_relay(m, j, h, v):
        cols = wide_cols[v]
        rland(v * 10 + 4 + m, relay2_ref.at[m, :, cols])
        p2_ref[j, half[h], cols] = (f32(p2_ref[j, half[h], cols]) + f32(relay2_ref[m, :, cols])).astype(jnp.bfloat16)

    for v in range(2):
        swap_land(dland, 0, v, got_ref, s)
        cols = slice(v * 512, (v + 1) * 512)
        rows = jnp.dot(
            order_ref[...], got_ref[:, :, cols].reshape(256, 512), preferred_element_type=jnp.float32
        ).astype(jnp.bfloat16)
        for q in range(4):
            at_col = v * 2048 + q * 512
            pool_ref[e, :, at_col : at_col + 512] = rows[q * 64 : (q + 1) * 64]
        for m, target in ((0, nxt), (1, prv), (2, sib)):
            ref = rows_of(e, None, v)
            xsend(v * 9 + m, ref, ref, to_e(target))
    for fetch in fetches:
        fetch.wait()
    for v in range(2):
        xarrive(2, sib, None, v)
    experts(0)
    for v in range(2):
        xarrive(0, prv, None, v)
        ref = rows_of(prv, 0, v)
        xsend(v * 9 + 3, ref, ref, to_e(nxt))
        ref = rows_of(prv, None, v)
        xsend(v * 9 + 4, ref, ref, to_e(sib))
        xarrive(1, nxt, None, v)
        ref = rows_of(nxt, 1, v)
        xsend(v * 9 + 5, ref, ref, to_e(prv))
        ref = rows_of(nxt, None, v)
        xsend(v * 9 + 6, ref, ref, to_e(sib))
    for v in range(2):
        xarrive(6, nxt ^ 1, None, v)
    experts(1)
    for v in range(2):
        xarrive(3, far, 0, v)
        ref = rows_of(far, 0, v)
        xsend(v * 9 + 7, ref, ref, to_e(sib))
        xarrive(5, far, 1, v)
        ref = rows_of(far, 1, v)
        xsend(v * 9 + 8, ref, ref, to_e(sib))
    for v in range(2):
        p2_ref[0, :, wide_cols[v]] = pair_sum(1, v).astype(jnp.bfloat16)
        rsend(v * 10 + 6, p2_ref.at[0, half[1], wide_cols[v]], inbox(0, 1, v), to_e(nxt))
    for v in range(2):
        xarrive(7, far ^ 1, 0, v)
        xarrive(8, far ^ 1, 1, v)
    experts(2)
    for v in range(2):
        cols = wide_cols[v]
        p2_ref[1, :, cols] = pair_sum(2, v).astype(jnp.bfloat16)
        rsend(v * 10 + 4, p2_ref.at[1, half[0], cols], relay2_ref.at[0, :, cols], to_e(nxt))
        rsend(v * 10 + 5, p2_ref.at[1, half[1], cols], relay2_ref.at[1, :, cols], to_e(prv))
    for v in range(2):
        xarrive(4, prv ^ 1, None, v)
    experts(3)
    for v in range(2):
        cols = wide_cols[v]
        add_relay(0, 0, 0, v)
        rsend(v * 10 + 8, p2_ref.at[0, half[0], cols], inbox(0, 0, v), to_e(nxt))
        p2_ref[2, :, cols] = pair_sum(3, v).astype(jnp.bfloat16)
        rsend(v * 10 + 7, p2_ref.at[2, half[0], cols], inbox(1, 0, v), to_e(prv))
        add_relay(1, 2, 1, v)
        rsend(v * 10 + 9, p2_ref.at[2, half[1], cols], inbox(1, 1, v), to_e(prv))
    for v in range(2):
        cols = wide_cols[v]
        total = pair_sum(0, v)
        for m, side, h in ((6, 0, 1), (7, 1, 0), (8, 0, 0), (9, 1, 1)):
            rland(v * 10 + m, inbox(side, h, v))
        total = (total + (f32(in2_ref[0, :, cols]) + f32(in2_ref[1, :, cols]))).astype(jnp.bfloat16)
        for q in range(4):
            stack_ref[q * 64 : (q + 1) * 64, v * 512 : (v + 1) * 512] = total[:, q * 512 : (q + 1) * 512]
        part_back = jnp.dot(
            back_ref[...], stack_ref[:, v * 512 : (v + 1) * 512], preferred_element_type=jnp.float32
        )
        back_out_ref[:, :, v * 512 : (v + 1) * 512] = part_back.astype(jnp.bfloat16).reshape(16, 16, 512)
        swap_send(bsend, 0, v, back_out_ref, back_got_ref, s)
    for v in range(2):
        swap_land(bland, 0, v, back_got_ref, s)
        values = back_got_ref[:, :, v * 512 : (v + 1) * 512].reshape(256, 512)
        moe = jnp.dot(weigh_ref[0], values, preferred_element_type=jnp.float32) + jnp.dot(
            weigh_ref[1], values, preferred_element_type=jnp.float32
        )
        for q in range(4):
            cols = slice(v * 2048 + q * 512, v * 2048 + (q + 1) * 512)
            o_ref[:, cols] = (f32(resid[:, cols]) + moe[q * 16 : (q + 1) * 16]).astype(jnp.bfloat16)
    for copy in sent:
        copy.wait_send()


def mix(gated, weight, tokens, gain, ids, gates, w_gate, w_up, w_down, collective_id):
    dma = pltpu.SemaphoreType.DMA
    bf16 = jnp.bfloat16
    whole = pl.BlockSpec(memory_space=pltpu.VMEM)
    return pl.pallas_call(
        mix_kernel,
        out_shape=jax.ShapeDtypeStruct((16, 4096), bf16),
        in_specs=[whole] * 6 + [pl.BlockSpec(memory_space=pl.ANY)] * 3,
        out_specs=whole,
        scratch_shapes=[
            pltpu.VMEM(w_gate.shape[1:], bf16),
            pltpu.VMEM(w_up.shape[1:], bf16),
            pltpu.VMEM(w_down.shape[1:], bf16),
            pltpu.VMEM((128, w_gate.shape[2]), bf16),
            pltpu.VMEM((8, 64, 4096), bf16),
            pltpu.VMEM((8, 64, 4096), bf16),
            pltpu.VMEM((4, 64, 4096), bf16),
            pltpu.VMEM((3, 64, 4096), bf16),
            pltpu.VMEM((2, 32, 4096), bf16),
            pltpu.VMEM((2, 64, 4096), bf16),
            pltpu.VMEM((256, 1024), bf16),
            pltpu.VMEM((4, 128, 1024), bf16),
            pltpu.VMEM((8, 64, 1024), bf16),
            pltpu.VMEM((4, 64, 1024), bf16),
            pltpu.VMEM((3, 64, 1024), bf16),
            pltpu.VMEM((2, 32, 1024), bf16),
            pltpu.VMEM((2, 64, 1024), bf16),
            pltpu.VMEM((4, 16, 1024), bf16),
            pltpu.VMEM((4, 16, 1024), bf16),
            pltpu.VMEM((64, 1024), bf16),
            pltpu.VMEM((16, 16, 1024), bf16),
            pltpu.VMEM((16, 16, 1024), bf16),
            pltpu.VMEM((16, 16, 1024), bf16),
            pltpu.VMEM((16, 16, 1024), bf16),
            pltpu.VMEM((256, 64), bf16),
            pltpu.VMEM((256, 256), bf16),
            pltpu.VMEM((256, 256), bf16),
            pltpu.VMEM((2, 64, 256), bf16),
            dma((6,)), dma((6,)), dma((10,)), dma((10,)), dma((4,)), dma((4,)),
            dma((32,)), dma((32,)), dma((18,)), dma((18,)), dma((20,)), dma((20,)), dma((32,)), dma((32,)), dma((3,)),
        ],
        compiler_params=pltpu.CompilerParams(
            collective_id=collective_id, has_side_effects=True, vmem_limit_bytes=VMEM_LIMIT
        ),
    )(gated, weight, tokens, gain[None, :], ids, gates, w_gate, w_up, w_down)


def lanes_of(value, width):
    return jnp.concatenate([value] * (width // 128), axis=1)


def split_sum(value):
    top = value.astype(jnp.bfloat16)
    low = (value - top.astype(jnp.float32)).astype(jnp.bfloat16)
    width = value.shape[1]
    return jnp.concatenate(
        [jnp.broadcast_to(top.astype(jnp.float32), (8, width)), jnp.broadcast_to(low.astype(jnp.float32), (8, width))],
        axis=0,
    ).astype(jnp.bfloat16)


def read_end(ref, index):
    final = ref[index, :STATE].astype(jnp.float32)
    rows = ref[index, STATE:].astype(jnp.float32)
    return final, rows[0:1] + rows[8:9]


def scan_kernel(
    x_ref, z_ref, taps_ref, cbias_ref, xproj_ref, dtw_ref, dtb_ref, a_ref, skip_ref, w_ref,
    out_ref, g_ref,
    pad_ref, inner_ref, part_ref, rbox_ref, proj_ref, b_ref, c_ref, step_ref, u_ref, ybox_ref, zbox_ref, zmsg_ref,
    ws, wr, as_, ar, bs, br, ys, yr, zs, zr, edge_s, edge_r, local_sem,
):
    s = lax.axis_index("seq")
    e = lax.axis_index("expert")
    at_y, along_y = ring_of(s, 0)
    at_z, along_z = ring_of(s, 1)
    tokens, width = x_ref.shape

    def convolve(low, high):
        rows = high - low
        part = jnp.zeros((rows, xproj_ref.shape[0]), jnp.float32)
        for at in range(0, width, 256):
            cols = slice(at, at + 256)
            conv = jnp.broadcast_to(cbias_ref[:, cols], (rows, 256))
            for tap in range(CONV):
                conv = conv + taps_ref[tap : tap + 1, cols] * pad_ref[5 + tap + low : 5 + tap + high, cols]
            inner = (conv / (1.0 + jnp.exp(-conv))).astype(jnp.bfloat16)
            inner_ref[low:high, cols] = inner
            part = part + lax.dot_general(
                inner, xproj_ref[:, cols], (((1,), (1,)), ((), ())), preferred_element_type=jnp.float32
            )
        part_ref[low // 16 : high // 16] = part.astype(jnp.bfloat16).reshape(rows // 16, 16, part.shape[1])

    greet(
        [{"expert": (e + d) % 8} for d in range(1, 8)]
        + [{"seq": (s + 1) % 16}, {"seq": (s + 15) % 16}]
        + [{"seq": along_y(d)} for d in (1, 2, 3)]
        + [{"seq": along_z(d)} for d in (1, 2, 3)]
    )
    sent = []
    wsend, wland = mailbox((ws, wr), sent)
    asend, aland = mailbox((as_, ar), sent)
    bsend, bland = mailbox((bs, br), sent)
    ysend, yland = mailbox((ys, yr), sent)
    zsend, zland = mailbox((zs, zr), sent)
    esend, eland = mailbox((edge_s, edge_r), sent)
    esend(0, x_ref.at[pl.ds(tokens - 8, 8)], pad_ref.at[pl.ds(0, 8)], {"seq": (s + 1) % 16})
    own = pltpu.make_async_copy(w_ref, g_ref.at[at_z], local_sem)
    own.start()
    half = w_ref.shape[0] // 2
    span = (pl.ds(0, half), pl.ds(half, half))
    block = lambda i, h: g_ref.at[i, span[h]]
    to_z = lambda d: {"seq": along_z(d)}
    own.wait()
    ring_gather_open(wsend, 0, block, at_z, to_z)
    pad_ref[8:] = x_ref[...]
    convolve(16, tokens)
    eland(0, pad_ref.at[pl.ds(0, 8)])
    pad_ref[:8] = jnp.where(s > 0, pad_ref[:8], 0.0)
    convolve(0, 16)
    for d in (4, 5, 3, 2, 6, 1, 7):
        to = (e + d) % 8
        asend(d, part_ref.at[to], rbox_ref.at[e], {"expert": to})
    rbox_ref[e] = part_ref[e]
    for d in range(1, 8):
        aland(d, rbox_ref.at[(e + 8 - d) % 8])
    proj_ref[e] = jnp.sum(rbox_ref[...].astype(jnp.float32), axis=0)
    for d in (4, 5, 3, 2, 6, 1, 7):
        bsend(d, proj_ref.at[e], proj_ref.at[e], {"expert": (e + d) % 8})
    ring_gather_pass(wsend, wland, 0, block, at_z, to_z)
    for d in range(1, 8):
        bland(d, proj_ref.at[(e + 8 - d) % 8])
    low = proj_ref[:, :, :RANK].reshape(tokens, RANK).astype(jnp.bfloat16)
    for at in range(0, width, 256):
        cols = slice(at, at + 256)
        raw = jnp.dot(low, dtw_ref[:, cols], preferred_element_type=jnp.float32) + dtb_ref[:, cols]
        step = jnp.maximum(raw, 0.0) + jnp.log1p(jnp.exp(-jnp.abs(raw)))
        step_ref[:, cols] = step
        u_ref[:, cols] = step * inner_ref[:, cols].astype(jnp.float32)
    same = lax.broadcasted_iota(jnp.int32, (1, STATE, STATE), 1) == lax.broadcasted_iota(
        jnp.int32, (1, STATE, STATE), 2
    )

    def spread(i, carry):
        rows = pl.ds(pl.multiple_of(i * 16, 16), 16)
        for ref, at in ((b_ref, RANK), (c_ref, RANK + STATE)):
            values = proj_ref[i][:, at : at + STATE]
            column = jnp.sum(jnp.where(same, values[:, None, :], 0.0), axis=-1, keepdims=True)
            ref[rows] = jnp.broadcast_to(column, (16, STATE, 128))
        return carry

    lax.fori_loop(0, 8, spread, 0)
    rate = a_ref[...]

    def advance(state, step8, u8, r, t):
        decay = jnp.exp(-(step8[r : r + 1, :] * rate))
        return decay * state + lanes_of(b_ref[t], width) * u8[r : r + 1, :]

    def first(g, state):
        base = pl.multiple_of(g * 8, 8)
        step8 = step_ref[pl.ds(base, 8), :]
        u8 = u_ref[pl.ds(base, 8), :]
        for r in range(8):
            state = advance(state, step8, u8, r, base + r)
        return state

    final = lax.fori_loop(0, tokens // 8, first, jnp.zeros_like(rate))
    ybox_ref[at_y, :STATE] = final.astype(jnp.bfloat16)
    ybox_ref[at_y, STATE:] = split_sum(jnp.sum(step_ref[...], axis=0, keepdims=True))
    for d in (2, 1, 3):
        ysend(d, ybox_ref.at[at_y], ybox_ref.at[at_y], {"seq": along_y(d)})
    for d in (1, 3, 2):
        yland(d, ybox_ref.at[(at_y + 4 - d) % 4])
    plane = jnp.zeros_like(rate)
    total = jnp.zeros((1, width), jnp.float32)
    for y in range(4):
        end, summed = read_end(ybox_ref, y)
        plane = jnp.exp(-(summed * rate)) * plane + end
        total = total + summed
    zmsg_ref[:STATE] = plane.astype(jnp.bfloat16)
    zmsg_ref[STATE:] = split_sum(total)
    for d in (2, 1, 3):
        zsend(d, zmsg_ref, zbox_ref.at[at_z], to_z(d))
    zbox_ref[at_z] = zmsg_ref[...]
    for d in (1, 3, 2):
        zland(d, zbox_ref.at[(at_z + 4 - d) % 4])
    start = jnp.zeros_like(rate)
    for ref, at in ((zbox_ref, at_z), (ybox_ref, at_y)):
        for i in range(3):
            end, summed = read_end(ref, i)
            start = jnp.where(i < at, jnp.exp(-(summed * rate)) * start + end, start)

    def second(g, state):
        base = pl.multiple_of(g * 8, 8)
        step8 = step_ref[pl.ds(base, 8), :]
        u8 = u_ref[pl.ds(base, 8), :]
        rows = []
        for r in range(8):
            state = advance(state, step8, u8, r, base + r)
            rows.append(jnp.sum(lanes_of(c_ref[base + r], width) * state, axis=0, keepdims=True))
        u_ref[pl.ds(base, 8), :] = jnp.concatenate(rows, axis=0)
        return state

    lax.fori_loop(0, tokens // 8, second, start)
    for at in range(0, width, 256):
        cols = slice(at, at + 256)
        z = z_ref[:, cols]
        out_ref[:, cols] = (
            (u_ref[:, cols] + skip_ref[:, cols] * inner_ref[:, cols].astype(jnp.float32))
            * (z / (1.0 + jnp.exp(-z)))
        ).astype(jnp.bfloat16)
    for m, h, o in ((2, 1, 3), (3, 0, 1), (4, 0, 2), (5, 1, 2)):
        wland(m, block((at_z + o) % 4, h))
    for copy in sent:
        copy.wait_send()


def scan(x, z, taps, conv_bias, xproj, dt_weight, dt_bias, rate, skip, weight, collective_id):
    dma = pltpu.SemaphoreType.DMA
    tokens, width = x.shape
    bf16, f32 = jnp.bfloat16, jnp.float32
    return pl.pallas_call(
        scan_kernel,
        out_shape=(
            jax.ShapeDtypeStruct((tokens, width), bf16),
            jax.ShapeDtypeStruct((4, *weight.shape), bf16),
        ),
        in_specs=[pl.BlockSpec(memory_space=pltpu.VMEM)] * 10,
        out_specs=[pl.BlockSpec(memory_space=pltpu.VMEM)] * 2,
        scratch_shapes=[
            pltpu.VMEM((tokens + 8, width), f32),
            pltpu.VMEM((tokens, width), bf16),
            pltpu.VMEM((8, 16, xproj.shape[1]), bf16),
            pltpu.VMEM((8, 16, xproj.shape[1]), bf16),
            pltpu.VMEM((8, 16, xproj.shape[1]), f32),
            pltpu.VMEM((tokens, STATE, 128), f32),
            pltpu.VMEM((tokens, STATE, 128), f32),
            pltpu.VMEM((tokens, width), f32),
            pltpu.VMEM((tokens, width), f32),
            pltpu.VMEM((4, 2 * STATE, width), bf16),
            pltpu.VMEM((4, 2 * STATE, width), bf16),
            pltpu.VMEM((2 * STATE, width), bf16),
            dma((6,)), dma((6,)), dma((8,)), dma((8,)), dma((8,)), dma((8,)),
            dma((4,)), dma((4,)), dma((4,)), dma((4,)), dma((1,)), dma((1,)), dma,
        ],
        compiler_params=pltpu.CompilerParams(
            collective_id=collective_id, has_side_effects=True, vmem_limit_bytes=VMEM_LIMIT
        ),
    )(
        x, z, taps, conv_bias[None, :], xproj.T, dt_weight, dt_bias[None, :], rate, skip[None, :], weight
    )


def per_device(
    tokens,
    gain_mamba,
    in_weight,
    conv_weight,
    conv_bias,
    xproj_weight,
    dt_weight,
    dt_bias,
    a_rate,
    skip_d,
    out_weight,
    gain_moe,
    expert_ids,
    gate_weights,
    w_gate,
    w_up,
    w_down,
):
    xpart, zpart = project(tokens, gain_mamba, in_weight, 3)
    gated, mixer_weight = scan(
        xpart, zpart, conv_weight, conv_bias, xproj_weight, dt_weight, dt_bias, a_rate, skip_d, out_weight, 1
    )
    return mix(
        gated, mixer_weight, tokens, gain_moe, expert_ids.T, gate_weights.T, w_gate, w_up, w_down, 4
    )


def solution(mesh):
    placed = (
        P(("seq", "expert"), None),
        P(),
        P(None, "seq", "expert"),
        P(None, "expert"),
        P("expert"),
        P("expert", None),
        P(None, "expert"),
        P("expert"),
        P(None, "expert"),
        P("expert"),
        P("expert", "seq"),
        P(),
        P(("seq", "expert"), None),
        P(("seq", "expert"), None),
        P("seq", None, "expert"),
        P("seq", None, "expert"),
        P("seq", "expert", None),
    )
    return jax.shard_map(
        per_device,
        mesh=mesh,
        in_specs=placed,
        out_specs=P(("seq", "expert"), None),
        check_vma=False,
    )
```

```python
import functools

import jax
import jax.numpy as jnp
from jax import lax
from jax.experimental import pallas as pl
from jax.experimental.pallas import tpu as pltpu
from jax.sharding import PartitionSpec as P

MESH = pl.DeviceIdType.MESH
VMEM_LIMIT = 56 * 2**20
PARTS = 2

STATE = 16
CONV = 4
RANK = 256
TOP = 2


def ring_of(axis_seq, kind):
    z, y = axis_seq // 4, axis_seq % 4
    if kind == 0:
        return y, lambda d: z * 4 + (y + d) % 4
    return z, lambda d: ((z + d) % 4) * 4 + y


def remote(src, dst, sems, index, target):
    return pltpu.make_async_remote_copy(
        src_ref=src,
        dst_ref=dst,
        send_sem=sems[0].at[index],
        recv_sem=sems[1].at[index],
        device_id=target,
        device_id_type=MESH,
    )


def greet(targets, meanwhile=lambda: None):
    barrier = pltpu.get_barrier_semaphore()
    for target in targets:
        pl.semaphore_signal(barrier, inc=1, device_id=target, device_id_type=MESH)
    meanwhile()
    pl.semaphore_wait(barrier, len(targets))


def expert_ring(e):
    return (e ^ 1, (e + 2) % 8, (e + 6) % 8)


def project_kernel(
    tok_ref, gain_ref, w_ref, x_ref, z_ref,
    n_ref, t_ref, g_ref, p_ref, relay_ref, in_ref,
    ws, wr, ts, tr, xs, xr, rs, rr, local_sems,
):
    s = lax.axis_index("seq")
    e = lax.axis_index("expert")
    at_y, along_y = ring_of(s, 0)
    at_z, along_z = ring_of(s, 1)
    sib, nxt, prv = expert_ring(e)
    gather = ((at_y, along_y), (at_z, along_z))
    reduce = ((at_z, along_z), (at_y, along_y))
    seq = lambda index: {"seq": index}
    exp = lambda index: {"expert": index}

    def normalise():
        wide = tok_ref[...].astype(jnp.float32)
        scale = lax.rsqrt(jnp.mean(wide * wide, axis=-1, keepdims=True) + 1e-05)
        normed = (wide * scale * gain_ref[...]).astype(jnp.bfloat16)
        for q in range(4):
            n_ref[0, q] = normed[:, q * 1024 : (q + 1) * 1024]
            for r in range(4):
                n_ref[1, q, :, r * 256 : (r + 1) * 256] = normed[:, (r * 4 + q) * 256 : (r * 4 + q + 1) * 256]

    greet(
        [seq(along_y(d)) for d in (1, 2, 3)]
        + [seq(along_z(d)) for d in (1, 2, 3)]
        + [exp(sib), exp(nxt), exp(prv)],
        normalise,
    )
    half = w_ref.shape[1] // 2
    halves = (pl.ds(0, half), pl.ds(half, half))
    sent, own = [], []
    wide_cols = w_ref.shape[2] // PARTS
    cols_of = [pl.ds(c * wide_cols, wide_cols) for c in range(PARTS)]

    def open_part(c):
        for k, (at, along) in enumerate(gather):
            for m, (h, d) in enumerate(((0, 1), (1, 3), (1, 1), (0, 3))):
                copy = remote(
                    w_ref.at[k, halves[h], cols_of[c]],
                    g_ref.at[k, at, halves[h], cols_of[c]],
                    (ws, wr),
                    (k * PARTS + c) * 6 + m,
                    seq(along(d)),
                )
                copy.start()
                sent.append(copy)

    def land_part(c, k, m, o, h):
        ref = g_ref.at[k, (gather[k][0] + o) % 4, halves[h], cols_of[c]]
        remote(ref, ref, (ws, wr), (k * PARTS + c) * 6 + m, seq(gather[k][1](1))).wait_recv()
        return ref

    def pass_part(c):
        for k, (at, along) in enumerate(gather):
            for m, o, h, d in ((0, 3, 0, 1), (1, 1, 1, 3)):
                ref = land_part(c, k, m, o, h)
                copy = remote(ref, ref, (ws, wr), (k * PARTS + c) * 6 + 4 + m, seq(along(d)))
                copy.start()
                sent.append(copy)

    open_part(0)
    for k, (at, along) in enumerate(gather):
        copy = pltpu.make_async_copy(w_ref.at[k], g_ref.at[k, at], local_sems.at[k])
        copy.start()
        own.append(copy)
    mine = pl.ds(pl.multiple_of(e * 16, 16), 16)
    for k, (at, along) in enumerate(reduce):
        for d in (2, 1, 3):
            copy = remote(
                n_ref.at[k, (at + d) % 4], t_ref.at[k, at, mine], (ts, tr), k * 4 + d, seq(along(d))
            )
            copy.start()
            sent.append(copy)
        copy = pltpu.make_async_copy(n_ref.at[k, at], t_ref.at[k, at, mine], local_sems.at[2 + k])
        copy.start()
        own.append(copy)
    for copy in own:
        copy.wait()
    rows_of = lambda index: pl.ds(pl.multiple_of(index * 16, 16), 16)

    def pass_on(k, m, index, part, target):
        span = (slice(None), slice(0, 2), slice(2, 4))[part]
        block = t_ref.at[k, span, rows_of(index)]
        copy = remote(block, block, (xs, xr), k * 9 + m, exp(target))
        copy.start()
        sent.append(copy)

    def arrive(k, m, index, part):
        span = (slice(None), slice(0, 2), slice(2, 4))[part]
        block = t_ref.at[k, span, rows_of(index)]
        remote(block, block, (xs, xr), k * 9 + m, exp(sib)).wait_recv()

    for k, (at, along) in enumerate(reduce):
        for d in (1, 3, 2):
            remote(
                n_ref.at[k, at], t_ref.at[k, (at + 4 - d) % 4, mine], (ts, tr), k * 4 + d, seq(along(d))
            ).wait_recv()
        pass_on(k, 0, e, 0, nxt)
        pass_on(k, 1, e, 0, prv)
        pass_on(k, 2, e, 0, sib)
    pass_part(0)
    if PARTS > 1:
        open_part(1)
    far = (e + 4) % 8
    for k in range(2):
        arrive(k, 0, prv, 0)
        pass_on(k, 3, prv, 1, nxt)
        pass_on(k, 4, prv, 0, sib)
        arrive(k, 1, nxt, 0)
        pass_on(k, 5, nxt, 2, prv)
        pass_on(k, 6, nxt, 0, sib)
    if PARTS > 1:
        pass_part(1)
    for k in range(2):
        arrive(k, 3, far, 1)
        pass_on(k, 7, far, 1, sib)
        arrive(k, 5, far, 2)
        pass_on(k, 8, far, 2, sib)
    for k in range(2):
        arrive(k, 2, e ^ 1, 0)
        arrive(k, 4, prv ^ 1, 0)
        arrive(k, 6, nxt ^ 1, 0)
        arrive(k, 7, far ^ 1, 1)
        arrive(k, 8, far ^ 1, 2)
    top, low = pl.ds(0, 64), pl.ds(64, 64)
    outs = (x_ref, z_ref)

    def product(k, block, c, put):
        rows = t_ref[k, block]
        for at in range(c * wide_cols, (c + 1) * wide_cols, 256):
            cols = pl.ds(at, 256)
            total = jnp.zeros((rows.shape[0], 256), jnp.float32)
            for q in range(4):
                total = total + jnp.dot(
                    rows[:, q * 256 : (q + 1) * 256],
                    g_ref[k, q, :, cols],
                    preferred_element_type=jnp.float32,
                )
            put(cols, total)

    def push(k, c, m, src, dst, target):
        copy = remote(src, dst, (rs, rr), (k * PARTS + c) * 6 + m, seq(target))
        copy.start()
        sent.append(copy)

    def landed(k, c, m, dst):
        remote(dst, dst, (rs, rr), (k * PARTS + c) * 6 + m, seq(along_y(1))).wait_recv()

    def multiply(c):
        here = cols_of[c]
        for d in (2, 1, 3, 0):
            for k, (at, along) in enumerate(reduce):

                def put(cols, total, k=k, d=d):
                    if d:
                        p_ref[k, d - 1, :, cols] = total.astype(jnp.bfloat16)
                    else:
                        outs[k][:, cols] = total

                product(k, (at + d) % 4, c, put)
                if d == 2:
                    push(k, c, 0, p_ref.at[k, 1, top, here], relay_ref.at[k, 0, :, here], along(1))
                    push(k, c, 1, p_ref.at[k, 1, low, here], relay_ref.at[k, 1, :, here], along(3))
                if d == 1:
                    push(k, c, 2, p_ref.at[k, 0, low, here], in_ref.at[k, 0, low, here], along(1))
                if d == 3:
                    push(k, c, 3, p_ref.at[k, 2, top, here], in_ref.at[k, 1, top, here], along(3))

    def add_on_the_way(c):
        here = cols_of[c]
        for k, (at, along) in enumerate(reduce):
            for m, j, rows, side, d in ((0, 0, top, 0, 1), (1, 2, low, 1, 3)):
                landed(k, c, m, relay_ref.at[k, m, :, here])
                p_ref[k, j, rows, here] = (
                    p_ref[k, j, rows, here].astype(jnp.float32)
                    + relay_ref[k, m, :, here].astype(jnp.float32)
                ).astype(jnp.bfloat16)
                push(k, c, 4 + m, p_ref.at[k, j, rows, here], in_ref.at[k, side, rows, here], along(d))

    def close(c):
        here = cols_of[c]
        for k in range(2):
            landed(k, c, 2, in_ref.at[k, 0, low, here])
            landed(k, c, 3, in_ref.at[k, 1, top, here])
            landed(k, c, 4, in_ref.at[k, 0, top, here])
            landed(k, c, 5, in_ref.at[k, 1, low, here])
            outs[k][:, here] = outs[k][:, here] + (
                in_ref[k, 0, :, here].astype(jnp.float32) + in_ref[k, 1, :, here].astype(jnp.float32)
            )

    for c in range(PARTS):
        for k in range(2):
            for m, o, h in ((2, 3, 1), (3, 1, 0), (4, 2, 0), (5, 2, 1)):
                land_part(c, k, m, o, h)
        multiply(c)
        if 0 < c < PARTS - 1:
            pass_part(c + 1)
        if c + 2 < PARTS:
            open_part(c + 2)
        add_on_the_way(c)
        if c:
            close(c - 1)
    close(PARTS - 1)
    for copy in sent:
        copy.wait_send()


def project(tokens, gain, weight, collective_id):
    width = weight.shape[2]
    out = jax.ShapeDtypeStruct((128, width), jnp.float32)
    dma = pltpu.SemaphoreType.DMA
    return pl.pallas_call(
        project_kernel,
        out_shape=(out, out),
        in_specs=[
            pl.BlockSpec(memory_space=pltpu.VMEM),
            pl.BlockSpec(memory_space=pltpu.VMEM),
            pl.BlockSpec(memory_space=pltpu.VMEM),
        ],
        out_specs=[pl.BlockSpec(memory_space=pltpu.VMEM)] * 2,
        scratch_shapes=[
            pltpu.VMEM((2, 4, 16, 1024), jnp.bfloat16),
            pltpu.VMEM((2, 4, 128, 1024), jnp.bfloat16),
            pltpu.VMEM((2, 4, 256, width), jnp.bfloat16),
            pltpu.VMEM((2, 3, 128, width), jnp.bfloat16),
            pltpu.VMEM((2, 2, 64, width), jnp.bfloat16),
            pltpu.VMEM((2, 2, 128, width), jnp.bfloat16),
            dma((12 * PARTS,)), dma((12 * PARTS,)), dma((8,)), dma((8,)), dma((18,)), dma((18,)),
            dma((12 * PARTS,)), dma((12 * PARTS,)),
            dma((4,)),
        ],
        compiler_params=pltpu.CompilerParams(
            collective_id=collective_id, has_side_effects=True, vmem_limit_bytes=VMEM_LIMIT
        ),
    )(tokens, gain[None, :], weight)


def mailbox(sems, sent):
    def send(i, src, dst, target):
        copy = remote(src, dst, sems, i, target)
        copy.start()
        sent.append(copy)

    def land(i, dst):
        remote(dst, dst, sems, i, {"expert": lax.axis_index("expert") ^ 1}).wait_recv()

    return send, land


def ring_gather_open(send, base, block, at, to):
    for m, (h, d) in enumerate(((0, 1), (1, 3), (1, 1), (0, 3))):
        send(base + m, block(at, h), block(at, h), to(d))


def ring_gather_pass(send, land, base, block, at, to):
    for m, h, o, d in ((0, 0, 3, 1), (1, 1, 1, 3)):
        ref = block((at + o) % 4, h)
        land(base + m, ref)
        send(base + 4 + m, ref, ref, to(d))


def expert_reduce(send, land, base, src, e, sib_ref, p_ref, relay_ref, in_ref):
    sib, nxt, prv = expert_ring(e)
    to = lambda index: {"expert": index}
    wide = lambda value: value.astype(jnp.float32)
    half = (pl.ds(0, 32), pl.ds(32, 32))
    for d in (2, 1, 3, 0):
        send(base + d, src(((e + 2 * d) % 8) ^ 1), sib_ref.at[d], to(sib))
    for d in (2, 1, 3):
        land(base + d, sib_ref.at[d])
        p_ref[d - 1] = (wide(src((e + 2 * d) % 8)[...]) + wide(sib_ref[d])).astype(jnp.bfloat16)
        if d == 2:
            send(base + 4, p_ref.at[1, half[0]], relay_ref.at[0], to(nxt))
            send(base + 5, p_ref.at[1, half[1]], relay_ref.at[1], to(prv))
        if d == 1:
            send(base + 6, p_ref.at[0, half[1]], in_ref.at[0, half[1]], to(nxt))
        if d == 3:
            send(base + 7, p_ref.at[2, half[0]], in_ref.at[1, half[0]], to(prv))
    land(base + 4, relay_ref.at[0])
    p_ref[0, half[0]] = (wide(p_ref[0, half[0]]) + wide(relay_ref[0])).astype(jnp.bfloat16)
    send(base + 8, p_ref.at[0, half[0]], in_ref.at[0, half[0]], to(nxt))
    land(base + 5, relay_ref.at[1])
    p_ref[2, half[1]] = (wide(p_ref[2, half[1]]) + wide(relay_ref[1])).astype(jnp.bfloat16)
    send(base + 9, p_ref.at[2, half[1]], in_ref.at[1, half[1]], to(prv))
    land(base + 0, sib_ref.at[0])
    total = wide(src(e)[...]) + wide(sib_ref[0])
    land(base + 6, in_ref.at[0, half[1]])
    land(base + 7, in_ref.at[1, half[0]])
    land(base + 8, in_ref.at[0, half[0]])
    land(base + 9, in_ref.at[1, half[1]])
    return total + (wide(in_ref[0]) + wide(in_ref[1]))


def swap_send(send, base, v, out_ref, got_ref, s):
    cols = pl.ds(v * 512, 512)
    for d in (10, 5, 6, 7, 9, 11, 13, 14, 15, 8, 2, 1, 3, 4, 12):
        to = (s + d) % 16
        send(base + v * 16 + d, out_ref.at[to, :, cols], got_ref.at[s, :, cols], {"seq": to})
    got_ref[s, :, cols] = out_ref[s, :, cols]


def swap_land(land, base, v, got_ref, s):
    for d in range(1, 16):
        land(base + v * 16 + d, got_ref.at[(s + 16 - d) % 16, :, pl.ds(v * 512, 512)])


def all_partners(s, e):
    return [{"seq": (s + d) % 16} for d in range(1, 16)] + [{"expert": i} for i in expert_ring(e)]


def routing(ids_ref, gates_ref):
    r_of = lax.broadcasted_iota(jnp.int32, (16, 16), 0)
    c_of = lax.broadcasted_iota(jnp.int32, (16, 16), 1)
    across = lambda col: jnp.sum(jnp.where(r_of == c_of, col, 0.0), axis=0, keepdims=True)
    upright = lambda row: jnp.sum(jnp.where(r_of == c_of, row, 0.0), axis=1, keepdims=True)
    line = [ids_ref[k : k + 1, :].astype(jnp.float32) for k in range(TOP)]
    column = [upright(row) for row in line]
    count = lambda hit: jnp.sum(jnp.where(hit, 1.0, 0.0), axis=1, keepdims=True)
    before, upto = c_of < r_of, c_of <= r_of
    slot = [
        count((column[0] == line[0]) & before) + count((column[0] == line[1]) & before),
        count((column[1] == line[0]) & upto) + count((column[1] == line[1]) & before),
    ]
    target = [column[k] * 4.0 + slot[k] for k in range(TOP)]
    m = lax.broadcasted_iota(jnp.int32, (256, 64), 0)
    n = lax.broadcasted_iota(jnp.int32, (256, 64), 1)
    place = m // 16 * 4 + m % 4
    hit = jnp.zeros((256, 64), jnp.float32)
    for k in range(TOP):
        wide = jnp.concatenate([across(target[k])] * 4, axis=1)
        hit = hit + jnp.where((place.astype(jnp.float32) == wide) & (m // 4 % 4 == n // 16), 1.0, 0.0)
    m = lax.broadcasted_iota(jnp.int32, (64, 256), 1)
    n = lax.broadcasted_iota(jnp.int32, (64, 256), 0)
    place = m // 16 * 4 + m % 4
    weigh = jnp.zeros((64, 256), jnp.float32)
    for k in range(TOP):
        tall = jnp.concatenate([target[k]] * 4, axis=0)
        gate = jnp.concatenate([upright(gates_ref[k : k + 1, :])] * 4, axis=0)
        weigh = weigh + jnp.where((place.astype(jnp.float32) == tall) & (m // 4 % 4 == n // 16), gate, 0.0)
    top = weigh.astype(jnp.bfloat16)
    return hit.astype(jnp.bfloat16), top, (weigh - top.astype(jnp.float32)).astype(jnp.bfloat16)


def reorder(flip):
    m = lax.broadcasted_iota(jnp.int32, (256, 256), flip)
    n = lax.broadcasted_iota(jnp.int32, (256, 256), 1 - flip)
    return jnp.where(m // 4 % 4 * 64 + m // 16 * 4 + m % 4 == n, 1.0, 0.0).astype(jnp.bfloat16)


def mix_kernel(
    gated_ref, w_ref, tok_ref, gain_ref, ids_ref, gates_ref, wg_hbm, wu_hbm, wd_hbm, o_ref,
    wg_ref, wu_ref, wd_ref, act_ref, pool_ref, part_ref, sib2_ref, p2_ref, relay2_ref, in2_ref, stack_ref,
    gg_ref, t_ref, sib_ref, p_ref, relay_ref, in_ref, u_ref, v_ref, n_ref, out_ref, got_ref, back_out_ref, back_got_ref, place_ref, order_ref, back_ref, weigh_ref,
    gs, gr, es, er, ys, yr, ds, dr, xs, xr, rs, rr, bs, br, fetch_sems,
):
    fetches = [
        pltpu.make_async_copy(src.at[0], dst, fetch_sems.at[i])
        for i, (src, dst) in enumerate(((wg_hbm, wg_ref), (wu_hbm, wu_ref), (wd_hbm, wd_ref)))
    ]
    for fetch in fetches:
        fetch.start()
    s = lax.axis_index("seq")
    e = lax.axis_index("expert")
    at, along = ring_of(s, 0)
    to = lambda d: {"seq": along(d)}
    greet(all_partners(s, e))
    sent = []
    gsend, gland = mailbox((gs, gr), sent)
    esend, eland = mailbox((es, er), sent)
    ysend, yland = mailbox((ys, yr), sent)
    dsend, dland = mailbox((ds, dr), sent)
    xsend, xland = mailbox((xs, xr), sent)
    rsend, rland = mailbox((rs, rr), sent)
    bsend, bland = mailbox((bs, br), sent)
    gg_ref[at] = gated_ref[...]
    span = (pl.ds(0, 64), pl.ds(64, 64))
    block = lambda i, h: gg_ref.at[i, span[h]]
    ring_gather_open(gsend, 0, block, at, to)


    def product(y):
        def tile(q, carry):
            total = jnp.dot(gg_ref[y], w_ref[q], preferred_element_type=jnp.float32)
            rows = pl.ds(pl.multiple_of(y * 16, 16), 16)
            cols = pl.ds(pl.multiple_of(q * 256, 256), 256)
            t_ref[:, rows, cols] = total.astype(jnp.bfloat16).reshape(8, 16, 256)
            return carry

        lax.fori_loop(0, 4, tile, 0)

    ring_gather_pass(gsend, gland, 0, block, at, to)
    product(at)
    place_ref[...], weigh_ref[0], weigh_ref[1] = routing(ids_ref, gates_ref)
    back_ref[...] = reorder(0)
    order_ref[...] = reorder(1)
    gland(2, block((at + 3) % 4, 1))
    product((at + 3) % 4)
    gland(3, block((at + 1) % 4, 0))
    product((at + 1) % 4)
    gland(4, block((at + 2) % 4, 0))
    gland(5, block((at + 2) % 4, 1))
    product((at + 2) % 4)
    total = expert_reduce(
        esend, eland, 0, lambda i: t_ref.at[i], e, sib_ref, p_ref, relay_ref, in_ref
    )
    for y in range(4):
        u_ref[y] = total[y * 16 : (y + 1) * 16].astype(jnp.bfloat16)
    for d in (2, 1, 3):
        ysend(d, u_ref.at[(at + d) % 4], v_ref.at[at], to(d))
    v_ref[at] = u_ref[at]
    for d in (1, 3, 2):
        yland(d, v_ref.at[(at + 4 - d) % 4])
    mixer = jnp.concatenate(
        [v_ref[y][:, z * 256 : (z + 1) * 256] for z in range(4) for y in range(4)], axis=1
    )
    resid = (tok_ref[...].astype(jnp.float32) + mixer.astype(jnp.float32)).astype(jnp.bfloat16)
    wide = resid.astype(jnp.float32)
    scale = lax.rsqrt(jnp.mean(wide * wide, axis=-1, keepdims=True) + 1e-05)
    normed = (wide * scale * gain_ref[...]).astype(jnp.bfloat16)
    for q in range(4):
        for v in range(2):
            at_col = v * 2048 + q * 512
            n_ref[q * 16 : (q + 1) * 16, v * 512 : (v + 1) * 512] = normed[:, at_col : at_col + 512]
    for v in range(2):
        cols = slice(v * 512, (v + 1) * 512)
        placed = jnp.dot(place_ref[...], n_ref[:, cols], preferred_element_type=jnp.float32)
        out_ref[:, :, cols] = placed.astype(jnp.bfloat16).reshape(16, 16, 512)
        swap_send(dsend, 0, v, out_ref, got_ref, s)
    sib, nxt, prv = expert_ring(e)
    far = (e + 4) % 8
    chip = lambda d: (e // 2 + d) % 4
    to_e = lambda index: {"expert": index}
    f32 = lambda value: value.astype(jnp.float32)
    half = (pl.ds(0, 32), pl.ds(32, 32))

    wide_cols = (pl.ds(0, 2048), pl.ds(2048, 2048))

    def rows_of(index, h, v):
        return pool_ref.at[index, slice(None) if h is None else half[h], wide_cols[v]]

    def xarrive(m, index, h, v):
        xland(v * 9 + m, rows_of(index, h, v))

    def experts(d):
        c = chip(d)
        pair = pl.ds(c * 2, 2)
        rows = pool_ref[pair].reshape(128, 4096)

        def hidden(cols):
            gate = jnp.dot(rows, wg_ref[:, cols], preferred_element_type=jnp.float32)
            upper = jnp.dot(rows, wu_ref[:, cols], preferred_element_type=jnp.float32)
            act_ref[:, cols] = (gate / (1.0 + jnp.exp(-gate)) * upper).astype(jnp.bfloat16)

        def hidden_tile(i, carry):
            hidden(pl.ds(pl.multiple_of(i * 256, 256), 256))
            return carry

        lax.fori_loop(0, 3, hidden_tile, 0)
        hidden(pl.ds(768, 128))
        act = act_ref[...]

        def down_tile(i, carry):
            cols = pl.ds(pl.multiple_of(i * 512, 512), 512)
            total = jnp.dot(act, wd_ref[:, cols], preferred_element_type=jnp.float32)
            part_ref[pair, :, cols] = total.astype(jnp.bfloat16).reshape(2, 64, 512)
            return carry

        for v in range(2):
            lax.fori_loop(v * 4, v * 4 + 4, down_tile, 0)
            offered = wide_cols[v]
            rsend(
                v * 10 + d, part_ref.at[((e + 2 * d) % 8) ^ 1, :, offered], sib2_ref.at[d, :, offered], to_e(sib)
            )

    def pair_sum(d, v):
        cols = wide_cols[v]
        rland(v * 10 + d, sib2_ref.at[d, :, cols])
        return f32(part_ref[(e + 2 * d) % 8, :, cols]) + f32(sib2_ref[d, :, cols])

    def inbox(side, h, v):
        return in2_ref.at[side, half[h], wide_cols[v]]

    def add_relay(m, j, h, v):
        cols = wide_cols[v]
        rland(v * 10 + 4 + m, relay2_ref.at[m, :, cols])
        p2_ref[j, half[h], cols] = (f32(p2_ref[j, half[h], cols]) + f32(relay2_ref[m, :, cols])).astype(jnp.bfloat16)

    for v in range(2):
        swap_land(dland, 0, v, got_ref, s)
        cols = slice(v * 512, (v + 1) * 512)
        rows = jnp.dot(
            order_ref[...], got_ref[:, :, cols].reshape(256, 512), preferred_element_type=jnp.float32
        ).astype(jnp.bfloat16)
        for q in range(4):
            at_col = v * 2048 + q * 512
            pool_ref[e, :, at_col : at_col + 512] = rows[q * 64 : (q + 1) * 64]
        for m, target in ((0, nxt), (1, prv), (2, sib)):
            ref = rows_of(e, None, v)
            xsend(v * 9 + m, ref, ref, to_e(target))
    for fetch in fetches:
        fetch.wait()
    for v in range(2):
        xarrive(2, sib, None, v)
    experts(0)
    for v in range(2):
        xarrive(0, prv, None, v)
        ref = rows_of(prv, 0, v)
        xsend(v * 9 + 3, ref, ref, to_e(nxt))
        ref = rows_of(prv, None, v)
        xsend(v * 9 + 4, ref, ref, to_e(sib))
        xarrive(1, nxt, None, v)
        ref = rows_of(nxt, 1, v)
        xsend(v * 9 + 5, ref, ref, to_e(prv))
        ref = rows_of(nxt, None, v)
        xsend(v * 9 + 6, ref, ref, to_e(sib))
    for v in range(2):
        xarrive(6, nxt ^ 1, None, v)
    experts(1)
    for v in range(2):
        xarrive(3, far, 0, v)
        ref = rows_of(far, 0, v)
        xsend(v * 9 + 7, ref, ref, to_e(sib))
        xarrive(5, far, 1, v)
        ref = rows_of(far, 1, v)
        xsend(v * 9 + 8, ref, ref, to_e(sib))
    for v in range(2):
        p2_ref[0, :, wide_cols[v]] = pair_sum(1, v).astype(jnp.bfloat16)
        rsend(v * 10 + 6, p2_ref.at[0, half[1], wide_cols[v]], inbox(0, 1, v), to_e(nxt))
    for v in range(2):
        xarrive(7, far ^ 1, 0, v)
        xarrive(8, far ^ 1, 1, v)
    experts(2)
    for v in range(2):
        cols = wide_cols[v]
        p2_ref[1, :, cols] = pair_sum(2, v).astype(jnp.bfloat16)
        rsend(v * 10 + 4, p2_ref.at[1, half[0], cols], relay2_ref.at[0, :, cols], to_e(nxt))
        rsend(v * 10 + 5, p2_ref.at[1, half[1], cols], relay2_ref.at[1, :, cols], to_e(prv))
    for v in range(2):
        xarrive(4, prv ^ 1, None, v)
    experts(3)
    for v in range(2):
        cols = wide_cols[v]
        add_relay(0, 0, 0, v)
        rsend(v * 10 + 8, p2_ref.at[0, half[0], cols], inbox(0, 0, v), to_e(nxt))
        p2_ref[2, :, cols] = pair_sum(3, v).astype(jnp.bfloat16)
        rsend(v * 10 + 7, p2_ref.at[2, half[0], cols], inbox(1, 0, v), to_e(prv))
        add_relay(1, 2, 1, v)
        rsend(v * 10 + 9, p2_ref.at[2, half[1], cols], inbox(1, 1, v), to_e(prv))
    for v in range(2):
        cols = wide_cols[v]
        total = pair_sum(0, v)
        for m, side, h in ((6, 0, 1), (7, 1, 0), (8, 0, 0), (9, 1, 1)):
            rland(v * 10 + m, inbox(side, h, v))
        total = (total + (f32(in2_ref[0, :, cols]) + f32(in2_ref[1, :, cols]))).astype(jnp.bfloat16)
        for q in range(4):
            stack_ref[q * 64 : (q + 1) * 64, v * 512 : (v + 1) * 512] = total[:, q * 512 : (q + 1) * 512]
        part_back = jnp.dot(
            back_ref[...], stack_ref[:, v * 512 : (v + 1) * 512], preferred_element_type=jnp.float32
        )
        back_out_ref[:, :, v * 512 : (v + 1) * 512] = part_back.astype(jnp.bfloat16).reshape(16, 16, 512)
        swap_send(bsend, 0, v, back_out_ref, back_got_ref, s)
    for v in range(2):
        swap_land(bland, 0, v, back_got_ref, s)
        values = back_got_ref[:, :, v * 512 : (v + 1) * 512].reshape(256, 512)
        moe = jnp.dot(weigh_ref[0], values, preferred_element_type=jnp.float32) + jnp.dot(
            weigh_ref[1], values, preferred_element_type=jnp.float32
        )
        for q in range(4):
            cols = slice(v * 2048 + q * 512, v * 2048 + (q + 1) * 512)
            o_ref[:, cols] = (f32(resid[:, cols]) + moe[q * 16 : (q + 1) * 16]).astype(jnp.bfloat16)
    for copy in sent:
        copy.wait_send()


def mix(gated, weight, tokens, gain, ids, gates, w_gate, w_up, w_down, collective_id):
    dma = pltpu.SemaphoreType.DMA
    bf16 = jnp.bfloat16
    whole = pl.BlockSpec(memory_space=pltpu.VMEM)
    return pl.pallas_call(
        mix_kernel,
        out_shape=jax.ShapeDtypeStruct((16, 4096), bf16),
        in_specs=[whole] * 6 + [pl.BlockSpec(memory_space=pl.ANY)] * 3,
        out_specs=whole,
        scratch_shapes=[
            pltpu.VMEM(w_gate.shape[1:], bf16),
            pltpu.VMEM(w_up.shape[1:], bf16),
            pltpu.VMEM(w_down.shape[1:], bf16),
            pltpu.VMEM((128, w_gate.shape[2]), bf16),
            pltpu.VMEM((8, 64, 4096), bf16),
            pltpu.VMEM((8, 64, 4096), bf16),
            pltpu.VMEM((4, 64, 4096), bf16),
            pltpu.VMEM((3, 64, 4096), bf16),
            pltpu.VMEM((2, 32, 4096), bf16),
            pltpu.VMEM((2, 64, 4096), bf16),
            pltpu.VMEM((256, 1024), bf16),
            pltpu.VMEM((4, 128, 1024), bf16),
            pltpu.VMEM((8, 64, 1024), bf16),
            pltpu.VMEM((4, 64, 1024), bf16),
            pltpu.VMEM((3, 64, 1024), bf16),
            pltpu.VMEM((2, 32, 1024), bf16),
            pltpu.VMEM((2, 64, 1024), bf16),
            pltpu.VMEM((4, 16, 1024), bf16),
            pltpu.VMEM((4, 16, 1024), bf16),
            pltpu.VMEM((64, 1024), bf16),
            pltpu.VMEM((16, 16, 1024), bf16),
            pltpu.VMEM((16, 16, 1024), bf16),
            pltpu.VMEM((16, 16, 1024), bf16),
            pltpu.VMEM((16, 16, 1024), bf16),
            pltpu.VMEM((256, 64), bf16),
            pltpu.VMEM((256, 256), bf16),
            pltpu.VMEM((256, 256), bf16),
            pltpu.VMEM((2, 64, 256), bf16),
            dma((6,)), dma((6,)), dma((10,)), dma((10,)), dma((4,)), dma((4,)),
            dma((32,)), dma((32,)), dma((18,)), dma((18,)), dma((20,)), dma((20,)), dma((32,)), dma((32,)), dma((3,)),
        ],
        compiler_params=pltpu.CompilerParams(
            collective_id=collective_id, has_side_effects=True, vmem_limit_bytes=VMEM_LIMIT
        ),
    )(gated, weight, tokens, gain[None, :], ids, gates, w_gate, w_up, w_down)


def lanes_of(value, width):
    return jnp.concatenate([value] * (width // 128), axis=1)


def split_sum(value):
    top = value.astype(jnp.bfloat16)
    low = (value - top.astype(jnp.float32)).astype(jnp.bfloat16)
    width = value.shape[1]
    return jnp.concatenate(
        [jnp.broadcast_to(top.astype(jnp.float32), (8, width)), jnp.broadcast_to(low.astype(jnp.float32), (8, width))],
        axis=0,
    ).astype(jnp.bfloat16)


def read_end(ref, index):
    final = ref[index, :STATE].astype(jnp.float32)
    rows = ref[index, STATE:].astype(jnp.float32)
    return final, rows[0:1] + rows[8:9]


def scan_kernel(
    x_ref, z_ref, taps_ref, cbias_ref, xproj_ref, dtw_ref, dtb_ref, a_ref, skip_ref, w_ref,
    out_ref, g_ref,
    pad_ref, inner_ref, part_ref, rbox_ref, proj_ref, b_ref, c_ref, step_ref, u_ref, ybox_ref, zbox_ref, zmsg_ref,
    ws, wr, as_, ar, bs, br, ys, yr, zs, zr, edge_s, edge_r, local_sem,
):
    s = lax.axis_index("seq")
    e = lax.axis_index("expert")
    at_y, along_y = ring_of(s, 0)
    at_z, along_z = ring_of(s, 1)
    tokens, width = x_ref.shape

    def convolve(low, high):
        rows = high - low
        part = jnp.zeros((rows, xproj_ref.shape[0]), jnp.float32)
        for at in range(0, width, 256):
            cols = slice(at, at + 256)
            conv = jnp.broadcast_to(cbias_ref[:, cols], (rows, 256))
            for tap in range(CONV):
                conv = conv + taps_ref[tap : tap + 1, cols] * pad_ref[5 + tap + low : 5 + tap + high, cols]
            inner = (conv / (1.0 + jnp.exp(-conv))).astype(jnp.bfloat16)
            inner_ref[low:high, cols] = inner
            part = part + lax.dot_general(
                inner, xproj_ref[:, cols], (((1,), (1,)), ((), ())), preferred_element_type=jnp.float32
            )
        part_ref[low // 16 : high // 16] = part.astype(jnp.bfloat16).reshape(rows // 16, 16, part.shape[1])

    greet(
        [{"expert": (e + d) % 8} for d in range(1, 8)]
        + [{"seq": (s + 1) % 16}, {"seq": (s + 15) % 16}]
        + [{"seq": along_y(d)} for d in (1, 2, 3)]
        + [{"seq": along_z(d)} for d in (1, 2, 3)]
    )
    sent = []
    wsend, wland = mailbox((ws, wr), sent)
    asend, aland = mailbox((as_, ar), sent)
    bsend, bland = mailbox((bs, br), sent)
    ysend, yland = mailbox((ys, yr), sent)
    zsend, zland = mailbox((zs, zr), sent)
    esend, eland = mailbox((edge_s, edge_r), sent)
    esend(0, x_ref.at[pl.ds(tokens - 8, 8)], pad_ref.at[pl.ds(0, 8)], {"seq": (s + 1) % 16})
    own = pltpu.make_async_copy(w_ref, g_ref.at[at_z], local_sem)
    own.start()
    half = w_ref.shape[0] // 2
    span = (pl.ds(0, half), pl.ds(half, half))
    block = lambda i, h: g_ref.at[i, span[h]]
    to_z = lambda d: {"seq": along_z(d)}
    own.wait()
    ring_gather_open(wsend, 0, block, at_z, to_z)
    pad_ref[8:] = x_ref[...]
    convolve(16, tokens)
    eland(0, pad_ref.at[pl.ds(0, 8)])
    pad_ref[:8] = jnp.where(s > 0, pad_ref[:8], 0.0)
    convolve(0, 16)
    for d in (4, 5, 3, 2, 6, 1, 7):
        to = (e + d) % 8
        asend(d, part_ref.at[to], rbox_ref.at[e], {"expert": to})
    rbox_ref[e] = part_ref[e]
    for d in range(1, 8):
        aland(d, rbox_ref.at[(e + 8 - d) % 8])
    proj_ref[e] = jnp.sum(rbox_ref[...].astype(jnp.float32), axis=0)
    for d in (4, 5, 3, 2, 6, 1, 7):
        bsend(d, proj_ref.at[e], proj_ref.at[e], {"expert": (e + d) % 8})
    ring_gather_pass(wsend, wland, 0, block, at_z, to_z)
    for d in range(1, 8):
        bland(d, proj_ref.at[(e + 8 - d) % 8])
    low = proj_ref[:, :, :RANK].reshape(tokens, RANK).astype(jnp.bfloat16)
    for at in range(0, width, 256):
        cols = slice(at, at + 256)
        raw = jnp.dot(low, dtw_ref[:, cols], preferred_element_type=jnp.float32) + dtb_ref[:, cols]
        step = jnp.maximum(raw, 0.0) + jnp.log1p(jnp.exp(-jnp.abs(raw)))
        step_ref[:, cols] = step
        u_ref[:, cols] = step * inner_ref[:, cols].astype(jnp.float32)
    same = lax.broadcasted_iota(jnp.int32, (1, STATE, STATE), 1) == lax.broadcasted_iota(
        jnp.int32, (1, STATE, STATE), 2
    )

    def spread(i, carry):
        rows = pl.ds(pl.multiple_of(i * 16, 16), 16)
        for ref, at in ((b_ref, RANK), (c_ref, RANK + STATE)):
            values = proj_ref[i][:, at : at + STATE]
            column = jnp.sum(jnp.where(same, values[:, None, :], 0.0), axis=-1, keepdims=True)
            ref[rows] = jnp.broadcast_to(column, (16, STATE, 128))
        return carry

    lax.fori_loop(0, 8, spread, 0)
    rate = a_ref[...]

    def advance(state, step8, u8, r, t):
        decay = jnp.exp(-(step8[r : r + 1, :] * rate))
        return decay * state + lanes_of(b_ref[t], width) * u8[r : r + 1, :]

    def first(g, state):
        base = pl.multiple_of(g * 8, 8)
        step8 = step_ref[pl.ds(base, 8), :]
        u8 = u_ref[pl.ds(base, 8), :]
        for r in range(8):
            state = advance(state, step8, u8, r, base + r)
        return state

    final = lax.fori_loop(0, tokens // 8, first, jnp.zeros_like(rate))
    ybox_ref[at_y, :STATE] = final.astype(jnp.bfloat16)
    ybox_ref[at_y, STATE:] = split_sum(jnp.sum(step_ref[...], axis=0, keepdims=True))
    for d in (2, 1, 3):
        ysend(d, ybox_ref.at[at_y], ybox_ref.at[at_y], {"seq": along_y(d)})
    for d in (1, 3, 2):
        yland(d, ybox_ref.at[(at_y + 4 - d) % 4])
    plane = jnp.zeros_like(rate)
    total = jnp.zeros((1, width), jnp.float32)
    for y in range(4):
        end, summed = read_end(ybox_ref, y)
        plane = jnp.exp(-(summed * rate)) * plane + end
        total = total + summed
    zmsg_ref[:STATE] = plane.astype(jnp.bfloat16)
    zmsg_ref[STATE:] = split_sum(total)
    for d in (2, 1, 3):
        zsend(d, zmsg_ref, zbox_ref.at[at_z], to_z(d))
    zbox_ref[at_z] = zmsg_ref[...]
    for d in (1, 3, 2):
        zland(d, zbox_ref.at[(at_z + 4 - d) % 4])
    start = jnp.zeros_like(rate)
    for ref, at in ((zbox_ref, at_z), (ybox_ref, at_y)):
        for i in range(3):
            end, summed = read_end(ref, i)
            start = jnp.where(i < at, jnp.exp(-(summed * rate)) * start + end, start)

    def second(g, state):
        base = pl.multiple_of(g * 8, 8)
        step8 = step_ref[pl.ds(base, 8), :]
        u8 = u_ref[pl.ds(base, 8), :]
        rows = []
        for r in range(8):
            state = advance(state, step8, u8, r, base + r)
            rows.append(jnp.sum(lanes_of(c_ref[base + r], width) * state, axis=0, keepdims=True))
        u_ref[pl.ds(base, 8), :] = jnp.concatenate(rows, axis=0)
        return state

    lax.fori_loop(0, tokens // 8, second, start)
    for at in range(0, width, 256):
        cols = slice(at, at + 256)
        z = z_ref[:, cols]
        out_ref[:, cols] = (
            (u_ref[:, cols] + skip_ref[:, cols] * inner_ref[:, cols].astype(jnp.float32))
            * (z / (1.0 + jnp.exp(-z)))
        ).astype(jnp.bfloat16)
    for m, h, o in ((2, 1, 3), (3, 0, 1), (4, 0, 2), (5, 1, 2)):
        wland(m, block((at_z + o) % 4, h))
    for copy in sent:
        copy.wait_send()


def scan(x, z, taps, conv_bias, xproj, dt_weight, dt_bias, rate, skip, weight, collective_id):
    dma = pltpu.SemaphoreType.DMA
    tokens, width = x.shape
    bf16, f32 = jnp.bfloat16, jnp.float32
    return pl.pallas_call(
        scan_kernel,
        out_shape=(
            jax.ShapeDtypeStruct((tokens, width), bf16),
            jax.ShapeDtypeStruct((4, *weight.shape), bf16),
        ),
        in_specs=[pl.BlockSpec(memory_space=pltpu.VMEM)] * 10,
        out_specs=[pl.BlockSpec(memory_space=pltpu.VMEM)] * 2,
        scratch_shapes=[
            pltpu.VMEM((tokens + 8, width), f32),
            pltpu.VMEM((tokens, width), bf16),
            pltpu.VMEM((8, 16, xproj.shape[1]), bf16),
            pltpu.VMEM((8, 16, xproj.shape[1]), bf16),
            pltpu.VMEM((8, 16, xproj.shape[1]), f32),
            pltpu.VMEM((tokens, STATE, 128), f32),
            pltpu.VMEM((tokens, STATE, 128), f32),
            pltpu.VMEM((tokens, width), f32),
            pltpu.VMEM((tokens, width), f32),
            pltpu.VMEM((4, 2 * STATE, width), bf16),
            pltpu.VMEM((4, 2 * STATE, width), bf16),
            pltpu.VMEM((2 * STATE, width), bf16),
            dma((6,)), dma((6,)), dma((8,)), dma((8,)), dma((8,)), dma((8,)),
            dma((4,)), dma((4,)), dma((4,)), dma((4,)), dma((1,)), dma((1,)), dma,
        ],
        compiler_params=pltpu.CompilerParams(
            collective_id=collective_id, has_side_effects=True, vmem_limit_bytes=VMEM_LIMIT
        ),
    )(
        x, z, taps, conv_bias[None, :], xproj.T, dt_weight, dt_bias[None, :], rate, skip[None, :], weight
    )


def per_device(
    tokens,
    gain_mamba,
    in_weight,
    conv_weight,
    conv_bias,
    xproj_weight,
    dt_weight,
    dt_bias,
    a_rate,
    skip_d,
    out_weight,
    gain_moe,
    expert_ids,
    gate_weights,
    w_gate,
    w_up,
    w_down,
):
    xpart, zpart = project(tokens, gain_mamba, in_weight, 3)
    gated, mixer_weight = scan(
        xpart, zpart, conv_weight, conv_bias, xproj_weight, dt_weight, dt_bias, a_rate, skip_d, out_weight, 1
    )
    return mix(
        gated, mixer_weight, tokens, gain_moe, expert_ids.T, gate_weights.T, w_gate, w_up, w_down, 4
    )


def solution(mesh):
    placed = (
        P(("seq", "expert"), None),
        P(),
        P(None, "seq", "expert"),
        P(None, "expert"),
        P("expert"),
        P("expert", None),
        P(None, "expert"),
        P("expert"),
        P(None, "expert"),
        P("expert"),
        P("expert", "seq"),
        P(),
        P(("seq", "expert"), None),
        P(("seq", "expert"), None),
        P("seq", None, "expert"),
        P("seq", None, "expert"),
        P("seq", "expert", None),
    )
    return jax.shard_map(
        per_device,
        mesh=mesh,
        in_specs=placed,
        out_specs=P(("seq", "expert"), None),
        check_vma=False,
    )
```
